128 devices in a mesh: dp: 16 (over y, z_lo, core), expert: 8 (over z_hi, x).
Axes of the slice: x: 4, y: 4, z: 4 (z_hi: 2, z_lo: 2; z = z_hi * 2 + z_lo), core: 2. Of those that a mesh axis runs over, the one named last changes fastest.
Arguments:
- queries: bfloat16 [2, 1024, 3072], P(None, 'dp', 'expert'), may hold values from -66 to 66
- prompt_kv: bfloat16 [2, 64, 256, 8, 256], P(None, 'dp', None, 'expert'), may hold values from -6 to 6
- new_kv: bfloat16 [2, 1024, 8, 256], P(None, 'dp', 'expert'), may hold values from -6 to 6
- prompt_slot: int32 [2, 64], replicated, may hold values from 0 to 63, each once within a row
- residual: bfloat16 [2, 1024, 6144], P(None, ('dp', 'expert')), may hold values from -6 to 6
- w_out: bfloat16 [3072, 6144], P('expert'), may hold values from -0.109375 to 0.109375
- norm_gain: float32 [6144], replicated, may hold values from 0.1 to 1.9
- w_router: bfloat16 [6144, 8], replicated, may hold values from -0.078125 to 0.078125
- routes: int32 [2, 1024, 2], P(None, ('dp', 'expert')), may hold values from 0 to 7, all different within a row; in each aligned block of 8 rows (0 to 7, 8 to 15, ..., all dimensions but the last counted through in order) at most 4 rows name the same one
- w_gate: bfloat16 [8, 6144, 8192], P('expert', None, 'dp'), may hold values from -0.078125 to 0.078125
- w_up: bfloat16 [8, 6144, 8192], P('expert', None, 'dp'), may hold values from -0.078125 to 0.078125
- w_down: bfloat16 [8, 8192, 6144], P('expert', 'dp'), may hold values from -0.0625 to 0.0625
Outputs:
- layer_out: bfloat16 [2, 1024, 6144], P(None, ('dp', 'expert'))
The draws below stay inside these ranges and needn't reach their ends.
Inputs may be any that keep to these rules, and one draw needn't show every extreme that they name: Each step's row is a permutation; the slot of prompt_kv that holds group g's prompt lies on the index of dp given by prompt_slot // 4. `routes`: the two experts of a row differ. In each step the 8 rows of one device name one expert at most 4 times together, a bound that some block reaches.
All inputs are finite; a program needn't handle non-finite values.
Results may differ from the reference program's by a relative error of at most 0.017.
Values may be sent and summed in bfloat16 or wider, within the bound.
A program may use at most 128 MiB of HBM per device.

```python
import math
import jax
import jax.numpy as jnp
import numpy as np
from jax import lax

D = 6144
HEAD = 128
Q_PER_KV = 3
FF = 8192
PROMPT = 256
STEPS = 2
GROUPS = 64
KV_HEADS = 8
Q_HEADS = 24
EXPERTS = 8
ROWS = 1024
MOE_ROWS = 8
CAP = 4
N_DP = 16


def draw_queries(key, part):
    key = jax.random.fold_in(key, 11)
    shape = (STEPS, ROWS, KV_HEADS, Q_PER_KV, HEAD)
    values = jnp.clip(jax.random.normal(key, shape, jnp.float32), -6.0, 6.0)
    return values.reshape(STEPS, ROWS, KV_HEADS * Q_PER_KV * HEAD).astype(jnp.bfloat16)


def draw_prompt_kv(key, part):
    key = jax.random.fold_in(key, 12)
    shape = (STEPS, GROUPS, PROMPT, KV_HEADS, 2 * HEAD)
    values = jnp.clip(jax.random.normal(key, shape, jnp.float32), -6.0, 6.0)
    return values.astype(jnp.bfloat16)


def shard_levels(stream_key, dims, pieces, smallest, top_value):
    factor_of = 1.0
    for dim, shards_of in pieces:
        draws = jax.random.uniform(jax.random.fold_in(jax.random.fold_in(stream_key, 6), dim), (shards_of,), jnp.float32, smallest / len(pieces), top_value / len(pieces))
        factor_of = factor_of * jnp.repeat(jnp.exp(draws), dims[dim] // shards_of).reshape((-1,) + (1,) * (len(dims) - 1 - dim))
    return factor_of


def assign_block(key, own, number, rows, count, top, bound, slope):
    order = jax.random.permutation(key, count)
    crowded, usual = shares(count, rows * top, bound, slope, True), shares(count, rows * top, bound, slope, False)
    places = jnp.arange(count)

    def named(sizes, offset_by):
        used = int((sizes > 0).sum())
        fixed = max(1, used // 4)
        moved = fixed + (places - fixed + offset_by * (used - fixed)) % max(1, count - fixed)
        return jnp.zeros((count,), jnp.int32).at[order[jnp.where(places < fixed, places, moved)]].set(jnp.asarray(sizes, jnp.int32))

    sizes = jnp.where(number % 4 == 0, named(crowded, number // 4), named(usual, number - number // 4 - 1))
    mixed = jax.random.permutation(jax.random.fold_in(own, 3), count)
    source_of, taker = mixed[0:count // 2 * 2:2], mixed[1:count // 2 * 2:2]
    margin = jnp.minimum(sizes[source_of] - 1, bound - sizes[taker]) // 2
    margin = jnp.where((source_of == order[0]) | (taker == order[0]) | (sizes[taker] == 0), 0, jnp.maximum(margin, 0))
    moved = jax.random.randint(jax.random.fold_in(own, 4), (count // 2,), 0, 1 << 20) % (margin + 1)
    sizes = sizes.at[source_of].add(-moved).at[taker].add(moved)
    members = jnp.searchsorted(jnp.cumsum(sizes), jnp.arange(rows * top), side="right").astype(jnp.int32)
    table = members.reshape(top, rows).T
    table = table[jax.random.permutation(jax.random.fold_in(own, 1), rows)]
    offset_by = jax.random.randint(jax.random.fold_in(own, 2), (rows, 1), 0, top)
    return jnp.take_along_axis(table, (jnp.arange(top)[None, :] + offset_by) % top, axis=1)


def shares(number_of, total, bound, lean, full):
    portions = [(1 << 20) // math.isqrt(rank ** lean) + 1 for rank in range(1, number_of + 1)]
    largest = bound if full else min(bound, max(-(-total // number_of), total * portions[0] // sum(portions)))
    least = 1 if total - largest >= number_of - 1 else 0
    given, rest = [largest] + [least] * (number_of - 1), total - largest - least * (number_of - 1)
    while rest > 0:
        free = [i for i in range(1, number_of) if given[i] < largest] or [i for i in range(1, number_of) if given[i] < bound]
        whole, left = sum([portions[i] for i in free]), rest
        for i in free:
            addition = min(bound - given[i], max(1, left * portions[i] // whole), rest)
            given[i] = given[i] + addition
            rest = rest - addition
    return np.array(given)


def scatter_about(stream_key, shape, scale, reach, pieces=(), kind=jnp.bfloat16):
    factor_of = shard_levels(stream_key, shape, pieces, -0.22, 0.18) if pieces else 1.0
    array = jax.random.normal(stream_key, shape, jnp.float32) * scale * factor_of
    return jnp.minimum(jnp.maximum(array, -reach), reach).astype(kind)


def setup_inputs(seed: int = 0) -> dict:
    seeds = jax.random.split(jax.random.key(seed), 13)
    queries = draw_queries(jax.random.fold_in(seeds[12], 71), 0)
    prompt_kv = draw_prompt_kv(jax.random.fold_in(seeds[12], 71), 0)
    new_kv = scatter_about(seeds[2], (STEPS, ROWS, KV_HEADS, 2 * HEAD), 1.0, 6.0, ((1, 16), (2, 8)))
    prompt_slot = jax.vmap(lambda own: jax.random.permutation(own, GROUPS))(jax.random.split(seeds[3], STEPS)).reshape((STEPS, GROUPS)).astype(jnp.int32)
    residual = scatter_about(seeds[4], (STEPS, ROWS, D), 1.0, 6.0, ((1, 128),))
    w_out = scatter_about(seeds[5], (Q_HEADS * HEAD, D), (Q_HEADS * HEAD) ** -0.5, 0.109375, ((0, 8),))
    norm_gain = jnp.clip(1.0 + 0.18 * jax.random.normal(seeds[6], (D,), jnp.float32), 0.1, 1.9)
    w_router = scatter_about(seeds[7], (D, EXPERTS), D ** -0.5, 0.078125)
    routes_keys = jax.random.split(jax.random.fold_in(seeds[8], 1), STEPS * ROWS // MOE_ROWS)
    routes_turns = jax.random.permutation(jax.random.fold_in(seeds[8], 3), STEPS * ROWS // MOE_ROWS)
    routes = jax.vmap(lambda own, number: assign_block(jax.random.fold_in(seeds[8], 2), own, number, MOE_ROWS, EXPERTS, 2, CAP, 2))(routes_keys, routes_turns).reshape((STEPS, ROWS, 2))
    w_gate = scatter_about(seeds[9], (EXPERTS, D, FF), D ** -0.5, 0.078125, ((0, 8), (2, 16)))
    w_up = scatter_about(seeds[10], (EXPERTS, D, FF), D ** -0.5, 0.078125, ((0, 8), (2, 16)))
    w_down = scatter_about(seeds[11], (EXPERTS, FF, D), FF ** -0.5, 0.0625, ((0, 8), (1, 16)))
    return {"queries": queries, "prompt_kv": prompt_kv, "new_kv": new_kv, "prompt_slot": prompt_slot, "residual": residual, "w_out": w_out, "norm_gain": norm_gain, "w_router": w_router, "routes": routes, "w_gate": w_gate, "w_up": w_up, "w_down": w_down}


tile_rows = 16

def attend_group(packed):
    query_rows, prompt, suffix = packed
    query_float = query_rows.astype(jnp.float32)
    prompt_keys = prompt[:, :, :HEAD].astype(jnp.float32)
    prompt_values = prompt[:, :, HEAD:].astype(jnp.float32)
    suffix_keys = suffix[..., :HEAD].astype(jnp.float32)
    suffix_values = suffix[..., HEAD:].astype(jnp.float32)
    factor = 1.0 / math.sqrt(HEAD)
    prompt_scores = jnp.einsum('jhad,phd->jhap', query_float, prompt_keys) * factor
    suffix_scores = jnp.einsum('jhad,sjhd->jhas', query_float, suffix_keys) * factor
    scores = jnp.concatenate([prompt_scores, suffix_scores], axis=-1)
    peak = lax.optimization_barrier(jnp.max(scores, axis=-1, keepdims=True))
    weights = jnp.exp(scores - peak)
    totals = lax.optimization_barrier(jnp.sum(weights, axis=-1))
    rounded = lax.optimization_barrier(weights.astype(jnp.bfloat16)).astype(jnp.float32)
    summed = jnp.einsum('jhap,phd->jhad', rounded[..., :PROMPT], prompt_values)
    summed = summed + jnp.einsum('jhas,sjhd->jhad', rounded[..., PROMPT:], suffix_values)
    return (summed / totals[..., None]).astype(jnp.bfloat16)

def run_experts(normed, chosen_ids, w_gate, w_up, w_down):
    width = normed.shape[1]
    pair_ids = chosen_ids.reshape(-1).astype(jnp.int32)
    pair_count = pair_ids.shape[0]
    expert_count = w_gate.shape[0]
    order = jnp.argsort(pair_ids, stable=True).astype(jnp.int32)
    sorted_rows = jnp.take(normed, order // 2, axis=0)
    padded_rows = jnp.concatenate([sorted_rows, jnp.zeros((tile_rows, width), normed.dtype)], axis=0)
    labels = jnp.arange(expert_count, dtype=jnp.int32)
    counts = lax.optimization_barrier(jnp.sum((pair_ids[None, :] == labels[:, None]).astype(jnp.int32), axis=1)).astype(jnp.int32)
    offsets = (jnp.cumsum(counts) - counts).astype(jnp.int32)
    tiles_each = ((counts + tile_rows - 1) // tile_rows).astype(jnp.int32)
    tile_end = jnp.cumsum(tiles_each).astype(jnp.int32)
    tile_begin = (tile_end - tiles_each).astype(jnp.int32)
    tile_total = pair_count // tile_rows + expert_count
    lanes = jnp.arange(tile_rows, dtype=jnp.int32)

    def one_tile(tile_index):
        owner = jnp.sum((tile_end <= tile_index).astype(jnp.int32)).astype(jnp.int32)
        clipped = jnp.minimum(owner, expert_count - 1).astype(jnp.int32)
        local = (tile_index - tile_begin[clipped]).astype(jnp.int32)
        first = (offsets[clipped] + local * tile_rows).astype(jnp.int32)
        live = (lanes < counts[clipped] - local * tile_rows) & (owner < expert_count)
        first = jnp.clip(first, 0, pair_count).astype(jnp.int32)
        block = lax.dynamic_slice_in_dim(padded_rows, first, tile_rows, 0)
        gate_part = jnp.dot(block, w_gate[clipped], preferred_element_type=jnp.float32)
        up_part = jnp.dot(block, w_up[clipped], preferred_element_type=jnp.float32)
        hidden = (jax.nn.silu(gate_part) * up_part).astype(jnp.bfloat16)
        produced = jnp.dot(hidden, w_down[clipped], preferred_element_type=jnp.float32)
        targets = jnp.where(live, first + lanes, pair_count).astype(jnp.int32)
        return (produced, targets)
    produced, targets = lax.map(one_tile, jnp.arange(tile_total, dtype=jnp.int32))
    collected = jnp.zeros((pair_count + 1, width), jnp.float32).at[targets.reshape(-1)].add(produced.reshape(-1, width))
    unsorted = jnp.zeros((pair_count, width), jnp.float32).at[order].set(collected[:pair_count])
    return unsorted.reshape(chosen_ids.shape[0], 2, width)

def reference(queries, prompt_kv, new_kv, prompt_slot, residual, w_out, norm_gain, w_router, routes, w_gate, w_up, w_down):
    results = []
    for step_index in range(STEPS):
        query_rows = queries[step_index].reshape(N_DP, GROUPS, KV_HEADS, Q_PER_KV, HEAD).transpose(1, 0, 2, 3, 4)
        prompts = jnp.take(prompt_kv[step_index], prompt_slot[step_index].astype(jnp.int32), axis=0)
        suffix = new_kv[:step_index + 1].reshape(step_index + 1, N_DP, GROUPS, KV_HEADS, 2 * HEAD).transpose(2, 0, 1, 3, 4)
        attended = lax.map(attend_group, (query_rows, prompts, suffix))
        attended = attended.transpose(1, 0, 2, 3, 4).reshape(ROWS, Q_HEADS * HEAD)
        mixed = residual[step_index].astype(jnp.float32) + jnp.dot(attended, w_out, preferred_element_type=jnp.float32)
        spread = jnp.sqrt(lax.optimization_barrier(jnp.mean(mixed * mixed, axis=-1, keepdims=True)) + 1e-05)
        normed = (mixed / spread * norm_gain).astype(jnp.bfloat16)
        logits = jnp.dot(normed, w_router, preferred_element_type=jnp.float32)
        chosen_ids = routes[step_index].astype(jnp.int32)
        chosen = jnp.take_along_axis(logits, chosen_ids, axis=1)
        gates = jax.nn.sigmoid(chosen - chosen[:, ::-1])
        expert_out = run_experts(normed, chosen_ids, w_gate, w_up, w_down)
        layer_rows = mixed + lax.optimization_barrier(jnp.sum(gates[:, :, None] * expert_out, axis=1))
        results.append(layer_rows.astype(jnp.bfloat16))
    return jnp.stack(results)
```

```python
import math

import jax
import jax.numpy as jnp
from jax import lax
from jax.experimental import pallas as pl
from jax.experimental.pallas import tpu as pltpu
from jax.sharding import PartitionSpec as P

HEAD = 128
MESH = pl.DeviceIdType.MESH
BF = jnp.bfloat16
F32 = jnp.float32
NEG = -1e30

STEPS = 2
NDP = 16
NEX = 8
GROUPS = 64
D = 6144
HALF = D // 2
QUART = D // 4
FFD = 512
ROWS = 8
SLOTS = 32
TILE = 512


def iota(shape, dim):
    return lax.broadcasted_iota(jnp.int32, shape, dim)


def dot(a, b):
    return jnp.dot(a, b, preferred_element_type=F32)


def dot_nt(a, b):
    return lax.dot_general(a, b, (((1,), (1,)), ((), ())), preferred_element_type=F32)


def ones_where(cond):
    return jnp.where(cond, 1.0, 0.0).astype(BF)


def to_column(row):
    n = row.shape[1]
    eye = iota((n, n), 0) == iota((n, n), 1)
    return jnp.sum(jnp.where(eye, row, 0), axis=1, keepdims=True)


def loop(n, fn):
    lax.fori_loop(0, n, lambda i, c: (fn(i), c)[1], 0)


def tile_at(i, base=0):
    return pl.ds(pl.multiple_of(base + i * TILE, TILE), TILE)


def kernel(
    q_ref, pkv_ref, nkv_ref, slot_ref, res_ref, wo_hbm, gain_ref, wr_ref, routes_ref, wg_hbm, wu_hbm, wd_hbm,
    out_ref,
    wo, wg, wu, wd,
    qs_send, qs_recv, at_send, at_recv, op_send, op_recv, ds_send, ds_recv,
    mixed, nb, gat, held, acc_g, acc_u, hid, pair, transit, ysum, zsum, rt_send, rt_recv,
    w_sem, q_sem, a_sem, o_sem, d_sem, g_sem, r_sem, t_sem,
):
    dp = lax.axis_index("dp")
    ex = lax.axis_index("expert")
    y = dp // 4
    zl = (dp // 2) % 2
    core = dp % 2

    def at_dp(dy, flip_z=0, flip_c=0):
        yy = (y + dy) % 4
        zz = 1 - zl if flip_z else zl
        cc = 1 - core if flip_c else core
        return yy * 4 + zz * 2 + cc

    def remote(src, dst, sems, idx, to_dp, to_ex):
        return pltpu.make_async_remote_copy(
            src_ref=src,
            dst_ref=dst,
            send_sem=sems.at[(0, *idx)],
            recv_sem=sems.at[(1, *idx)],
            device_id=(to_dp, to_ex),
            device_id_type=MESH,
        )

    weights = [
        pltpu.make_async_copy(src, dst, w_sem.at[i])
        for i, (src, dst) in enumerate(((wo_hbm, wo), (wg_hbm, wg), (wu_hbm, wu), (wd_hbm, wd)))
    ]
    for copy in weights:
        copy.start()

    barrier = pltpu.get_barrier_semaphore()
    for d in range(1, NDP):
        pl.semaphore_signal(barrier, inc=1, device_id=((dp + d) % NDP, ex), device_id_type=MESH)
    for d in range(1, NEX):
        pl.semaphore_signal(barrier, inc=1, device_id=(dp, (ex + d) % NEX), device_id_type=MESH)

    row = iota((256, 128), 0)
    part_of = (row & 15) >> 2
    slot_rows = [slot_ref[t : t + 1, :] for t in range(STEPS)]
    r64 = iota((256, GROUPS), 0)
    want = 4 * (r64 >> 4) + (r64 & 3)

    def by_part(full):
        picked = jnp.zeros((256, HEAD), F32)
        for a in range(4):
            picked = jnp.where(part_of == a, full[:, a * HEAD : (a + 1) * HEAD], picked)
        return picked.astype(BF).reshape(NDP, 16, HEAD)

    for t in range(STEPS):
        order = ones_where(slot_rows[t] == want)
        first = dot(order, jnp.concatenate([q_ref[t], nkv_ref[t][:, :HEAD]], axis=1))
        qs_send[:, t, 0] = by_part(first)
        if t == 0:
            zero = jnp.zeros((GROUPS, 3 * HEAD), BF)
            second = jnp.concatenate([zero, nkv_ref[0][:, HEAD:]], axis=1)
        else:
            zero = jnp.zeros((GROUPS, HEAD), BF)
            second = jnp.concatenate([nkv_ref[0][:, :HEAD], zero, nkv_ref[0][:, HEAD:], nkv_ref[1][:, HEAD:]], axis=1)
        qs_send[:, t, 1] = by_part(dot(order, second))

    pl.semaphore_wait(barrier, NDP - 1 + NEX - 1)

    def spread_dp(send, recv, sems):
        return [remote(send.at[(dp + d) % NDP], recv.at[dp], sems, (d - 1,), (dp + d) % NDP, ex) for d in range(1, NDP)]

    q_copies = spread_dp(qs_send, qs_recv, q_sem)
    for copy in q_copies:
        copy.start()
    qs_recv[dp] = qs_send[dp]
    for copy in q_copies:
        copy.wait_recv()

    factor = 1.0 / math.sqrt(HEAD)
    r_s = iota((256, 1024), 0)
    own_prompt = (r_s & 3) == (iota((256, 1024), 1) >> 8)
    r_e, c_e = iota((256, 256), 0), iota((256, 256), 1)
    same_source = (r_e >> 4) == (c_e >> 4)

    def pick(block, base):
        return dot(ones_where(same_source & ((c_e & 15) == base + (r_e & 3))), block)

    for t in range(STEPS):
        first = qs_recv[:, t, 0].reshape(256, HEAD)
        second = qs_recv[:, t, 1].reshape(256, HEAD)
        stored = pkv_ref[t].reshape(1024, 2 * HEAD)
        scores = jnp.where(own_prompt, dot_nt(first, stored[:, :HEAD]) * factor, NEG)
        first_f = first.astype(F32)
        recent = [(pick(first, 12), pick(second, 12))]
        if t == 1:
            recent.append((pick(second, 0), pick(second, 8)))
        recent_scores = [jnp.sum(first_f * keys, axis=1, keepdims=True) * factor for keys, _ in recent]
        peak = jnp.max(scores, axis=1, keepdims=True)
        for s in recent_scores:
            peak = jnp.maximum(peak, s)
        weight = jnp.exp(scores - peak)
        total = jnp.sum(weight, axis=1, keepdims=True)
        summed = dot(weight.astype(BF), stored[:, HEAD:])
        for s, (_, values) in zip(recent_scores, recent):
            w = jnp.exp(s - peak)
            total = total + w
            summed = summed + w.astype(BF).astype(F32) * values
        at_send[:, t] = (summed / total).astype(BF).reshape(NDP, 16, HEAD)

    a_copies = spread_dp(at_send, at_recv, a_sem)
    for copy in a_copies:
        copy.start()
    at_recv[dp] = at_send[dp]
    for copy in a_copies:
        copy.wait_recv()

    c64 = iota((GROUPS, 256), 1)
    want_c = 4 * (c64 >> 4) + (c64 & 3)
    weights[0].wait()

    def spread_ex(send, recv, sems, t):
        return [
            remote(send.at[t, (ex + d) % NEX], recv.at[t, ex], sems, (t, d - 1), dp, (ex + d) % NEX)
            for d in range(1, NEX)
        ]

    o_copies = []
    for t in range(STEPS):
        back = at_recv[:, t].reshape(256, HEAD)
        back_f = back.astype(F32)
        parted = jnp.concatenate([jnp.where(part_of == a, back_f, 0.0).astype(BF) for a in range(3)], axis=1)
        order = ones_where(to_column(slot_rows[t]) == want_c)
        attended = dot(order, parted).astype(BF)

        def project(i, t=t, attended=attended):
            lo = dot(attended, wo[:, tile_at(i)])
            hi = dot(attended, wo[:, tile_at(i, HALF)])
            for e in range(NEX):
                both = jnp.concatenate([lo[e * 8 : e * 8 + 8], hi[e * 8 : e * 8 + 8]], axis=0)
                op_send[t, e, :, tile_at(i)] = both.astype(BF)

        loop(HALF // TILE, project)
        o_copies.append(spread_ex(op_send, op_recv, o_sem, t))
        for copy in o_copies[t]:
            copy.start()

    d_copies = [None, None]
    targets = [None, None]

    def mix(t):
        for copy in o_copies[t]:
            copy.wait_recv()

        def add(i, squares):
            total = op_send[t, ex, :, tile_at(i)].astype(F32)
            for d in range(1, NEX):
                total = total + op_recv[t, (ex + d) % NEX, :, tile_at(i)].astype(F32)
            lo = res_ref[t, :, tile_at(i)].astype(F32)
            hi = res_ref[t, :, tile_at(i, HALF)].astype(F32)
            total = total + jnp.concatenate([lo, hi], axis=0)
            mixed[t, :, tile_at(i)] = total
            return squares + total * total

        squares = lax.fori_loop(0, HALF // TILE, add, jnp.zeros((16, TILE), F32))
        per_half = jnp.sum(squares, axis=1, keepdims=True)
        inverse = 1.0 / jnp.sqrt((per_half[:8] + per_half[8:]) / D + 1e-05)
        inverse = jnp.concatenate([inverse, inverse], axis=0)

        def scale(i):
            lower = iota((16, TILE), 0) < 8
            gain = jnp.where(lower, gain_ref[:, tile_at(i)], gain_ref[:, tile_at(i, HALF)])
            nb[:, tile_at(i)] = (mixed[t, :, tile_at(i)] * inverse * gain).astype(BF)

        loop(HALF // TILE, scale)
        normed = nb[...].astype(F32)
        lo, hi = normed[:8], normed[8:]
        logits = dot_nt(lo.astype(BF), wr_ref[:, :HALF]) + dot_nt(hi.astype(BF), wr_ref[:, HALF:])
        rows = [routes_ref[t][k : k + 1, :] for k in range(2)]
        cols = [to_column(r) for r in rows]
        chosen = [jnp.sum(jnp.where(iota((8, 8), 1) == c, logits, 0.0), axis=1, keepdims=True) for c in cols]
        before = iota((8, 8), 1) < iota((8, 8), 0)
        cells = []
        for k in range(2):
            gat[t, k] = jnp.broadcast_to(jax.nn.sigmoid(chosen[k] - chosen[1 - k]), (8, 128))
            place = jnp.zeros((8, 1), jnp.int32)
            for other in rows:
                place = place + jnp.sum(jnp.where(before & (cols[k] == other), 1, 0), axis=1, keepdims=True)
            cells.append(cols[k] * 4 + place)
        targets[t] = cells
        c32 = iota((8, 32), 1) & 7
        cell_rows = [jnp.sum(jnp.where(c32 == iota((8, 32), 0), c, 0), axis=0, keepdims=True) for c in cells]
        r_d, c_d = iota((128, 32), 0), iota((128, 32), 1)
        cell = 4 * (r_d >> 4) + (r_d & 3)
        same_quarter = ((r_d & 15) >> 2) == (c_d >> 3)
        choose = ones_where(same_quarter & ((cell_rows[0] == cell) | (cell_rows[1] == cell)))
        quarters = jnp.concatenate([lo[:, :QUART], lo[:, QUART:], hi[:, :QUART], hi[:, QUART:]], axis=0).astype(BF)
        for i in range(QUART // TILE):
            cut = slice(i * TILE, (i + 1) * TILE)
            ds_send[t, :, :, cut] = dot(choose, quarters[:, cut]).astype(BF).reshape(NEX, 16, TILE)
        d_copies[t] = spread_ex(ds_send, ds_recv, d_sem, t)
        for copy in d_copies[t]:
            copy.start()

    r_u, c_u = iota((128, 128), 0), iota((128, 128), 1)
    unfold_matrix = ones_where(((r_u >> 5) == ((c_u & 15) >> 2)) & (((r_u & 31) >> 2) == (c_u >> 4)) & ((r_u & 3) == (c_u & 3)))
    fold_matrix = ones_where(((c_u >> 5) == ((r_u & 15) >> 2)) & (((c_u & 31) >> 2) == (r_u >> 4)) & ((c_u & 3) == (r_u & 3)))


    def unfold(t):
        for copy in d_copies[t]:
            copy.wait_recv()
        ds_recv[t, ex] = ds_send[t, ex]
        for i in range(QUART // TILE):
            cut = slice(i * TILE, (i + 1) * TILE)
            rows = dot(unfold_matrix, ds_recv[t, :, :, cut].reshape(128, TILE)).astype(BF)
            for quarter in range(4):
                start = quarter * QUART + i * TILE
                held[t, dp, :, start : start + TILE] = rows[quarter * SLOTS : (quarter + 1) * SLOTS]

    g_copies = [{}, {}]

    def give(t, kind, ref, to_dp):
        copy = remote(ref, ref, g_sem, (t, kind), to_dp, ex)
        copy.start()
        g_copies[t][kind] = copy

    def gather_own(t):
        own = held.at[t, dp]
        give(t, 0, own, at_dp(0, 1))
        give(t, 1, own, at_dp(1))
        give(t, 2, own, at_dp(3))
        give(t, 9, own, at_dp(0, 0, 1))

    def gather_z(t):
        g_copies[t][0].wait_recv()
        other = held.at[t, at_dp(0, 1)]
        give(t, 3, other, at_dp(1))
        give(t, 4, other, at_dp(3))
        give(t, 10, other, at_dp(0, 0, 1))

    def gather_near(t, plane):
        for kind, dy, to_dy, part in ((1, 3, 1, 0), (2, 1, 3, 16)):
            g_copies[t][kind + 2 * plane].wait_recv()
            source = at_dp(dy, plane)
            give(t, kind + 4 + 2 * plane, held.at[t, source, pl.ds(part, 16)], at_dp(to_dy))
            give(t, 9 + 2 * dy + plane, held.at[t, source], at_dp(0, 0, 1))

    def gather_far(t, plane):
        for kind in (5, 6):
            g_copies[t][kind + 2 * plane].wait_recv()
        give(t, 13 + plane, held.at[t, at_dp(2, plane)], at_dp(0, 0, 1))

    def gather_end(t):
        for kind in range(9, 17):
            g_copies[t][kind].wait_recv()

    def gate_up(t, first, last):
        if first == 0:
            acc_g[...] = jnp.zeros_like(acc_g)
            acc_u[...] = jnp.zeros_like(acc_u)

        def step(i):
            x = held[t, :, :, tile_at(i, first * TILE)].reshape(NDP * SLOTS, TILE)
            acc_g[...] += dot(x, wg[tile_at(i, first * TILE), :])
            acc_u[...] += dot(x, wu[tile_at(i, first * TILE), :])

        loop(last - first, step)

    def activate(t):
        hid[...] = (jax.nn.silu(acc_g[...]) * acc_u[...]).astype(BF)
        for copy in g_copies[t].values():
            copy.wait_send()

    def down(t, first, last):
        def step(i):
            y_part = dot(hid[...], wd[:, tile_at(i, first * TILE)])
            held[t, :, :, tile_at(i, first * TILE)] = y_part.astype(BF).reshape(NDP, SLOTS, TILE)

        loop(last - first, step)

    r_copies = [{}, {}]

    def pass_on(t, kind, src, dst, to_dp):
        copy = remote(src, dst, r_sem, (t, kind), to_dp, ex)
        copy.start()
        r_copies[t][kind] = copy

    def reduce_cores(t):
        for dy in (2, 1, 3, 0):
            for plane in range(2):
                kind = 2 * dy + plane
                pass_on(t, kind, held.at[t, at_dp(dy, plane, 1)], pair.at[t, kind], at_dp(0, 0, 1))

    def reduce_far(t):
        for plane in range(2):
            r_copies[t][4 + plane].wait_recv()
            there = at_dp(2, plane)

            def add(i, there=there, plane=plane):
                cut = tile_at(i)
                total = held[t, there, :, cut].astype(F32) + pair[t, 4 + plane, :, cut].astype(F32)
                held[t, there, :, cut] = total.astype(BF)

            loop(D // TILE, add)
            pass_on(t, 8 + plane, held.at[t, there, pl.ds(0, 16)], transit.at[t, 0, plane], at_dp(1))
            pass_on(t, 10 + plane, held.at[t, there, pl.ds(16, 16)], transit.at[t, 1, plane], at_dp(3))

    def reduce_near(t, way):
        dy = 1 if way == 0 else 3
        for plane in range(2):
            r_copies[t][2 * dy + plane].wait_recv()
            r_copies[t][8 + 2 * way + plane].wait_recv()
            there = at_dp(dy, plane)

            def add(i, there=there, plane=plane):
                cut = tile_at(i)
                total = held[t, there, :, cut].astype(F32) + pair[t, 2 * dy + plane, :, cut].astype(F32)
                moved = transit[t, way, plane, :, cut].astype(F32)
                if way == 0:
                    total = jnp.concatenate([total[:16] + moved, total[16:]], axis=0)
                else:
                    total = jnp.concatenate([total[:16], total[16:] + moved], axis=0)
                held[t, there, :, cut] = total.astype(BF)

            loop(D // TILE, add)
            pass_on(t, 12 + 2 * way + plane, held.at[t, there], ysum.at[t, way, plane], at_dp(dy))

    def here(t, plane, cut):
        total = held[t, at_dp(0, plane), :, cut].astype(F32) + pair[t, plane, :, cut].astype(F32)
        return total + ysum[t, 0, plane, :, cut].astype(F32) + ysum[t, 1, plane, :, cut].astype(F32)

    def reduce_here(t):
        for plane in (1, 0):
            for kind in (plane, 12 + plane, 14 + plane):
                r_copies[t][kind].wait_recv()
            if plane == 1:

                def add(i):
                    held[t, at_dp(0, 1), :, tile_at(i)] = here(t, 1, tile_at(i)).astype(BF)

                loop(D // TILE, add)
                pass_on(t, 16, held.at[t, at_dp(0, 1)], zsum.at[t], at_dp(0, 1))

    t_copies = [None, None]

    def finish(t):
        r_copies[t][16].wait_recv()
        for i in range(QUART // TILE):
            parts = []
            for quarter in range(4):
                cut = slice(quarter * QUART + i * TILE, quarter * QUART + (i + 1) * TILE)
                parts.append((here(t, 0, cut) + zsum[t, :, cut].astype(F32)).astype(BF))
            folded = dot(fold_matrix, jnp.concatenate(parts, axis=0)).astype(BF)
            rt_send[t, :, :, i * TILE : (i + 1) * TILE] = folded.reshape(NEX, 16, TILE)
        t_copies[t] = spread_ex(rt_send, rt_recv, t_sem, t)
        for copy in t_copies[t]:
            copy.start()
        rt_recv[t, ex] = rt_send[t, ex]

    def combine(t):
        for copy in t_copies[t]:
            copy.wait_recv()
        both = jnp.concatenate(targets[t], axis=0)
        c_c = iota((16, 128), 1)
        mine = both == 4 * (c_c >> 4) + (c_c & 3)
        gate0, gate1 = gat[t, 0][:, :1], gat[t, 1][:, :1]
        for i in range(QUART // TILE):
            came = rt_recv[t, :, :, i * TILE : (i + 1) * TILE].reshape(128, TILE)
            for quarter in range(4):
                out = dot(ones_where(mine & (((c_c & 15) >> 2) == quarter)), came)
                upper = (quarter // 2) * 8
                start = (quarter % 2) * QUART + i * TILE
                total = mixed[t, upper : upper + 8, start : start + TILE] + gate0 * out[:8] + gate1 * out[8:]
                place = quarter * QUART + i * TILE
                out_ref[t, :, place : place + TILE] = total.astype(BF)

    mix(0)
    unfold(0)
    gather_own(0)
    mix(1)
    gather_z(0)
    unfold(1)
    gather_own(1)
    gather_near(0, 0)
    gather_near(0, 1)
    gather_z(1)
    gather_far(0, 0)
    gather_far(0, 1)
    gather_end(0)
    for copy in weights[1:]:
        copy.wait()
    gate_up(0, 0, 4)
    gather_near(1, 0)
    gate_up(0, 4, 8)
    gather_near(1, 1)
    gate_up(0, 8, 12)
    activate(0)
    down(0, 0, 4)
    gather_far(1, 0)
    down(0, 4, 8)
    down(0, 8, 12)
    reduce_cores(0)
    gather_far(1, 1)
    gather_end(1)
    reduce_far(0)
    gate_up(1, 0, 6)
    reduce_near(0, 0)
    reduce_near(0, 1)
    gate_up(1, 6, 12)
    activate(1)
    down(1, 0, 6)
    reduce_here(0)
    down(1, 6, 12)
    reduce_cores(1)
    finish(0)
    reduce_far(1)
    reduce_near(1, 0)
    reduce_near(1, 1)
    reduce_here(1)
    combine(0)
    finish(1)
    combine(1)

    for copy in q_copies + a_copies:
        copy.wait_send()
    for t in range(STEPS):
        for copy in o_copies[t] + d_copies[t] + list(r_copies[t].values()) + t_copies[t]:
            copy.wait_send()


def body(queries, prompt_kv, new_kv, prompt_slot, residual, w_out, norm_gain, w_router, routes, w_gate, w_up, w_down):
    vmem = pl.BlockSpec(memory_space=pltpu.VMEM)
    hbm = pl.BlockSpec(memory_space=pl.ANY)
    dma = pltpu.SemaphoreType.DMA
    return pl.pallas_call(
        kernel,
        out_shape=jax.ShapeDtypeStruct((STEPS, ROWS, D), BF),
        in_specs=[vmem] * 5 + [hbm] + [vmem] * 3 + [hbm] * 3,
        out_specs=vmem,
        scratch_shapes=[
            pltpu.VMEM((3 * HEAD, D), BF),
            pltpu.VMEM((D, FFD), BF),
            pltpu.VMEM((D, FFD), BF),
            pltpu.VMEM((FFD, D), BF),
            pltpu.VMEM((NDP, STEPS, 2, 16, HEAD), BF),
            pltpu.VMEM((NDP, STEPS, 2, 16, HEAD), BF),
            pltpu.VMEM((NDP, STEPS, 16, HEAD), BF),
            pltpu.VMEM((NDP, STEPS, 16, HEAD), BF),
            pltpu.VMEM((STEPS, NEX, 16, HALF), BF),
            pltpu.VMEM((STEPS, NEX, 16, HALF), BF),
            pltpu.VMEM((STEPS, NEX, 16, QUART), BF),
            pltpu.VMEM((STEPS, NEX, 16, QUART), BF),
            pltpu.VMEM((STEPS, 16, HALF), F32),
            pltpu.VMEM((16, HALF), BF),
            pltpu.VMEM((STEPS, 2, 8, 128), F32),
            pltpu.VMEM((STEPS, NDP, SLOTS, D), BF),
            pltpu.VMEM((NDP * SLOTS, FFD), F32),
            pltpu.VMEM((NDP * SLOTS, FFD), F32),
            pltpu.VMEM((NDP * SLOTS, FFD), BF),
            pltpu.VMEM((STEPS, 8, SLOTS, D), BF),
            pltpu.VMEM((STEPS, 2, 2, 16, D), BF),
            pltpu.VMEM((STEPS, 2, 2, SLOTS, D), BF),
            pltpu.VMEM((STEPS, SLOTS, D), BF),
            pltpu.VMEM((STEPS, NEX, 16, QUART), BF),
            pltpu.VMEM((STEPS, NEX, 16, QUART), BF),
            dma((4,)),
            dma((2, NDP - 1)),
            dma((2, NDP - 1)),
            dma((2, STEPS, NEX - 1)),
            dma((2, STEPS, NEX - 1)),
            dma((2, STEPS, 17)),
            dma((2, STEPS, 17)),
            dma((2, STEPS, NEX - 1)),
        ],
        compiler_params=pltpu.CompilerParams(
            collective_id=0, has_side_effects=True, vmem_limit_bytes=63 * 1024 * 1024
        ),
    )(
        queries,
        prompt_kv[:, :, :, 0, :],
        new_kv[:, :, 0, :],
        prompt_slot,
        residual,
        w_out,
        norm_gain.reshape(1, D),
        w_router.T,
        jnp.transpose(routes, (0, 2, 1)),
        w_gate[0],
        w_up[0],
        w_down[0],
    )


def solution(mesh):
    placed = (
        P(None, "dp", "expert"),
        P(None, "dp", None, "expert", None),
        P(None, "dp", "expert", None),
        P(),
        P(None, ("dp", "expert"), None),
        P("expert", None),
        P(),
        P(),
        P(None, ("dp", "expert"), None),
        P("expert", None, "dp"),
        P("expert", None, "dp"),
        P("expert", "dp", None),
    )
    return jax.shard_map(body, mesh=mesh, in_specs=placed, out_specs=P(None, ("dp", "expert"), None), check_vma=False)
```

```python
import math

import jax
import jax.numpy as jnp
from jax import lax
from jax.experimental import pallas as pl
from jax.experimental.pallas import tpu as pltpu
from jax.sharding import PartitionSpec as P

HEAD = 128
MESH = pl.DeviceIdType.MESH
BF = jnp.bfloat16
F32 = jnp.float32
NEG = -1e30

STEPS = 2
NDP = 16
NEX = 8
GROUPS = 64
D = 6144
HALF = D // 2
QUART = D // 4
FFD = 512
ROWS = 8
SLOTS = 32
TILE = 512
NA = 4096


def iota(shape, dim):
    return lax.broadcasted_iota(jnp.int32, shape, dim)


def dot(a, b):
    return jnp.dot(a, b, preferred_element_type=F32)


def dot_nt(a, b):
    return lax.dot_general(a, b, (((1,), (1,)), ((), ())), preferred_element_type=F32)


def ones_where(cond):
    return jnp.where(cond, 1.0, 0.0).astype(BF)


def to_column(row):
    n = row.shape[1]
    eye = iota((n, n), 0) == iota((n, n), 1)
    return jnp.sum(jnp.where(eye, row, 0), axis=1, keepdims=True)


def loop(n, fn):
    lax.fori_loop(0, n, lambda i, c: (fn(i), c)[1], 0)


def tile_at(i, base=0):
    return pl.ds(pl.multiple_of(base + i * TILE, TILE), TILE)


def kernel(
    q_ref, pkv_ref, nkv_ref, slot_ref, res_ref, wo_hbm, gain_ref, wr_ref, routes_ref, wg_hbm, wu_hbm, wd_hbm,
    out_ref,
    wo, wg, wu, wd,
    qs_send, qs_recv, at_send, at_recv, op_send, op_recv, ds_send, ds_recv,
    mixed, nb, gat, held, acc_g, acc_u, hid, pair, transit, ysum, zsum, zcross, rt_send, rt_recv,
    w_sem, q_sem, a_sem, o_sem, d_sem, g_sem, r_sem, t_sem,
):
    dp = lax.axis_index("dp")
    ex = lax.axis_index("expert")
    y = dp // 4
    zl = (dp // 2) % 2
    core = dp % 2

    def at_dp(dy, flip_z=0, flip_c=0):
        yy = (y + dy) % 4
        zz = 1 - zl if flip_z else zl
        cc = 1 - core if flip_c else core
        return yy * 4 + zz * 2 + cc

    to_arrive, to_leave = [], []

    def start(copy):
        copy.start()
        to_arrive.append(copy)
        to_leave.append(copy)

    def arrived(copy):
        copy.wait_recv()
        to_arrive[:] = [c for c in to_arrive if c is not copy]

    def left(copy):
        copy.wait_send()
        to_leave[:] = [c for c in to_leave if c is not copy]

    def remote(src, dst, sems, idx, to_dp, to_ex):
        return pltpu.make_async_remote_copy(
            src_ref=src,
            dst_ref=dst,
            send_sem=sems.at[(0, *idx)],
            recv_sem=sems.at[(1, *idx)],
            device_id=(to_dp, to_ex),
            device_id_type=MESH,
        )

    weights = [
        pltpu.make_async_copy(src, dst, w_sem.at[i])
        for i, (src, dst) in enumerate(((wo_hbm, wo), (wg_hbm, wg), (wu_hbm, wu), (wd_hbm, wd)))
    ]
    for copy in weights:
        copy.start()

    barrier = pltpu.get_barrier_semaphore()
    for d in range(1, NDP):
        pl.semaphore_signal(barrier, inc=1, device_id=((dp + d) % NDP, ex), device_id_type=MESH)
    for d in range(1, NEX):
        pl.semaphore_signal(barrier, inc=1, device_id=(dp, (ex + d) % NEX), device_id_type=MESH)

    row = iota((256, 128), 0)
    part_of = (row & 15) >> 2
    slot_rows = [slot_ref[t : t + 1, :] for t in range(STEPS)]
    r64 = iota((256, GROUPS), 0)
    want = 4 * (r64 >> 4) + (r64 & 3)

    def by_part(full):
        picked = jnp.zeros((256, HEAD), F32)
        for a in range(4):
            picked = jnp.where(part_of == a, full[:, a * HEAD : (a + 1) * HEAD], picked)
        return picked.astype(BF).reshape(NDP, 16, HEAD)

    for t in range(STEPS):
        order = ones_where(slot_rows[t] == want)
        first = dot(order, jnp.concatenate([q_ref[t], nkv_ref[t][:, :HEAD]], axis=1))
        qs_send[t, :, 0] = by_part(first)
        if t == 0:
            zero = jnp.zeros((GROUPS, 3 * HEAD), BF)
            second = jnp.concatenate([zero, nkv_ref[0][:, HEAD:]], axis=1)
        else:
            zero = jnp.zeros((GROUPS, HEAD), BF)
            second = jnp.concatenate([nkv_ref[0][:, :HEAD], zero, nkv_ref[0][:, HEAD:], nkv_ref[1][:, HEAD:]], axis=1)
        qs_send[t, :, 1] = by_part(dot(order, second))

    pl.semaphore_wait(barrier, NDP - 1 + NEX - 1)

    def spread_dp(send, recv, sems, t):
        copies = []
        for d in range(1, NDP):
            to = (dp + d) % NDP
            copies.append(remote(send.at[t, to], recv.at[t, dp], sems, (t, d - 1), to, ex))
        for copy in copies:
            start(copy)
        recv[t, dp] = send[t, dp]
        return copies

    q_copies = [spread_dp(qs_send, qs_recv, q_sem, t) for t in range(STEPS)]

    factor = 1.0 / math.sqrt(HEAD)
    r_s = iota((256, 1024), 0)
    own_prompt = (r_s & 3) == (iota((256, 1024), 1) >> 8)
    r_e, c_e = iota((256, 256), 0), iota((256, 256), 1)
    same_source = (r_e >> 4) == (c_e >> 4)

    def pick(block, base):
        return dot(ones_where(same_source & ((c_e & 15) == base + (r_e & 3))), block)

    a_copies = []
    for t in range(STEPS):
        for copy in q_copies[t]:
            arrived(copy)
        first = qs_recv[t, :, 0].reshape(256, HEAD)
        second = qs_recv[t, :, 1].reshape(256, HEAD)
        stored = pkv_ref[t].reshape(1024, 2 * HEAD)
        scores = jnp.where(own_prompt, dot_nt(first, stored[:, :HEAD]) * factor, NEG)
        first_f = first.astype(F32)
        recent = [(pick(first, 12), pick(second, 12))]
        if t == 1:
            recent.append((pick(second, 0), pick(second, 8)))
        recent_scores = [jnp.sum(first_f * keys, axis=1, keepdims=True) * factor for keys, _ in recent]
        peak = jnp.max(scores, axis=1, keepdims=True)
        for s in recent_scores:
            peak = jnp.maximum(peak, s)
        weight = jnp.exp(scores - peak)
        total = jnp.sum(weight, axis=1, keepdims=True)
        summed = dot(weight.astype(BF), stored[:, HEAD:])
        for s, (_, values) in zip(recent_scores, recent):
            w = jnp.exp(s - peak)
            total = total + w
            summed = summed + w.astype(BF).astype(F32) * values
        at_send[t] = (summed / total).astype(BF).reshape(NDP, 16, HEAD)
        a_copies.append(spread_dp(at_send, at_recv, a_sem, t))

    c64 = iota((GROUPS, 256), 1)
    want_c = 4 * (c64 >> 4) + (c64 & 3)
    weights[0].wait()

    def spread_ex(send, recv, sems, t):
        return [
            remote(send.at[t, (ex + d) % NEX], recv.at[t, ex], sems, (t, d - 1), dp, (ex + d) % NEX)
            for d in range(1, NEX)
        ]

    o_copies = []
    for t in range(STEPS):
        for copy in a_copies[t]:
            arrived(copy)
        back = at_recv[t].reshape(256, HEAD)
        back_f = back.astype(F32)
        parted = jnp.concatenate([jnp.where(part_of == a, back_f, 0.0).astype(BF) for a in range(3)], axis=1)
        order = ones_where(to_column(slot_rows[t]) == want_c)
        attended = dot(order, parted).astype(BF)

        def project(i, t=t, attended=attended):
            lo = dot(attended, wo[:, tile_at(i)])
            hi = dot(attended, wo[:, tile_at(i, HALF)])
            for e in range(NEX):
                both = jnp.concatenate([lo[e * 8 : e * 8 + 8], hi[e * 8 : e * 8 + 8]], axis=0)
                op_send[t, e, :, tile_at(i)] = both.astype(BF)

        loop(HALF // TILE, project)
        o_copies.append(spread_ex(op_send, op_recv, o_sem, t))
        for copy in o_copies[t]:
            start(copy)

    d_copies = [None, None]
    targets = [None, None]

    def mix(t):
        for copy in o_copies[t]:
            arrived(copy)

        def add(i, squares):
            total = op_send[t, ex, :, tile_at(i)].astype(F32)
            for d in range(1, NEX):
                total = total + op_recv[t, (ex + d) % NEX, :, tile_at(i)].astype(F32)
            lo = res_ref[t, :, tile_at(i)].astype(F32)
            hi = res_ref[t, :, tile_at(i, HALF)].astype(F32)
            total = total + jnp.concatenate([lo, hi], axis=0)
            mixed[t, :, tile_at(i)] = total
            return squares + total * total

        squares = lax.fori_loop(0, HALF // TILE, add, jnp.zeros((16, TILE), F32))
        per_half = jnp.sum(squares, axis=1, keepdims=True)
        inverse = 1.0 / jnp.sqrt((per_half[:8] + per_half[8:]) / D + 1e-05)
        inverse = jnp.concatenate([inverse, inverse], axis=0)

        def scale(i):
            lower = iota((16, TILE), 0) < 8
            gain = jnp.where(lower, gain_ref[:, tile_at(i)], gain_ref[:, tile_at(i, HALF)])
            nb[:, tile_at(i)] = (mixed[t, :, tile_at(i)] * inverse * gain).astype(BF)

        loop(HALF // TILE, scale)
        normed = nb[...].astype(F32)
        lo, hi = normed[:8], normed[8:]
        logits = dot_nt(lo.astype(BF), wr_ref[:, :HALF]) + dot_nt(hi.astype(BF), wr_ref[:, HALF:])
        rows = [routes_ref[t][k : k + 1, :] for k in range(2)]
        cols = [to_column(r) for r in rows]
        chosen = [jnp.sum(jnp.where(iota((8, 8), 1) == c, logits, 0.0), axis=1, keepdims=True) for c in cols]
        before = iota((8, 8), 1) < iota((8, 8), 0)
        cells = []
        for k in range(2):
            gat[t, k] = jnp.broadcast_to(jax.nn.sigmoid(chosen[k] - chosen[1 - k]), (8, 128))
            place = jnp.zeros((8, 1), jnp.int32)
            for other in rows:
                place = place + jnp.sum(jnp.where(before & (cols[k] == other), 1, 0), axis=1, keepdims=True)
            cells.append(cols[k] * 4 + place)
        targets[t] = cells
        c32 = iota((8, 32), 1) & 7
        cell_rows = [jnp.sum(jnp.where(c32 == iota((8, 32), 0), c, 0), axis=0, keepdims=True) for c in cells]
        r_d, c_d = iota((128, 32), 0), iota((128, 32), 1)
        cell = 4 * (r_d >> 4) + (r_d & 3)
        same_quarter = ((r_d & 15) >> 2) == (c_d >> 3)
        choose = ones_where(same_quarter & ((cell_rows[0] == cell) | (cell_rows[1] == cell)))
        quarters = jnp.concatenate([lo[:, :QUART], lo[:, QUART:], hi[:, :QUART], hi[:, QUART:]], axis=0).astype(BF)
        for i in range(QUART // TILE):
            cut = slice(i * TILE, (i + 1) * TILE)
            ds_send[t, :, :, cut] = dot(choose, quarters[:, cut]).astype(BF).reshape(NEX, 16, TILE)
        d_copies[t] = spread_ex(ds_send, ds_recv, d_sem, t)
        for copy in d_copies[t]:
            start(copy)

    r_u, c_u = iota((128, 128), 0), iota((128, 128), 1)
    unfold_matrix = ones_where(((r_u >> 5) == ((c_u & 15) >> 2)) & (((r_u & 31) >> 2) == (c_u >> 4)) & ((r_u & 3) == (c_u & 3)))
    fold_matrix = ones_where(((c_u >> 5) == ((r_u & 15) >> 2)) & (((c_u & 31) >> 2) == (r_u >> 4)) & ((c_u & 3) == (r_u & 3)))


    def unfold(t):
        for copy in d_copies[t]:
            arrived(copy)
        ds_recv[t, ex] = ds_send[t, ex]
        for i in range(QUART // TILE):
            cut = slice(i * TILE, (i + 1) * TILE)
            rows = dot(unfold_matrix, ds_recv[t, :, :, cut].reshape(128, TILE)).astype(BF)
            for quarter in range(4):
                start = quarter * QUART + i * TILE
                held[t, dp, :, start : start + TILE] = rows[quarter * SLOTS : (quarter + 1) * SLOTS]

    part_a, part_b = pl.ds(0, NA), pl.ds(NA, D - NA)
    whole = slice(None)
    lower, upper = pl.ds(0, 16), pl.ds(16, 16)
    g_copies = [{}, {}]

    def give(t, name, device, to_dp, rows=whole, columns=whole):
        ref = held.at[t, device, rows, columns]
        copy = remote(ref, ref, g_sem, (t, len(g_copies[t])), to_dp, ex)
        start(copy)
        g_copies[t][name] = copy

    def got(t, *names):
        for name in names:
            arrived(g_copies[t][name])

    def to_core(t, dy, plane):
        give(t, f"core{dy}{plane}", at_dp(dy, plane), at_dp(0, 0, 1))

    def gather_own(t):
        give(t, "z", dp, at_dp(0, 1), columns=part_a)
        give(t, "up0", dp, at_dp(1))
        give(t, "down0", dp, at_dp(3))
        give(t, "cross0", dp, at_dp(0, 1), columns=part_b)
        to_core(t, 0, 0)

    def gather_z(t):
        got(t, "z")
        give(t, "up1", at_dp(0, 1), at_dp(1), columns=part_a)
        give(t, "down1", at_dp(0, 1), at_dp(3), columns=part_a)

    def gather_near(t, plane):
        columns = part_a if plane else whole
        got(t, f"up{plane}")
        give(t, f"far_up{plane}", at_dp(3, plane), at_dp(1), lower, columns)
        got(t, f"down{plane}")
        give(t, f"far_down{plane}", at_dp(1, plane), at_dp(3), upper, columns)
        if plane == 0:
            for dy in (3, 1):
                give(t, f"cross{dy}", at_dp(dy), at_dp(0, 1), columns=part_b)
                to_core(t, dy, 0)

    def gather_far(t):
        got(t, "far_up0", "far_down0")
        give(t, "cross2", at_dp(2), at_dp(0, 1), columns=part_b)
        to_core(t, 2, 0)

    def gather_cross(t, *dys):
        for dy in dys:
            if dy == 2:
                got(t, "far_up1", "far_down1")
            got(t, f"cross{dy}")
            to_core(t, dy, 1)

    def gather_end(t):
        for dy in (0, 1, 3, 2):
            got(t, f"core{dy}0", f"core{dy}1")

    def gate_up(t, first, last):
        if first == 0:
            acc_g[...] = jnp.zeros_like(acc_g)
            acc_u[...] = jnp.zeros_like(acc_u)

        def step(i):
            x = held[t, :, :, tile_at(i, first * TILE)].reshape(NDP * SLOTS, TILE)
            acc_g[...] += dot(x, wg[tile_at(i, first * TILE), :])
            acc_u[...] += dot(x, wu[tile_at(i, first * TILE), :])

        loop(last - first, step)

    def activate(t):
        hid[...] = (jax.nn.silu(acc_g[...]) * acc_u[...]).astype(BF)
        for copy in g_copies[t].values():
            left(copy)

    def down(t, first, last):
        def step(i):
            y_part = dot(hid[...], wd[:, tile_at(i, first * TILE)])
            held[t, :, :, tile_at(i, first * TILE)] = y_part.astype(BF).reshape(NDP, SLOTS, TILE)

        loop(last - first, step)

    r_copies = [{}, {}]

    def pass_on(t, name, src, dst, to_dp):
        copy = remote(src, dst, r_sem, (t, len(r_copies[t])), to_dp, ex)
        start(copy)
        r_copies[t][name] = copy

    def came(t, *names):
        for name in names:
            arrived(r_copies[t][name])

    def part(t, dy, plane, rows, cut):
        return held[t, at_dp(dy, plane), rows, cut].astype(F32) + pair[t, 2 * dy + plane, rows, cut].astype(F32)

    def crossed(t, dy, rows, i):
        return zcross[t, dy, rows, tile_at(i)].astype(F32)

    def over_a(t, dy, plane, rows, *more):
        def step(i):
            cut = tile_at(i)
            total = part(t, dy, plane, rows, cut)
            for term in more:
                total = total + term(cut)
            held[t, at_dp(dy, plane), rows, cut] = total.astype(BF)

        loop(NA // TILE, step)

    def over_b(t, dy, plane, rows, *more):
        def step(i):
            cut = tile_at(i, NA)
            total = part(t, dy, plane, rows, cut)
            if plane == 0:
                total = total + crossed(t, dy, rows, i)
            for term in more:
                total = total + term(cut)
            held[t, at_dp(dy, plane), rows, cut] = total.astype(BF)

        loop((D - NA) // TILE, step)

    def reduce_cores(t):
        for dy, plane in ((2, 1), (1, 1), (3, 1), (0, 1), (2, 0), (1, 0), (3, 0), (0, 0)):
            kind = 2 * dy + plane
            pass_on(t, f"core{dy}{plane}", held.at[t, at_dp(dy, plane, 1)], pair.at[t, kind], at_dp(0, 0, 1))

    def send_transit(t, plane):
        columns = part_a if plane else whole
        for way, to_dy, rows in ((0, 1, lower), (1, 3, upper)):
            src = held.at[t, at_dp(2, plane), rows, columns]
            dst = transit.at[t, way, plane, whole, columns]
            pass_on(t, f"transit{way}{plane}", src, dst, at_dp(to_dy))

    def reduce_cross(t):
        for dy in (2, 1, 3, 0):
            came(t, f"core{dy}1")
            over_b(t, dy, 1, whole)
            pass_on(t, f"cross{dy}", held.at[t, at_dp(dy, 1), whole, part_b], zcross.at[t, dy], at_dp(0, 1))
            if dy == 2:
                over_a(t, 2, 1, whole)
                send_transit(t, 1)

    def send_sum(t, name, way, plane, rows):
        columns = part_a if plane else whole
        dy = 1 if way == 0 else 3
        src = held.at[t, at_dp(dy, plane), rows, columns]
        pass_on(t, f"{name}{way}{plane}", src, ysum.at[t, way, plane, rows, columns], at_dp(dy))

    def reduce_free1(t):
        for way, dy, rows in ((0, 1, upper), (1, 3, lower)):
            over_a(t, dy, 1, rows)
            send_sum(t, "free", way, 1, rows)

    def reduce_far(t):
        came(t, "core20", "cross2")
        over_a(t, 2, 0, whole)
        over_b(t, 2, 0, whole)
        send_transit(t, 0)

    def reduce_free0(t):
        for way, dy, rows in ((0, 1, upper), (1, 3, lower)):
            came(t, f"core{dy}0", f"cross{dy}")
            over_a(t, dy, 0, rows)
            over_b(t, dy, 0, rows)
            send_sum(t, "free", way, 0, rows)

    def reduce_bound(t, plane):
        for way, dy, rows in ((0, 1, lower), (1, 3, upper)):
            came(t, f"transit{way}{plane}")

            def moved(cut, way=way):
                return transit[t, way, plane, :, cut].astype(F32)

            over_a(t, dy, plane, rows, moved)
            if plane == 0:
                over_b(t, dy, plane, rows, moved)
            send_sum(t, "bound", way, plane, rows)

    def around(t, plane, cut):
        return ysum[t, 0, plane, :, cut].astype(F32) + ysum[t, 1, plane, :, cut].astype(F32)

    def came_around(t, plane):
        came(t, *(f"{name}{way}{plane}" for name in ("free", "bound") for way in range(2)))

    def reduce_here(t):
        came_around(t, 1)
        over_a(t, 0, 1, whole, lambda cut: around(t, 1, cut))
        pass_on(t, "z", held.at[t, at_dp(0, 1), whole, part_a], zsum.at[t], at_dp(0, 1))

    t_copies = [None, None]

    def finish(t):
        came_around(t, 0)
        came(t, "core00", "cross0", "z")
        for i in range(QUART // TILE):
            parts = []
            for quarter in range(4):
                cut = slice(quarter * QUART + i * TILE, quarter * QUART + (i + 1) * TILE)
                total = part(t, 0, 0, whole, cut) + around(t, 0, cut)
                if cut.start < NA:
                    total = total + zsum[t, :, cut].astype(F32)
                else:
                    total = total + zcross[t, 0, :, cut.start - NA : cut.stop - NA].astype(F32)
                parts.append(total.astype(BF))
            folded = dot(fold_matrix, jnp.concatenate(parts, axis=0)).astype(BF)
            rt_send[t, :, :, i * TILE : (i + 1) * TILE] = folded.reshape(NEX, 16, TILE)
        t_copies[t] = spread_ex(rt_send, rt_recv, t_sem, t)
        for copy in t_copies[t]:
            start(copy)
        rt_recv[t, ex] = rt_send[t, ex]

    def combine(t):
        for copy in t_copies[t]:
            arrived(copy)
        both = jnp.concatenate(targets[t], axis=0)
        c_c = iota((16, 128), 1)
        mine = both == 4 * (c_c >> 4) + (c_c & 3)
        gate0, gate1 = gat[t, 0][:, :1], gat[t, 1][:, :1]
        for i in range(QUART // TILE):
            came = rt_recv[t, :, :, i * TILE : (i + 1) * TILE].reshape(128, TILE)
            for quarter in range(4):
                out = dot(ones_where(mine & (((c_c & 15) >> 2) == quarter)), came)
                upper = (quarter // 2) * 8
                start = (quarter % 2) * QUART + i * TILE
                total = mixed[t, upper : upper + 8, start : start + TILE] + gate0 * out[:8] + gate1 * out[8:]
                place = quarter * QUART + i * TILE
                out_ref[t, :, place : place + TILE] = total.astype(BF)

    mix(0)
    unfold(0)
    gather_own(0)
    mix(1)
    gather_z(0)
    gather_near(0, 0)
    unfold(1)
    gather_near(0, 1)
    gather_own(1)
    gather_cross(0, 0, 1, 3)
    gather_far(0)
    gather_cross(0, 2)
    for copy in weights[1:]:
        copy.wait()
    gather_end(0)
    gate_up(0, 0, 6)
    gather_z(1)
    gate_up(0, 6, 12)
    gather_near(1, 0)
    activate(0)
    down(0, 0, 6)
    gather_near(1, 1)
    down(0, 6, 12)
    reduce_cores(0)
    gather_cross(1, 0, 1, 3)
    reduce_cross(0)
    reduce_free1(0)
    gather_far(1)
    reduce_far(0)
    reduce_free0(0)
    gather_cross(1, 2)
    gather_end(1)
    gate_up(1, 0, 4)
    reduce_bound(0, 1)
    gate_up(1, 4, 8)
    reduce_bound(0, 0)
    gate_up(1, 8, 12)
    activate(1)
    down(1, 0, 12)
    reduce_cores(1)
    reduce_here(0)
    reduce_cross(1)
    reduce_free1(1)
    reduce_far(1)
    reduce_free0(1)
    finish(0)
    reduce_bound(1, 1)
    reduce_bound(1, 0)
    combine(0)
    reduce_here(1)
    finish(1)
    combine(1)

    for copy in list(to_arrive):
        arrived(copy)
    for copy in list(to_leave):
        left(copy)


def body(queries, prompt_kv, new_kv, prompt_slot, residual, w_out, norm_gain, w_router, routes, w_gate, w_up, w_down):
    vmem = pl.BlockSpec(memory_space=pltpu.VMEM)
    hbm = pl.BlockSpec(memory_space=pl.ANY)
    dma = pltpu.SemaphoreType.DMA
    return pl.pallas_call(
        kernel,
        out_shape=jax.ShapeDtypeStruct((STEPS, ROWS, D), BF),
        in_specs=[vmem] * 5 + [hbm] + [vmem] * 3 + [hbm] * 3,
        out_specs=vmem,
        scratch_shapes=[
            pltpu.VMEM((3 * HEAD, D), BF),
            pltpu.VMEM((D, FFD), BF),
            pltpu.VMEM((D, FFD), BF),
            pltpu.VMEM((FFD, D), BF),
            pltpu.VMEM((STEPS, NDP, 2, 16, HEAD), BF),
            pltpu.VMEM((STEPS, NDP, 2, 16, HEAD), BF),
            pltpu.VMEM((STEPS, NDP, 16, HEAD), BF),
            pltpu.VMEM((STEPS, NDP, 16, HEAD), BF),
            pltpu.VMEM((STEPS, NEX, 16, HALF), BF),
            pltpu.VMEM((STEPS, NEX, 16, HALF), BF),
            pltpu.VMEM((STEPS, NEX, 16, QUART), BF),
            pltpu.VMEM((STEPS, NEX, 16, QUART), BF),
            pltpu.VMEM((STEPS, 16, HALF), F32),
            pltpu.VMEM((16, HALF), BF),
            pltpu.VMEM((STEPS, 2, 8, 128), F32),
            pltpu.VMEM((STEPS, NDP, SLOTS, D), BF),
            pltpu.VMEM((NDP * SLOTS, FFD), F32),
            pltpu.VMEM((NDP * SLOTS, FFD), F32),
            pltpu.VMEM((NDP * SLOTS, FFD), BF),
            pltpu.VMEM((STEPS, 8, SLOTS, D), BF),
            pltpu.VMEM((STEPS, 2, 2, 16, D), BF),
            pltpu.VMEM((STEPS, 2, 2, SLOTS, D), BF),
            pltpu.VMEM((STEPS, SLOTS, NA), BF),
            pltpu.VMEM((STEPS, 4, SLOTS, D - NA), BF),
            pltpu.VMEM((STEPS, NEX, 16, QUART), BF),
            pltpu.VMEM((STEPS, NEX, 16, QUART), BF),
            dma((4,)),
            dma((2, STEPS, NDP - 1)),
            dma((2, STEPS, NDP - 1)),
            dma((2, STEPS, NEX - 1)),
            dma((2, STEPS, NEX - 1)),
            dma((2, STEPS, 40)),
            dma((2, STEPS, 40)),
            dma((2, STEPS, NEX - 1)),
        ],
        compiler_params=pltpu.CompilerParams(
            collective_id=0, has_side_effects=True, vmem_limit_bytes=63 * 1024 * 1024
        ),
    )(
        queries,
        prompt_kv[:, :, :, 0, :],
        new_kv[:, :, 0, :],
        prompt_slot,
        residual,
        w_out,
        norm_gain.reshape(1, D),
        w_router.T,
        jnp.transpose(routes, (0, 2, 1)),
        w_gate[0],
        w_up[0],
        w_down[0],
    )


def solution(mesh):
    placed = (
        P(None, "dp", "expert"),
        P(None, "dp", None, "expert", None),
        P(None, "dp", "expert", None),
        P(),
        P(None, ("dp", "expert"), None),
        P("expert", None),
        P(),
        P(),
        P(None, ("dp", "expert"), None),
        P("expert", None, "dp"),
        P("expert", None, "dp"),
        P("expert", "dp", None),
    )
    return jax.shard_map(body, mesh=mesh, in_specs=placed, out_specs=P(None, ("dp", "expert"), None), check_vma=False)
```

```python
import math

import jax
import jax.numpy as jnp
from jax import lax
from jax.experimental import pallas as pl
from jax.experimental.pallas import tpu as pltpu
from jax.sharding import PartitionSpec as P

HEAD = 128
MESH = pl.DeviceIdType.MESH
BF = jnp.bfloat16
F32 = jnp.float32
NEG = -1e30

STEPS = 2
NDP = 16
NEX = 8
GROUPS = 64
D = 6144
HALF = D // 2
QUART = D // 4
FFD = 512
ROWS = 8
SLOTS = 32
TILE = 512
NA = 4608


def iota(shape, dim):
    return lax.broadcasted_iota(jnp.int32, shape, dim)


def dot(a, b):
    return jnp.dot(a, b, preferred_element_type=F32)


def dot_nt(a, b):
    return lax.dot_general(a, b, (((1,), (1,)), ((), ())), preferred_element_type=F32)


def ones_where(cond):
    return jnp.where(cond, 1.0, 0.0).astype(BF)


def to_column(row):
    n = row.shape[1]
    eye = iota((n, n), 0) == iota((n, n), 1)
    return jnp.sum(jnp.where(eye, row, 0), axis=1, keepdims=True)


def loop(n, fn):
    lax.fori_loop(0, n, lambda i, c: (fn(i), c)[1], 0)


def tile_at(i, base=0):
    return pl.ds(pl.multiple_of(base + i * TILE, TILE), TILE)


def kernel(
    q_ref, pkv_ref, nkv_ref, slot_ref, res_ref, wo_hbm, gain_ref, wr_ref, routes_ref, wg_hbm, wu_hbm, wd_hbm,
    out_ref,
    wo, wg, wu, wd,
    qs_send, qs_recv, at_send, at_recv, op_send, op_recv, ds_send, ds_recv,
    mixed, nb, gat, held, acc_g, acc_u, hid, pair, transit, ysum, zsum, zcross, rt_send, rt_recv,
    w_sem, q_sem, a_sem, o_sem, d_sem, g_sem, r_sem, t_sem,
):
    dp = lax.axis_index("dp")
    ex = lax.axis_index("expert")
    y = dp // 4
    zl = (dp // 2) % 2
    core = dp % 2

    def at_dp(dy, flip_z=0, flip_c=0):
        yy = (y + dy) % 4
        zz = 1 - zl if flip_z else zl
        cc = 1 - core if flip_c else core
        return yy * 4 + zz * 2 + cc

    to_arrive, to_leave = [], []

    def start(copy):
        copy.start()
        to_arrive.append(copy)
        to_leave.append(copy)

    def arrived(copy):
        copy.wait_recv()
        to_arrive[:] = [c for c in to_arrive if c is not copy]

    def left(copy):
        copy.wait_send()
        to_leave[:] = [c for c in to_leave if c is not copy]

    def remote(src, dst, sems, idx, to_dp, to_ex):
        return pltpu.make_async_remote_copy(
            src_ref=src,
            dst_ref=dst,
            send_sem=sems.at[(0, *idx)],
            recv_sem=sems.at[(1, *idx)],
            device_id=(to_dp, to_ex),
            device_id_type=MESH,
        )

    weights = [
        pltpu.make_async_copy(src, dst, w_sem.at[i])
        for i, (src, dst) in enumerate(((wo_hbm, wo), (wg_hbm, wg), (wu_hbm, wu), (wd_hbm, wd)))
    ]
    for copy in weights:
        copy.start()

    barrier = pltpu.get_barrier_semaphore()
    for d in range(1, NDP):
        pl.semaphore_signal(barrier, inc=1, device_id=((dp + d) % NDP, ex), device_id_type=MESH)
    for d in range(1, NEX):
        pl.semaphore_signal(barrier, inc=1, device_id=(dp, (ex + d) % NEX), device_id_type=MESH)
    for d in range(4):
        other = (4 - ex // 4 * 4) + d
        pl.semaphore_signal(barrier, inc=1, device_id=(at_dp(0, 1), other), device_id_type=MESH)

    row = iota((256, 128), 0)
    part_of = (row & 15) >> 2
    slot_rows = [slot_ref[t : t + 1, :] for t in range(STEPS)]
    r64 = iota((256, GROUPS), 0)
    want = 4 * (r64 >> 4) + (r64 & 3)

    def by_part(full):
        picked = jnp.zeros((256, HEAD), F32)
        for a in range(4):
            picked = jnp.where(part_of == a, full[:, a * HEAD : (a + 1) * HEAD], picked)
        return picked.astype(BF).reshape(NDP, 16, HEAD)

    for t in range(STEPS):
        order = ones_where(slot_rows[t] == want)
        first = dot(order, jnp.concatenate([q_ref[t], nkv_ref[t][:, :HEAD]], axis=1))
        qs_send[t, :, 0] = by_part(first)
        if t == 0:
            zero = jnp.zeros((GROUPS, 3 * HEAD), BF)
            second = jnp.concatenate([zero, nkv_ref[0][:, HEAD:]], axis=1)
        else:
            zero = jnp.zeros((GROUPS, HEAD), BF)
            second = jnp.concatenate([nkv_ref[0][:, :HEAD], zero, nkv_ref[0][:, HEAD:], nkv_ref[1][:, HEAD:]], axis=1)
        qs_send[t, :, 1] = by_part(dot(order, second))

    pl.semaphore_wait(barrier, NDP - 1 + NEX - 1 + 4)

    def spread_dp(send, recv, sems, t):
        copies = []
        for d in range(1, NDP):
            to = (dp + d) % NDP
            copies.append(remote(send.at[t, to], recv.at[t, dp], sems, (t, d - 1), to, ex))
        for copy in copies:
            start(copy)
        recv[t, dp] = send[t, dp]
        return copies

    q_copies = [spread_dp(qs_send, qs_recv, q_sem, t) for t in range(STEPS)]

    factor = 1.0 / math.sqrt(HEAD)
    r_s = iota((256, 1024), 0)
    own_prompt = (r_s & 3) == (iota((256, 1024), 1) >> 8)
    r_e, c_e = iota((256, 256), 0), iota((256, 256), 1)
    same_source = (r_e >> 4) == (c_e >> 4)

    def pick(block, base):
        return dot(ones_where(same_source & ((c_e & 15) == base + (r_e & 3))), block)

    a_copies = []
    for t in range(STEPS):
        for copy in q_copies[t]:
            arrived(copy)
        first = qs_recv[t, :, 0].reshape(256, HEAD)
        second = qs_recv[t, :, 1].reshape(256, HEAD)
        stored = pkv_ref[t].reshape(1024, 2 * HEAD)
        scores = jnp.where(own_prompt, dot_nt(first, stored[:, :HEAD]) * factor, NEG)
        first_f = first.astype(F32)
        recent = [(pick(first, 12), pick(second, 12))]
        if t == 1:
            recent.append((pick(second, 0), pick(second, 8)))
        recent_scores = [jnp.sum(first_f * keys, axis=1, keepdims=True) * factor for keys, _ in recent]
        peak = jnp.max(scores, axis=1, keepdims=True)
        for s in recent_scores:
            peak = jnp.maximum(peak, s)
        weight = jnp.exp(scores - peak)
        total = jnp.sum(weight, axis=1, keepdims=True)
        summed = dot(weight.astype(BF), stored[:, HEAD:])
        for s, (_, values) in zip(recent_scores, recent):
            w = jnp.exp(s - peak)
            total = total + w
            summed = summed + w.astype(BF).astype(F32) * values
        at_send[t] = (summed / total).astype(BF).reshape(NDP, 16, HEAD)
        a_copies.append(spread_dp(at_send, at_recv, a_sem, t))

    c64 = iota((GROUPS, 256), 1)
    want_c = 4 * (c64 >> 4) + (c64 & 3)
    weights[0].wait()

    def crossing(other):
        return y * 4 + (zl + other // 4 + ex // 4) % 2 * 2 + core

    def spread_ex(send, recv, sems, t, nearest=True):
        copies = []
        for d in range(1, NEX):
            other = (ex + d) % NEX
            to = crossing(other) if nearest else dp
            copies.append(remote(send.at[t, other], recv.at[t, ex], sems, (t, d - 1), to, other))
        return copies

    o_copies = []
    for t in range(STEPS):
        for copy in a_copies[t]:
            arrived(copy)
        back = at_recv[t].reshape(256, HEAD)
        back_f = back.astype(F32)
        parted = jnp.concatenate([jnp.where(part_of == a, back_f, 0.0).astype(BF) for a in range(3)], axis=1)
        order = ones_where(to_column(slot_rows[t]) == want_c)
        attended = dot(order, parted).astype(BF)

        def project(i, t=t, attended=attended):
            lo = dot(attended, wo[:, tile_at(i)])
            hi = dot(attended, wo[:, tile_at(i, HALF)])
            for e in range(NEX):
                both = jnp.concatenate([lo[e * 8 : e * 8 + 8], hi[e * 8 : e * 8 + 8]], axis=0)
                op_send[t, e, :, tile_at(i)] = both.astype(BF)

        loop(HALF // TILE, project)
        o_copies.append(spread_ex(op_send, op_recv, o_sem, t, nearest=False))
        if t == 0:
            for copy in o_copies[0]:
                start(copy)

    d_copies = [None, None]
    targets = [None, None]

    def mix(t):
        for copy in o_copies[t]:
            arrived(copy)

        def add(i, squares):
            total = op_send[t, ex, :, tile_at(i)].astype(F32)
            for d in range(1, NEX):
                total = total + op_recv[t, (ex + d) % NEX, :, tile_at(i)].astype(F32)
            lo = res_ref[t, :, tile_at(i)].astype(F32)
            hi = res_ref[t, :, tile_at(i, HALF)].astype(F32)
            total = total + jnp.concatenate([lo, hi], axis=0)
            mixed[t, :, tile_at(i)] = total
            return squares + total * total

        squares = lax.fori_loop(0, HALF // TILE, add, jnp.zeros((16, TILE), F32))
        per_half = jnp.sum(squares, axis=1, keepdims=True)
        inverse = 1.0 / jnp.sqrt((per_half[:8] + per_half[8:]) / D + 1e-05)
        inverse = jnp.concatenate([inverse, inverse], axis=0)

        def scale(i):
            lower = iota((16, TILE), 0) < 8
            gain = jnp.where(lower, gain_ref[:, tile_at(i)], gain_ref[:, tile_at(i, HALF)])
            nb[:, tile_at(i)] = (mixed[t, :, tile_at(i)] * inverse * gain).astype(BF)

        loop(HALF // TILE, scale)
        normed = nb[...].astype(F32)
        lo, hi = normed[:8], normed[8:]
        logits = dot_nt(lo.astype(BF), wr_ref[:, :HALF]) + dot_nt(hi.astype(BF), wr_ref[:, HALF:])
        rows = [routes_ref[t][k : k + 1, :] for k in range(2)]
        cols = [to_column(r) for r in rows]
        chosen = [jnp.sum(jnp.where(iota((8, 8), 1) == c, logits, 0.0), axis=1, keepdims=True) for c in cols]
        before = iota((8, 8), 1) < iota((8, 8), 0)
        cells = []
        for k in range(2):
            gat[t, k] = jnp.broadcast_to(jax.nn.sigmoid(chosen[k] - chosen[1 - k]), (8, 128))
            place = jnp.zeros((8, 1), jnp.int32)
            for other in rows:
                place = place + jnp.sum(jnp.where(before & (cols[k] == other), 1, 0), axis=1, keepdims=True)
            cells.append(cols[k] * 4 + place)
        targets[t] = cells
        c32 = iota((8, 32), 1) & 7
        cell_rows = [jnp.sum(jnp.where(c32 == iota((8, 32), 0), c, 0), axis=0, keepdims=True) for c in cells]
        r_d, c_d = iota((128, 32), 0), iota((128, 32), 1)
        cell = 4 * (r_d >> 4) + (r_d & 3)
        same_quarter = ((r_d & 15) >> 2) == (c_d >> 3)
        choose = ones_where(same_quarter & ((cell_rows[0] == cell) | (cell_rows[1] == cell)))
        quarters = jnp.concatenate([lo[:, :QUART], lo[:, QUART:], hi[:, :QUART], hi[:, QUART:]], axis=0).astype(BF)
        for i in range(QUART // TILE):
            cut = slice(i * TILE, (i + 1) * TILE)
            ds_send[t, :, :, cut] = dot(choose, quarters[:, cut]).astype(BF).reshape(NEX, 16, TILE)
        d_copies[t] = spread_ex(ds_send, ds_recv, d_sem, t)
        for copy in d_copies[t]:
            start(copy)
        if t == 0:
            for copy in o_copies[1]:
                start(copy)

    r_u, c_u = iota((128, 128), 0), iota((128, 128), 1)
    unfold_matrix = ones_where(((r_u >> 5) == ((c_u & 15) >> 2)) & (((r_u & 31) >> 2) == (c_u >> 4)) & ((r_u & 3) == (c_u & 3)))
    fold_matrix = ones_where(((c_u >> 5) == ((r_u & 15) >> 2)) & (((c_u & 31) >> 2) == (r_u >> 4)) & ((c_u & 3) == (r_u & 3)))


    def unfold(t):
        for copy in d_copies[t]:
            arrived(copy)
        ds_recv[t, ex] = ds_send[t, ex]
        for i in range(QUART // TILE):
            cut = slice(i * TILE, (i + 1) * TILE)
            rows = dot(unfold_matrix, ds_recv[t, :, :, cut].reshape(128, TILE)).astype(BF)
            for quarter in range(4):
                start = quarter * QUART + i * TILE
                held[t, dp, :, start : start + TILE] = rows[quarter * SLOTS : (quarter + 1) * SLOTS]

    part_a, part_b = pl.ds(0, NA), pl.ds(NA, D - NA)
    whole = slice(None)
    lower, upper = pl.ds(0, 16), pl.ds(16, 16)
    g_copies = [{}, {}]

    def give(t, name, device, to_dp, rows=whole, columns=whole):
        ref = held.at[t, device, rows, columns]
        copy = remote(ref, ref, g_sem, (t, len(g_copies[t])), to_dp, ex)
        start(copy)
        g_copies[t][name] = copy

    def got(t, *names):
        for name in names:
            arrived(g_copies[t][name])

    def to_core(t, dy, plane):
        give(t, f"core{dy}{plane}", at_dp(dy, plane), at_dp(0, 0, 1))

    def gather_own(t):
        give(t, "z", dp, at_dp(0, 1), columns=part_a)
        give(t, "up0", dp, at_dp(1))
        give(t, "down0", dp, at_dp(3))
        give(t, "cross0", dp, at_dp(0, 1), columns=part_b)
        to_core(t, 0, 0)

    def gather_z(t):
        got(t, "z")
        give(t, "up1", at_dp(0, 1), at_dp(1), columns=part_a)
        give(t, "down1", at_dp(0, 1), at_dp(3), columns=part_a)

    def gather_near(t, plane):
        columns = part_a if plane else whole
        got(t, f"up{plane}")
        give(t, f"far_up{plane}", at_dp(3, plane), at_dp(1), lower, columns)
        got(t, f"down{plane}")
        give(t, f"far_down{plane}", at_dp(1, plane), at_dp(3), upper, columns)
        if plane == 0:
            for dy in (3, 1):
                give(t, f"cross{dy}", at_dp(dy), at_dp(0, 1), columns=part_b)
                to_core(t, dy, 0)

    def gather_far(t):
        got(t, "far_up0", "far_down0")
        give(t, "cross2", at_dp(2), at_dp(0, 1), columns=part_b)
        to_core(t, 2, 0)

    def gather_cross(t, *dys):
        for dy in dys:
            if dy == 2:
                got(t, "far_up1", "far_down1")
            got(t, f"cross{dy}")
            to_core(t, dy, 1)

    def gather_end(t):
        for dy in (0, 1, 3, 2):
            got(t, f"core{dy}0", f"core{dy}1")

    def gate_up(t, first, last):
        if first == 0:
            acc_g[...] = jnp.zeros_like(acc_g)
            acc_u[...] = jnp.zeros_like(acc_u)

        def step(i):
            x = held[t, :, :, tile_at(i, first * TILE)].reshape(NDP * SLOTS, TILE)
            acc_g[...] += dot(x, wg[tile_at(i, first * TILE), :])
            acc_u[...] += dot(x, wu[tile_at(i, first * TILE), :])

        loop(last - first, step)

    def activate(t):
        hid[...] = (jax.nn.silu(acc_g[...]) * acc_u[...]).astype(BF)
        for copy in g_copies[t].values():
            left(copy)

    def down(t, first, last):
        def step(i):
            y_part = dot(hid[...], wd[:, tile_at(i, first * TILE)])
            held[t, :, :, tile_at(i, first * TILE)] = y_part.astype(BF).reshape(NDP, SLOTS, TILE)

        loop(last - first, step)

    r_copies = [{}, {}]

    def pass_on(t, name, src, dst, to_dp):
        copy = remote(src, dst, r_sem, (t, len(r_copies[t])), to_dp, ex)
        start(copy)
        r_copies[t][name] = copy

    def came(t, *names):
        for name in names:
            arrived(r_copies[t][name])

    def part(t, dy, plane, rows, cut):
        return held[t, at_dp(dy, plane), rows, cut].astype(F32) + pair[t, 2 * dy + plane, rows, cut].astype(F32)

    def crossed(t, dy, rows, i):
        return zcross[t, dy, rows, tile_at(i)].astype(F32)

    def over_a(t, dy, plane, rows, *more):
        def step(i):
            cut = tile_at(i)
            total = part(t, dy, plane, rows, cut)
            for term in more:
                total = total + term(cut)
            held[t, at_dp(dy, plane), rows, cut] = total.astype(BF)

        loop(NA // TILE, step)

    def over_b(t, dy, plane, rows, *more):
        def step(i):
            cut = tile_at(i, NA)
            total = part(t, dy, plane, rows, cut)
            if plane == 0:
                total = total + crossed(t, dy, rows, i)
            for term in more:
                total = total + term(cut)
            held[t, at_dp(dy, plane), rows, cut] = total.astype(BF)

        loop((D - NA) // TILE, step)

    def reduce_cores(t):
        for dy, plane in ((2, 1), (1, 1), (3, 1), (0, 1), (2, 0), (1, 0), (3, 0), (0, 0)):
            kind = 2 * dy + plane
            pass_on(t, f"core{dy}{plane}", held.at[t, at_dp(dy, plane, 1)], pair.at[t, kind], at_dp(0, 0, 1))

    def send_transit(t, plane):
        columns = part_a if plane else whole
        for way, to_dy, rows in ((0, 1, lower), (1, 3, upper)):
            src = held.at[t, at_dp(2, plane), rows, columns]
            dst = transit.at[t, way, plane, whole, columns]
            pass_on(t, f"transit{way}{plane}", src, dst, at_dp(to_dy))

    def reduce_cross(t):
        for dy in (2, 1, 3, 0):
            came(t, f"core{dy}1")
            over_b(t, dy, 1, whole)
            pass_on(t, f"cross{dy}", held.at[t, at_dp(dy, 1), whole, part_b], zcross.at[t, dy], at_dp(0, 1))
            if dy == 2:
                over_a(t, 2, 1, whole)
                send_transit(t, 1)

    def send_sum(t, name, way, plane, rows):
        columns = part_a if plane else whole
        dy = 1 if way == 0 else 3
        src = held.at[t, at_dp(dy, plane), rows, columns]
        pass_on(t, f"{name}{way}{plane}", src, ysum.at[t, way, plane, rows, columns], at_dp(dy))

    def reduce_free1(t):
        for way, dy, rows in ((0, 1, upper), (1, 3, lower)):
            over_a(t, dy, 1, rows)
            send_sum(t, "free", way, 1, rows)

    def reduce_far(t):
        came(t, "core20", "cross2")
        over_a(t, 2, 0, whole)
        over_b(t, 2, 0, whole)
        send_transit(t, 0)

    def reduce_free0(t):
        for way, dy, rows in ((0, 1, upper), (1, 3, lower)):
            came(t, f"core{dy}0", f"cross{dy}")
            over_a(t, dy, 0, rows)
            over_b(t, dy, 0, rows)
            send_sum(t, "free", way, 0, rows)

    def reduce_bound(t, plane):
        for way, dy, rows in ((0, 1, lower), (1, 3, upper)):
            came(t, f"transit{way}{plane}")

            def moved(cut, way=way):
                return transit[t, way, plane, :, cut].astype(F32)

            over_a(t, dy, plane, rows, moved)
            if plane == 0:
                over_b(t, dy, plane, rows, moved)
            send_sum(t, "bound", way, plane, rows)

    def around(t, plane, cut):
        return ysum[t, 0, plane, :, cut].astype(F32) + ysum[t, 1, plane, :, cut].astype(F32)

    def came_around(t, plane):
        came(t, *(f"{name}{way}{plane}" for name in ("free", "bound") for way in range(2)))

    def reduce_here(t):
        came_around(t, 1)
        over_a(t, 0, 1, whole, lambda cut: around(t, 1, cut))
        pass_on(t, "z", held.at[t, at_dp(0, 1), whole, part_a], zsum.at[t], at_dp(0, 1))

    t_copies = [None, None]

    def finish(t):
        came_around(t, 0)
        came(t, "core00", "cross0", "z")
        for i in range(QUART // TILE):
            parts = []
            for quarter in range(4):
                cut = slice(quarter * QUART + i * TILE, quarter * QUART + (i + 1) * TILE)
                total = part(t, 0, 0, whole, cut) + around(t, 0, cut)
                if cut.start < NA:
                    total = total + zsum[t, :, cut].astype(F32)
                else:
                    total = total + zcross[t, 0, :, cut.start - NA : cut.stop - NA].astype(F32)
                parts.append(total.astype(BF))
            folded = dot(fold_matrix, jnp.concatenate(parts, axis=0)).astype(BF)
            rt_send[t, :, :, i * TILE : (i + 1) * TILE] = folded.reshape(NEX, 16, TILE)
        t_copies[t] = spread_ex(rt_send, rt_recv, t_sem, t)
        for copy in t_copies[t]:
            start(copy)
        rt_recv[t, ex] = rt_send[t, ex]

    def combine(t):
        for copy in t_copies[t]:
            arrived(copy)
        both = jnp.concatenate(targets[t], axis=0)
        c_c = iota((16, 128), 1)
        mine = both == 4 * (c_c >> 4) + (c_c & 3)
        gate0, gate1 = gat[t, 0][:, :1], gat[t, 1][:, :1]
        for i in range(QUART // TILE):
            came = rt_recv[t, :, :, i * TILE : (i + 1) * TILE].reshape(128, TILE)
            for quarter in range(4):
                out = dot(ones_where(mine & (((c_c & 15) >> 2) == quarter)), came)
                upper = (quarter // 2) * 8
                start = (quarter % 2) * QUART + i * TILE
                total = mixed[t, upper : upper + 8, start : start + TILE] + gate0 * out[:8] + gate1 * out[8:]
                place = quarter * QUART + i * TILE
                out_ref[t, :, place : place + TILE] = total.astype(BF)

    mix(0)
    unfold(0)
    gather_own(0)
    mix(1)
    gather_z(0)
    gather_near(0, 0)
    unfold(1)
    gather_near(0, 1)
    gather_own(1)
    gather_cross(0, 0, 1, 3)
    gather_far(0)
    gather_cross(0, 2)
    for copy in weights[1:]:
        copy.wait()
    gather_end(0)
    gate_up(0, 0, 6)
    gather_z(1)
    gate_up(0, 6, 12)
    gather_near(1, 0)
    activate(0)
    down(0, 0, 6)
    gather_near(1, 1)
    down(0, 6, 12)
    reduce_cores(0)
    gather_cross(1, 0, 1, 3)
    gather_far(1)
    gather_cross(1, 2)
    reduce_cross(0)
    reduce_free1(0)
    reduce_far(0)
    gather_end(1)
    gate_up(1, 0, 3)
    reduce_bound(0, 1)
    reduce_free0(0)
    gate_up(1, 3, 9)
    reduce_bound(0, 0)
    gate_up(1, 9, 12)
    activate(1)
    down(1, 0, 12)
    reduce_cores(1)
    reduce_here(0)
    reduce_cross(1)
    reduce_free1(1)
    reduce_far(1)
    finish(0)
    reduce_bound(1, 1)
    reduce_free0(1)
    reduce_bound(1, 0)
    combine(0)
    reduce_here(1)
    finish(1)
    combine(1)

    for copy in list(to_arrive):
        arrived(copy)
    for copy in list(to_leave):
        left(copy)


def body(queries, prompt_kv, new_kv, prompt_slot, residual, w_out, norm_gain, w_router, routes, w_gate, w_up, w_down):
    vmem = pl.BlockSpec(memory_space=pltpu.VMEM)
    hbm = pl.BlockSpec(memory_space=pl.ANY)
    dma = pltpu.SemaphoreType.DMA
    return pl.pallas_call(
        kernel,
        out_shape=jax.ShapeDtypeStruct((STEPS, ROWS, D), BF),
        in_specs=[vmem] * 5 + [hbm] + [vmem] * 3 + [hbm] * 3,
        out_specs=vmem,
        scratch_shapes=[
            pltpu.VMEM((3 * HEAD, D), BF),
            pltpu.VMEM((D, FFD), BF),
            pltpu.VMEM((D, FFD), BF),
            pltpu.VMEM((FFD, D), BF),
            pltpu.VMEM((STEPS, NDP, 2, 16, HEAD), BF),
            pltpu.VMEM((STEPS, NDP, 2, 16, HEAD), BF),
            pltpu.VMEM((STEPS, NDP, 16, HEAD), BF),
            pltpu.VMEM((STEPS, NDP, 16, HEAD), BF),
            pltpu.VMEM((STEPS, NEX, 16, HALF), BF),
            pltpu.VMEM((STEPS, NEX, 16, HALF), BF),
            pltpu.VMEM((STEPS, NEX, 16, QUART), BF),
            pltpu.VMEM((STEPS, NEX, 16, QUART), BF),
            pltpu.VMEM((STEPS, 16, HALF), F32),
            pltpu.VMEM((16, HALF), BF),
            pltpu.VMEM((STEPS, 2, 8, 128), F32),
            pltpu.VMEM((STEPS, NDP, SLOTS, D), BF),
            pltpu.VMEM((NDP * SLOTS, FFD), F32),
            pltpu.VMEM((NDP * SLOTS, FFD), F32),
            pltpu.VMEM((NDP * SLOTS, FFD), BF),
            pltpu.VMEM((STEPS, 8, SLOTS, D), BF),
            pltpu.VMEM((STEPS, 2, 2, 16, D), BF),
            pltpu.VMEM((STEPS, 2, 2, SLOTS, D), BF),
            pltpu.VMEM((STEPS, SLOTS, NA), BF),
            pltpu.VMEM((STEPS, 4, SLOTS, D - NA), BF),
            pltpu.VMEM((STEPS, NEX, 16, QUART), BF),
            pltpu.VMEM((STEPS, NEX, 16, QUART), BF),
            dma((4,)),
            dma((2, STEPS, NDP - 1)),
            dma((2, STEPS, NDP - 1)),
            dma((2, STEPS, NEX - 1)),
            dma((2, STEPS, NEX - 1)),
            dma((2, STEPS, 40)),
            dma((2, STEPS, 40)),
            dma((2, STEPS, NEX - 1)),
        ],
        compiler_params=pltpu.CompilerParams(
            collective_id=0, has_side_effects=True, vmem_limit_bytes=63 * 1024 * 1024
        ),
    )(
        queries,
        prompt_kv[:, :, :, 0, :],
        new_kv[:, :, 0, :],
        prompt_slot,
        residual,
        w_out,
        norm_gain.reshape(1, D),
        w_router.T,
        jnp.transpose(routes, (0, 2, 1)),
        w_gate[0],
        w_up[0],
        w_down[0],
    )


def solution(mesh):
    placed = (
        P(None, "dp", "expert"),
        P(None, "dp", None, "expert", None),
        P(None, "dp", "expert", None),
        P(),
        P(None, ("dp", "expert"), None),
        P("expert", None),
        P(),
        P(),
        P(None, ("dp", "expert"), None),
        P("expert", None, "dp"),
        P("expert", None, "dp"),
        P("expert", "dp", None),
    )
    return jax.shard_map(body, mesh=mesh, in_specs=placed, out_specs=P(None, ("dp", "expert"), None), check_vma=False)
```

```python
import math

import jax
import jax.numpy as jnp
from jax import lax
from jax.experimental import pallas as pl
from jax.experimental.pallas import tpu as pltpu
from jax.sharding import PartitionSpec as P

HEAD = 128
MESH = pl.DeviceIdType.MESH
BF = jnp.bfloat16
F32 = jnp.float32
NEG = -1e30

STEPS = 2
NDP = 16
NEX = 8
GROUPS = 64
D = 6144
HALF = D // 2
NC = 2048
AB = D - NC
QUART = AB // 4
RAW = NC // 2 + 128
FFD = 512
ROWS = 8
SLOTS = 32
TILE = 512
NA = 3072


def iota(shape, dim):
    return lax.broadcasted_iota(jnp.int32, shape, dim)


def dot(a, b):
    return jnp.dot(a, b, preferred_element_type=F32)


def dot_nt(a, b):
    return lax.dot_general(a, b, (((1,), (1,)), ((), ())), preferred_element_type=F32)


def ones_where(cond):
    return jnp.where(cond, 1.0, 0.0).astype(BF)


def to_column(row):
    n = row.shape[1]
    eye = iota((n, n), 0) == iota((n, n), 1)
    return jnp.sum(jnp.where(eye, row, 0), axis=1, keepdims=True)


def loop(n, fn):
    lax.fori_loop(0, n, lambda i, c: (fn(i), c)[1], 0)


def tile_at(i, base=0):
    return pl.ds(pl.multiple_of(base + i * TILE, TILE), TILE)


def kernel(
    q_ref, pkv_ref, nkv_ref, slot_ref, res_ref, wo_hbm, gain_ref, wr_ref, routes_ref, wg_hbm, wu_hbm, wd_hbm,
    out_ref,
    wg, wu, wd,
    qs_send, qs_recv, at_send, at_recv, op_send, op_recv, ds_send, ds_recv,
    mixed, nb, gat, held, acc_g, acc_u, hid, pair, transit, ysum, zsum, zcross, rt_send, rt_recv,
    raw_send, raw_recv, cs_send, cs_recv, cr_recv, y_send, y_recv,
    w_sem, q_sem, a_sem, o_sem, d_sem, g_sem, r_sem, t_sem, raw_sem, dc_sem, ec_sem, y_sem,
):
    dp = lax.axis_index("dp")
    ex = lax.axis_index("expert")
    y = dp // 4
    zl = (dp // 2) % 2
    core = dp % 2

    def at_dp(dy, flip_z=0, flip_c=0):
        yy = (y + dy) % 4
        zz = 1 - zl if flip_z else zl
        cc = 1 - core if flip_c else core
        return yy * 4 + zz * 2 + cc

    to_arrive, to_leave = [], []

    def start(copy):
        copy.start()
        to_arrive.append(copy)
        to_leave.append(copy)

    def arrived(copy):
        copy.wait_recv()
        to_arrive[:] = [c for c in to_arrive if c is not copy]

    def left(copy):
        copy.wait_send()
        to_leave[:] = [c for c in to_leave if c is not copy]

    def remote(src, dst, sems, idx, to_dp, to_ex):
        return pltpu.make_async_remote_copy(
            src_ref=src,
            dst_ref=dst,
            send_sem=sems.at[(0, *idx)],
            recv_sem=sems.at[(1, *idx)],
            device_id=(to_dp, to_ex),
            device_id_type=MESH,
        )

    wo = pair.at[pl.ds(0, 3 * HEAD)]
    weights = [
        pltpu.make_async_copy(src, dst, w_sem.at[i])
        for i, (src, dst) in enumerate(((wo_hbm, wo), (wg_hbm, wg), (wu_hbm, wu), (wd_hbm, wd)))
    ]
    for copy in weights:
        copy.start()

    barrier = pltpu.get_barrier_semaphore()
    for d in range(1, NDP):
        pl.semaphore_signal(barrier, inc=1, device_id=((dp + d) % NDP, ex), device_id_type=MESH)
    for d in range(1, NEX):
        pl.semaphore_signal(barrier, inc=1, device_id=(dp, (ex + d) % NEX), device_id_type=MESH)
    for d in range(4):
        other = (4 - ex // 4 * 4) + d
        pl.semaphore_signal(barrier, inc=1, device_id=(at_dp(0, 1), other), device_id_type=MESH)

    row = iota((256, 128), 0)
    part_of = (row & 15) >> 2
    slot_rows = [slot_ref[t : t + 1, :] for t in range(STEPS)]
    r64 = iota((256, GROUPS), 0)
    want = 4 * (r64 >> 4) + (r64 & 3)

    def by_part(full):
        picked = jnp.zeros((256, HEAD), F32)
        for a in range(4):
            picked = jnp.where(part_of == a, full[:, a * HEAD : (a + 1) * HEAD], picked)
        return picked.astype(BF).reshape(NDP, 16, HEAD)

    for t in range(STEPS):
        order = ones_where(slot_rows[t] == want)
        first = dot(order, jnp.concatenate([q_ref[t], nkv_ref[t][:, :HEAD]], axis=1))
        qs_send[t, :, 0] = by_part(first)
        if t == 0:
            zero = jnp.zeros((GROUPS, 3 * HEAD), BF)
            second = jnp.concatenate([zero, nkv_ref[0][:, HEAD:]], axis=1)
        else:
            zero = jnp.zeros((GROUPS, HEAD), BF)
            second = jnp.concatenate([nkv_ref[0][:, :HEAD], zero, nkv_ref[0][:, HEAD:], nkv_ref[1][:, HEAD:]], axis=1)
        qs_send[t, :, 1] = by_part(dot(order, second))

    pl.semaphore_wait(barrier, NDP - 1 + NEX - 1 + 4)

    def spread_dp(send, recv, sems, t):
        copies = []
        for d in range(1, NDP):
            to = (dp + d) % NDP
            copies.append(remote(send.at[t, to], recv.at[t, dp], sems, (t, d - 1), to, ex))
        for copy in copies:
            start(copy)
        recv[t, dp] = send[t, dp]
        return copies

    q_copies = [spread_dp(qs_send, qs_recv, q_sem, t) for t in range(STEPS)]

    factor = 1.0 / math.sqrt(HEAD)
    r_s = iota((256, 1024), 0)
    own_prompt = (r_s & 3) == (iota((256, 1024), 1) >> 8)
    r_e, c_e = iota((256, 256), 0), iota((256, 256), 1)
    same_source = (r_e >> 4) == (c_e >> 4)

    def pick(block, base):
        return dot(ones_where(same_source & ((c_e & 15) == base + (r_e & 3))), block)

    a_copies = []
    for t in range(STEPS):
        for copy in q_copies[t]:
            arrived(copy)
        first = qs_recv[t, :, 0].reshape(256, HEAD)
        second = qs_recv[t, :, 1].reshape(256, HEAD)
        stored = pkv_ref[t].reshape(1024, 2 * HEAD)
        scores = jnp.where(own_prompt, dot_nt(first, stored[:, :HEAD]) * factor, NEG)
        first_f = first.astype(F32)
        recent = [(pick(first, 12), pick(second, 12))]
        if t == 1:
            recent.append((pick(second, 0), pick(second, 8)))
        recent_scores = [jnp.sum(first_f * keys, axis=1, keepdims=True) * factor for keys, _ in recent]
        peak = jnp.max(scores, axis=1, keepdims=True)
        for s in recent_scores:
            peak = jnp.maximum(peak, s)
        weight = jnp.exp(scores - peak)
        total = jnp.sum(weight, axis=1, keepdims=True)
        summed = dot(weight.astype(BF), stored[:, HEAD:])
        for s, (_, values) in zip(recent_scores, recent):
            w = jnp.exp(s - peak)
            total = total + w
            summed = summed + w.astype(BF).astype(F32) * values
        at_send[t] = (summed / total).astype(BF).reshape(NDP, 16, HEAD)
        a_copies.append(spread_dp(at_send, at_recv, a_sem, t))

    c64 = iota((GROUPS, 256), 1)
    want_c = 4 * (c64 >> 4) + (c64 & 3)
    weights[0].wait()

    def crossing(other):
        return y * 4 + (zl + other // 4 + ex // 4) % 2 * 2 + core

    def spread_ex(send, recv, sems, t, nearest=True):
        copies = []
        for d in range(1, NEX):
            other = (ex + d) % NEX
            to = crossing(other) if nearest else dp
            copies.append(remote(send.at[t, other], recv.at[t, ex], sems, (t, d - 1), to, other))
        return copies

    o_copies = []
    for t in range(STEPS):
        for copy in a_copies[t]:
            arrived(copy)
        back = at_recv[t].reshape(256, HEAD)
        back_f = back.astype(F32)
        parted = jnp.concatenate([jnp.where(part_of == a, back_f, 0.0).astype(BF) for a in range(3)], axis=1)
        order = ones_where(to_column(slot_rows[t]) == want_c)
        attended = dot(order, parted).astype(BF)

        def project(i, t=t, attended=attended):
            lo = dot(attended, pair[pl.ds(0, 3 * HEAD), tile_at(i)])
            hi = dot(attended, pair[pl.ds(0, 3 * HEAD), tile_at(i, HALF)])
            for e in range(NEX):
                both = jnp.concatenate([lo[e * 8 : e * 8 + 8], hi[e * 8 : e * 8 + 8]], axis=0)
                op_send[t, e, :, tile_at(i)] = both.astype(BF)

        loop(HALF // TILE, project)
        o_copies.append(spread_ex(op_send, op_recv, o_sem, t, nearest=False))
        if t == 0:
            for copy in o_copies[0]:
                start(copy)

    d_copies = [None, None]
    targets = [None, None]
    raw_copies = [[], []]
    chip = dp // 2

    def mix(t):
        for copy in o_copies[t]:
            arrived(copy)

        def add(i, squares):
            total = op_send[t, ex, :, tile_at(i)].astype(F32)
            for d in range(1, NEX):
                total = total + op_recv[t, (ex + d) % NEX, :, tile_at(i)].astype(F32)
            lo = res_ref[t, :, tile_at(i)].astype(F32)
            hi = res_ref[t, :, tile_at(i, HALF)].astype(F32)
            total = total + jnp.concatenate([lo, hi], axis=0)
            mixed[t, :, tile_at(i)] = total
            return squares + total * total

        squares = lax.fori_loop(0, HALF // TILE, add, jnp.zeros((16, TILE), F32))
        per_half = jnp.sum(squares, axis=1, keepdims=True)
        inverse = 1.0 / jnp.sqrt((per_half[:8] + per_half[8:]) / D + 1e-05)
        inverse = jnp.concatenate([inverse, inverse], axis=0)

        def scale(i):
            lower = iota((16, TILE), 0) < 8
            gain = jnp.where(lower, gain_ref[:, tile_at(i)], gain_ref[:, tile_at(i, HALF)])
            nb[:, tile_at(i)] = (mixed[t, :, tile_at(i)] * inverse * gain).astype(BF)

        loop(HALF // TILE, scale)
        normed = nb[...].astype(F32)
        lo, hi = normed[:8], normed[8:]
        logits = dot_nt(lo.astype(BF), wr_ref[:, :HALF]) + dot_nt(hi.astype(BF), wr_ref[:, HALF:])
        rows = [routes_ref[t][k : k + 1, :] for k in range(2)]
        cols = [to_column(r) for r in rows]
        chosen = [jnp.sum(jnp.where(iota((8, 8), 1) == c, logits, 0.0), axis=1, keepdims=True) for c in cols]
        before = iota((8, 8), 1) < iota((8, 8), 0)
        cells, gates = [], []
        for k in range(2):
            gate = jax.nn.sigmoid(chosen[k] - chosen[1 - k])
            gat[t, k] = jnp.broadcast_to(gate, (8, 128))
            rounded = gate.astype(BF).astype(F32)
            gates += [rounded, gate - rounded]
            place = jnp.zeros((8, 1), jnp.int32)
            for other in rows:
                place = place + jnp.sum(jnp.where(before & (cols[k] == other), 1, 0), axis=1, keepdims=True)
            cells.append(cols[k] * 4 + place)
        targets[t] = cells
        c32 = iota((8, 32), 1) & 7
        cell_rows = [jnp.sum(jnp.where(c32 == iota((8, 32), 0), c, 0), axis=0, keepdims=True) for c in cells]
        r_d, c_d = iota((128, 32), 0), iota((128, 32), 1)
        cell = 4 * (r_d >> 4) + (r_d & 3)
        same_quarter = ((r_d & 15) >> 2) == (c_d >> 3)
        choose = ones_where(same_quarter & ((cell_rows[0] == cell) | (cell_rows[1] == cell)))
        quarters = jnp.concatenate([lo[:, :QUART], lo[:, QUART : 2 * QUART], lo[:, 2 * QUART :], hi[:, :QUART]], axis=0).astype(BF)
        for i in range(QUART // TILE):
            cut = slice(i * TILE, (i + 1) * TILE)
            ds_send[t, :, :, cut] = dot(choose, quarters[:, cut]).astype(BF).reshape(NEX, 16, TILE)
        d_copies[t] = spread_ex(ds_send, ds_recv, d_sem, t)
        for copy in d_copies[t]:
            start(copy)
        lane = iota((8, 128), 1)
        info = jnp.zeros((8, 128), F32)
        for i, v in enumerate([c.astype(F32) for c in cells] + gates):
            info = jnp.where(lane == i, v, info)
        raw_send[t, :, NC // 2 :] = jnp.concatenate([info, info], axis=0).astype(BF)
        raw_send[t, :, : NC // 2] = jnp.concatenate([hi[:, QUART : 2 * QUART], hi[:, 2 * QUART :]], axis=0).astype(BF)
        for d in range(1, 8):
            copy = remote(raw_send.at[t], raw_recv.at[t, chip], raw_sem, (t, d), at_dp(d // 2, d % 2), ex)
            start(copy)
            raw_copies[t].append(copy)
        raw_recv[t, chip] = raw_send[t]
        if t == 0:
            for copy in o_copies[1]:
                start(copy)

    r_u, c_u = iota((128, 128), 0), iota((128, 128), 1)
    unfold_matrix = ones_where(((r_u >> 5) == ((c_u & 15) >> 2)) & (((r_u & 31) >> 2) == (c_u >> 4)) & ((r_u & 3) == (c_u & 3)))
    fold_matrix = ones_where(((c_u >> 5) == ((r_u & 15) >> 2)) & (((c_u & 31) >> 2) == (r_u >> 4)) & ((c_u & 3) == (r_u & 3)))


    def unfold(t):
        for copy in d_copies[t]:
            arrived(copy)
        ds_recv[t, ex] = ds_send[t, ex]
        for i in range(QUART // TILE):
            cut = slice(i * TILE, (i + 1) * TILE)
            rows = dot(unfold_matrix, ds_recv[t, :, :, cut].reshape(128, TILE)).astype(BF)
            for quarter in range(4):
                start = quarter * QUART + i * TILE
                held[t, dp, :, start : start + TILE] = rows[quarter * SLOTS : (quarter + 1) * SLOTS]

    zh = ex // 4
    r256, c256 = iota((256, 256), 0), iota((256, 256), 1)

    def swap(cross_of, flip_row):
        cross = (cross_of >> 2) ^ zh
        major, minor = r256 >> 5, (r256 & 31) >> 2
        col_major, col_minor = c256 >> 5, (c256 & 31) >> 2
        if flip_row:
            same = (minor == col_major) & ((major ^ cross) == col_minor)
        else:
            same = (major == col_minor) & (minor == (col_major ^ cross))
        return ones_where(same & ((r256 & 3) == (c256 & 3)))

    to_chips = swap((r256 & 31) >> 2, True)
    to_experts = swap(r256 >> 5, False)
    dc_copies = [None, None]
    info_of = [None, None]

    def dispatch_c(t):
        for copy in raw_copies[t]:
            arrived(copy)
        info = raw_recv[t, :, :, NC // 2 :].reshape(128, 128).astype(F32)
        info_of[t] = info
        eye = iota((128, 128), 0) == iota((128, 128), 1)
        wanted = [jnp.sum(jnp.where(eye, info[:, k : k + 1], 0.0), axis=0, keepdims=True) for k in range(2)]
        r, c = iota((256, 128), 0), iota((256, 128), 1)
        cell = (4 * (r >> 5) + (r & 3)).astype(F32)
        match = ((wanted[0] == cell) | (wanted[1] == cell)) & (((r & 31) >> 2) == (c >> 4))
        for h in range(2):
            choose = ones_where(match & (((c & 15) >> 3) == h))
            for i in range(NC // 2 // TILE):
                cut = slice(i * TILE, (i + 1) * TILE)
                out = dot(choose, raw_recv[t, :, :, cut].reshape(128, TILE)).astype(BF)
                cs_send[t, :, :, h * (NC // 2) + i * TILE : h * (NC // 2) + (i + 1) * TILE] = out.reshape(NEX, SLOTS, TILE)
        dc_copies[t] = spread_ex(cs_send, cs_recv, dc_sem, t)
        for copy in dc_copies[t]:
            start(copy)
        cs_recv[t, ex] = cs_send[t, ex]

    def place_c(t):
        for copy in dc_copies[t]:
            arrived(copy)
        for i in range(NC // TILE):
            cut = slice(i * TILE, (i + 1) * TILE)
            out = dot(to_chips, cs_recv[t, :, :, cut].reshape(256, TILE)).astype(BF)
            for k in range(8):
                held[t, k * 2 + core, :, AB + i * TILE : AB + (i + 1) * TILE] = out[k * SLOTS : (k + 1) * SLOTS]
        for d in range(8):
            give(t, f"last{d}", at_dp(d // 2, d % 2), at_dp(0, 0, 1), columns=part_c)

    part_a, part_b = pl.ds(0, NA), pl.ds(NA, AB - NA)
    part_ab, part_c = pl.ds(0, AB), pl.ds(AB, NC)
    whole = slice(None)
    lower, upper = pl.ds(0, 16), pl.ds(16, 16)
    g_copies = [{}, {}]

    def give(t, name, device, to_dp, rows=whole, columns=part_ab):
        ref = held.at[t, device, rows, columns]
        copy = remote(ref, ref, g_sem, (t, len(g_copies[t])), to_dp, ex)
        start(copy)
        g_copies[t][name] = copy

    def got(t, *names):
        for name in names:
            arrived(g_copies[t][name])

    def to_core(t, dy, plane):
        give(t, f"core{dy}{plane}", at_dp(dy, plane), at_dp(0, 0, 1))

    def gather_own(t):
        give(t, "z", dp, at_dp(0, 1), columns=part_a)
        give(t, "up0", dp, at_dp(1))
        give(t, "down0", dp, at_dp(3))
        give(t, "cross0", dp, at_dp(0, 1), columns=part_b)
        to_core(t, 0, 0)

    def gather_z(t):
        got(t, "z")
        give(t, "up1", at_dp(0, 1), at_dp(1), columns=part_a)
        give(t, "down1", at_dp(0, 1), at_dp(3), columns=part_a)

    def gather_near(t, plane):
        columns = part_a if plane else part_ab
        got(t, f"up{plane}")
        give(t, f"far_up{plane}", at_dp(3, plane), at_dp(1), lower, columns)
        got(t, f"down{plane}")
        give(t, f"far_down{plane}", at_dp(1, plane), at_dp(3), upper, columns)
        if plane == 0:
            for dy in (3, 1):
                give(t, f"cross{dy}", at_dp(dy), at_dp(0, 1), columns=part_b)
                to_core(t, dy, 0)

    def gather_far(t):
        got(t, "far_up0", "far_down0")
        give(t, "cross2", at_dp(2), at_dp(0, 1), columns=part_b)
        to_core(t, 2, 0)

    def gather_cross(t, *dys):
        for dy in dys:
            if dy == 2:
                got(t, "far_up1", "far_down1")
            got(t, f"cross{dy}")
            to_core(t, dy, 1)

    def gather_end(t):
        for dy in (0, 1, 3, 2):
            got(t, f"core{dy}0", f"core{dy}1")

    def gather_last(t):
        got(t, *(f"last{d}" for d in range(8)))

    def gate_up(t, first, last):
        if first == 0:
            acc_g[...] = jnp.zeros_like(acc_g)
            acc_u[...] = jnp.zeros_like(acc_u)

        def step(i):
            x = held[t, :, :, tile_at(i, first * TILE)].reshape(NDP * SLOTS, TILE)
            acc_g[...] += dot(x, wg[tile_at(i, first * TILE), :])
            acc_u[...] += dot(x, wu[tile_at(i, first * TILE), :])

        loop(last - first, step)

    def activate(t):
        hid[...] = (jax.nn.silu(acc_g[...]) * acc_u[...]).astype(BF)
        for copy in g_copies[t].values():
            left(copy)

    def down(t, first, last):
        def step(i):
            y_part = dot(hid[...], wd[:, tile_at(i, first * TILE)])
            held[t, :, :, tile_at(i, first * TILE)] = y_part.astype(BF).reshape(NDP, SLOTS, TILE)

        loop(last - first, step)

    r_copies = [{}, {}]

    def pass_on(t, name, src, dst, to_dp):
        copy = remote(src, dst, r_sem, (t, len(r_copies[t])), to_dp, ex)
        start(copy)
        r_copies[t][name] = copy

    def came(t, *names):
        for name in names:
            if any(c is r_copies[t][name] for c in to_arrive):
                arrived(r_copies[t][name])

    def pair_rows(t, kind, rows=whole):
        start, size = (0, SLOTS) if rows is whole else (rows.start, rows.size)
        return pl.ds(pl.multiple_of((t * 8 + kind) * SLOTS + start, 16), size)

    def part(t, dy, plane, rows, cut):
        other = pair[pair_rows(t, 2 * dy + plane, rows), cut]
        return held[t, at_dp(dy, plane), rows, cut].astype(F32) + other.astype(F32)

    def crossed(t, dy, rows, i):
        return zcross[t, dy, rows, tile_at(i)].astype(F32)

    def over_a(t, dy, plane, rows, *more):
        def step(i):
            cut = tile_at(i)
            total = part(t, dy, plane, rows, cut)
            for term in more:
                total = total + term(cut)
            held[t, at_dp(dy, plane), rows, cut] = total.astype(BF)

        loop(NA // TILE, step)

    def over_b(t, dy, plane, rows, *more):
        def step(i):
            cut = tile_at(i, NA)
            total = part(t, dy, plane, rows, cut)
            if plane == 0:
                total = total + crossed(t, dy, rows, i)
            for term in more:
                total = total + term(cut)
            held[t, at_dp(dy, plane), rows, cut] = total.astype(BF)

        loop((AB - NA) // TILE, step)

    def reduce_cores(t, name, columns):
        for dy, plane in ((2, 1), (1, 1), (3, 1), (0, 1), (2, 0), (1, 0), (3, 0), (0, 0)):
            src = held.at[t, at_dp(dy, plane, 1), whole, columns]
            dst = pair.at[pair_rows(t, 2 * dy + plane), columns]
            pass_on(t, f"{name}{dy}{plane}", src, dst, at_dp(0, 0, 1))

    def send_transit(t, plane):
        columns = part_a if plane else part_ab
        for way, to_dy, rows in ((0, 1, lower), (1, 3, upper)):
            src = held.at[t, at_dp(2, plane), rows, columns]
            dst = transit.at[t, way, plane, whole, columns]
            pass_on(t, f"transit{way}{plane}", src, dst, at_dp(to_dy))

    def reduce_cross(t):
        for dy in (2, 1, 3, 0):
            came(t, f"core{dy}1")
            over_b(t, dy, 1, whole)
            pass_on(t, f"cross{dy}", held.at[t, at_dp(dy, 1), whole, part_b], zcross.at[t, dy], at_dp(0, 1))
            if dy == 2:
                over_a(t, 2, 1, whole)
                send_transit(t, 1)

    def send_sum(t, name, way, plane, rows):
        columns = part_a if plane else part_ab
        dy = 1 if way == 0 else 3
        src = held.at[t, at_dp(dy, plane), rows, columns]
        pass_on(t, f"{name}{way}{plane}", src, ysum.at[t, way, plane, rows, columns], at_dp(dy))

    def reduce_free1(t):
        for way, dy, rows in ((0, 1, upper), (1, 3, lower)):
            over_a(t, dy, 1, rows)
            send_sum(t, "free", way, 1, rows)

    def reduce_far(t):
        came(t, "core20", "cross2")
        over_a(t, 2, 0, whole)
        over_b(t, 2, 0, whole)
        send_transit(t, 0)

    def reduce_free0(t):
        for way, dy, rows in ((0, 1, upper), (1, 3, lower)):
            came(t, f"core{dy}0", f"cross{dy}")
            over_a(t, dy, 0, rows)
            over_b(t, dy, 0, rows)
            send_sum(t, "free", way, 0, rows)

    def reduce_bound(t, plane):
        for way, dy, rows in ((0, 1, lower), (1, 3, upper)):
            came(t, f"transit{way}{plane}")

            def moved(cut, way=way):
                return transit[t, way, plane, :, cut].astype(F32)

            over_a(t, dy, plane, rows, moved)
            if plane == 0:
                over_b(t, dy, plane, rows, moved)
            send_sum(t, "bound", way, plane, rows)

    def around(t, plane, cut):
        return ysum[t, 0, plane, :, cut].astype(F32) + ysum[t, 1, plane, :, cut].astype(F32)

    def came_around(t, plane):
        came(t, *(f"{name}{way}{plane}" for name in ("free", "bound") for way in range(2)))

    def reduce_here(t):
        came_around(t, 1)
        over_a(t, 0, 1, whole, lambda cut: around(t, 1, cut))
        pass_on(t, "z", held.at[t, at_dp(0, 1), whole, part_a], zsum.at[t], at_dp(0, 1))

    ec_copies = [None, None]
    y_copies = [[], []]

    def reduce_c(t):
        for copy in dc_copies[t]:
            left(copy)
        came(t, *(f"last{dy}{plane}" for dy in range(4) for plane in range(2)))
        for i in range(NC // TILE):
            cut = slice(AB + i * TILE, AB + (i + 1) * TILE)
            parts = []
            for k in range(8):
                kind = (k // 2 + 4 - y) % 4 * 2 + (k % 2 + zl) % 2
                total = held[t, k * 2 + core, :, cut].astype(F32) + pair[pair_rows(t, kind), cut].astype(F32)
                parts.append(total.astype(BF))
            out = dot(to_experts, jnp.concatenate(parts, axis=0)).astype(BF)
            cs_send[t, :, :, i * TILE : (i + 1) * TILE] = out.reshape(NEX, SLOTS, TILE)
        ec_copies[t] = spread_ex(cs_send, cr_recv, ec_sem, t)
        for copy in ec_copies[t]:
            start(copy)
        cr_recv[t, ex] = cs_send[t, ex]

    def combine_c(t):
        for copy in ec_copies[t]:
            arrived(copy)
        info = raw_recv[t, :, :, NC // 2 :].reshape(128, 128).astype(F32)
        r, c = iota((128, 256), 0), iota((128, 256), 1)
        cell = (4 * (c >> 5) + (c & 3)).astype(F32)
        same = ((c & 31) >> 2) == (r >> 4)
        choose = [ones_where(same & (info[:, k : k + 1] == cell)) for k in range(2)]
        gate = [info[:, 2 + 2 * k : 3 + 2 * k] + info[:, 3 + 2 * k : 4 + 2 * k] for k in range(2)]
        first_half = (iota((128, TILE), 0) & 15) < 8

        def both(start):
            came_in = cr_recv[t, :, :, start : start + TILE].reshape(256, TILE)
            return gate[0] * dot(choose[0], came_in) + gate[1] * dot(choose[1], came_in)

        for i in range(NC // 2 // TILE):
            out = jnp.where(first_half, both(i * TILE), both(NC // 2 + i * TILE)).astype(BF)
            y_send[t, :, :, i * TILE : (i + 1) * TILE] = out.reshape(8, 16, TILE)
        for d in range(1, 8):
            to_y, to_z = (y + d // 2) % 4, (zl + d % 2) % 2
            src = y_send.at[t, to_y * 2 + to_z]
            copy = remote(src, y_recv.at[t, chip], y_sem, (t, d), at_dp(d // 2, d % 2), ex)
            start(copy)
            y_copies[t].append(copy)
        y_recv[t, chip] = y_send[t, chip]

    t_copies = [None, None]

    def finish(t):
        came_around(t, 0)
        came(t, "core00", "cross0", "z")
        for i in range(QUART // TILE):
            parts = []
            for quarter in range(4):
                cut = slice(quarter * QUART + i * TILE, quarter * QUART + (i + 1) * TILE)
                total = part(t, 0, 0, whole, cut) + around(t, 0, cut)
                if cut.start < NA:
                    total = total + zsum[t, :, cut].astype(F32)
                else:
                    total = total + zcross[t, 0, :, cut.start - NA : cut.stop - NA].astype(F32)
                parts.append(total.astype(BF))
            folded = dot(fold_matrix, jnp.concatenate(parts, axis=0)).astype(BF)
            rt_send[t, :, :, i * TILE : (i + 1) * TILE] = folded.reshape(NEX, 16, TILE)
        t_copies[t] = spread_ex(rt_send, rt_recv, t_sem, t)
        for copy in t_copies[t]:
            start(copy)
        rt_recv[t, ex] = rt_send[t, ex]

    def combine(t):
        for copy in t_copies[t]:
            arrived(copy)
        both = jnp.concatenate(targets[t], axis=0)
        c_c = iota((16, 128), 1)
        mine = both == 4 * (c_c >> 4) + (c_c & 3)
        gate0, gate1 = gat[t, 0][:, :1], gat[t, 1][:, :1]
        for i in range(QUART // TILE):
            came = rt_recv[t, :, :, i * TILE : (i + 1) * TILE].reshape(128, TILE)
            for quarter in range(4):
                out = dot(ones_where(mine & (((c_c & 15) >> 2) == quarter)), came)
                place = quarter * QUART + i * TILE
                first, start = place // HALF * 8, place % HALF
                total = mixed[t, first : first + 8, start : start + TILE] + gate0 * out[:8] + gate1 * out[8:]
                out_ref[t, :, place : place + TILE] = total.astype(BF)

    def combine_last(t):
        for copy in y_copies[t]:
            arrived(copy)
        for i in range(NC // 2 // TILE):
            total = jnp.zeros((16, TILE), F32)
            for k in range(8):
                total = total + y_recv[t, k, :, i * TILE : (i + 1) * TILE].astype(F32)
            for h in range(2):
                place = AB + h * (NC // 2) + i * TILE
                both = mixed[t, 8:, place - HALF : place - HALF + TILE] + total[8 * h : 8 * h + 8]
                out_ref[t, :, place : place + TILE] = both.astype(BF)

    mix(0)
    unfold(0)
    gather_own(0)
    gather_z(0)
    gather_near(0, 0)
    mix(1)
    dispatch_c(0)
    gather_near(0, 1)
    unfold(1)
    gather_own(1)
    gather_cross(0, 0, 1, 3)
    gather_far(0)
    gather_cross(0, 2)
    dispatch_c(1)
    gather_z(1)
    for copy in weights[1:]:
        copy.wait()
    gather_end(0)
    gate_up(0, 0, 4)
    gather_near(1, 0)
    gate_up(0, 4, 8)
    place_c(0)
    gather_near(1, 1)
    gather_cross(1, 0, 1, 3)
    gather_last(0)
    gate_up(0, 8, 12)
    gather_far(1)
    activate(0)
    down(0, 8, 12)
    reduce_cores(0, "last", part_c)
    gather_cross(1, 2)
    down(0, 0, 8)
    reduce_cores(0, "core", part_ab)
    reduce_c(0)
    gather_end(1)
    reduce_cross(0)
    reduce_free1(0)
    gate_up(1, 0, 2)
    reduce_far(0)
    gate_up(1, 2, 5)
    reduce_bound(0, 1)
    reduce_free0(0)
    gate_up(1, 5, 8)
    place_c(1)
    reduce_bound(0, 0)
    gather_last(1)
    gate_up(1, 8, 12)
    activate(1)
    down(1, 8, 12)
    reduce_cores(1, "last", part_c)
    combine_c(0)
    down(1, 0, 4)
    reduce_here(0)
    reduce_c(1)
    down(1, 4, 8)
    reduce_cores(1, "core", part_ab)
    finish(0)
    reduce_cross(1)
    reduce_free1(1)
    reduce_far(1)
    reduce_bound(1, 1)
    reduce_free0(1)
    reduce_bound(1, 0)
    combine(0)
    combine_last(0)
    combine_c(1)
    reduce_here(1)
    finish(1)
    combine_last(1)
    combine(1)

    for copy in list(to_arrive):
        arrived(copy)
    for copy in list(to_leave):
        left(copy)


def body(queries, prompt_kv, new_kv, prompt_slot, residual, w_out, norm_gain, w_router, routes, w_gate, w_up, w_down):
    vmem = pl.BlockSpec(memory_space=pltpu.VMEM)
    hbm = pl.BlockSpec(memory_space=pl.ANY)
    dma = pltpu.SemaphoreType.DMA
    return pl.pallas_call(
        kernel,
        out_shape=jax.ShapeDtypeStruct((STEPS, ROWS, D), BF),
        in_specs=[vmem] * 5 + [hbm] + [vmem] * 3 + [hbm] * 3,
        out_specs=vmem,
        scratch_shapes=[
            pltpu.VMEM((D, FFD), BF),
            pltpu.VMEM((D, FFD), BF),
            pltpu.VMEM((FFD, D), BF),
            pltpu.VMEM((STEPS, NDP, 2, 16, HEAD), BF),
            pltpu.VMEM((STEPS, NDP, 2, 16, HEAD), BF),
            pltpu.VMEM((STEPS, NDP, 16, HEAD), BF),
            pltpu.VMEM((STEPS, NDP, 16, HEAD), BF),
            pltpu.VMEM((STEPS, NEX, 16, HALF), BF),
            pltpu.VMEM((STEPS, NEX, 16, HALF), BF),
            pltpu.VMEM((STEPS, NEX, 16, QUART), BF),
            pltpu.VMEM((STEPS, NEX, 16, QUART), BF),
            pltpu.VMEM((STEPS, 16, HALF), F32),
            pltpu.VMEM((16, HALF), BF),
            pltpu.VMEM((STEPS, 2, 8, 128), F32),
            pltpu.VMEM((STEPS, NDP, SLOTS, D), BF),
            pltpu.VMEM((NDP * SLOTS, FFD), F32),
            pltpu.VMEM((NDP * SLOTS, FFD), F32),
            pltpu.VMEM((NDP * SLOTS, FFD), BF),
            pltpu.VMEM((STEPS * 8 * SLOTS, D), BF),
            pltpu.VMEM((STEPS, 2, 2, 16, AB), BF),
            pltpu.VMEM((STEPS, 2, 2, SLOTS, AB), BF),
            pltpu.VMEM((STEPS, SLOTS, NA), BF),
            pltpu.VMEM((STEPS, 4, SLOTS, AB - NA), BF),
            pltpu.VMEM((STEPS, NEX, 16, QUART), BF),
            pltpu.VMEM((STEPS, NEX, 16, QUART), BF),
            pltpu.VMEM((STEPS, 16, RAW), BF),
            pltpu.VMEM((STEPS, 8, 16, RAW), BF),
            pltpu.VMEM((STEPS, NEX, SLOTS, NC), BF),
            pltpu.VMEM((STEPS, NEX, SLOTS, NC), BF),
            pltpu.VMEM((STEPS, NEX, SLOTS, NC), BF),
            pltpu.VMEM((STEPS, 8, 16, NC // 2), BF),
            pltpu.VMEM((STEPS, 8, 16, NC // 2), BF),
            dma((4,)),
            dma((2, STEPS, NDP - 1)),
            dma((2, STEPS, NDP - 1)),
            dma((2, STEPS, NEX - 1)),
            dma((2, STEPS, NEX - 1)),
            dma((2, STEPS, 40)),
            dma((2, STEPS, 40)),
            dma((2, STEPS, NEX - 1)),
            dma((2, STEPS, 8)),
            dma((2, STEPS, NEX - 1)),
            dma((2, STEPS, NEX - 1)),
            dma((2, STEPS, 8)),
        ],
        compiler_params=pltpu.CompilerParams(
            collective_id=0, has_side_effects=True, vmem_limit_bytes=63 * 1024 * 1024
        ),
    )(
        queries,
        prompt_kv[:, :, :, 0, :],
        new_kv[:, :, 0, :],
        prompt_slot,
        residual,
        w_out,
        norm_gain.reshape(1, D),
        w_router.T,
        jnp.transpose(routes, (0, 2, 1)),
        w_gate[0],
        w_up[0],
        w_down[0],
    )


def solution(mesh):
    placed = (
        P(None, "dp", "expert"),
        P(None, "dp", None, "expert", None),
        P(None, "dp", "expert", None),
        P(),
        P(None, ("dp", "expert"), None),
        P("expert", None),
        P(),
        P(),
        P(None, ("dp", "expert"), None),
        P("expert", None, "dp"),
        P("expert", None, "dp"),
        P("expert", "dp", None),
    )
    return jax.shard_map(body, mesh=mesh, in_specs=placed, out_specs=P(None, ("dp", "expert"), None), check_vma=False)
```

```python
import math

import jax
import jax.numpy as jnp
from jax import lax
from jax.experimental import pallas as pl
from jax.experimental.pallas import tpu as pltpu
from jax.sharding import PartitionSpec as P

HEAD = 128
MESH = pl.DeviceIdType.MESH
BF = jnp.bfloat16
F32 = jnp.float32
NEG = -1e30

STEPS = 2
NDP = 16
NEX = 8
GROUPS = 64
D = 6144
HALF = D // 2
NC = 2048
AB = D - NC
QUART = AB // 4
RAW = NC // 2 + 128
FFD = 512
ROWS = 8
SLOTS = 32
TILE = 512
NA = 3072


def iota(shape, dim):
    return lax.broadcasted_iota(jnp.int32, shape, dim)


def dot(a, b):
    return jnp.dot(a, b, preferred_element_type=F32)


def dot_nt(a, b):
    return lax.dot_general(a, b, (((1,), (1,)), ((), ())), preferred_element_type=F32)


def ones_where(cond):
    return jnp.where(cond, 1.0, 0.0).astype(BF)


def to_column(row):
    n = row.shape[1]
    eye = iota((n, n), 0) == iota((n, n), 1)
    return jnp.sum(jnp.where(eye, row, 0), axis=1, keepdims=True)


def loop(n, fn):
    lax.fori_loop(0, n, lambda i, c: (fn(i), c)[1], 0)


def tile_at(i, base=0):
    return pl.ds(pl.multiple_of(base + i * TILE, TILE), TILE)


def kernel(
    q_ref, pkv_ref, nkv_ref, slot_ref, res_ref, wo_hbm, gain_ref, wr_ref, routes_ref, wg_hbm, wu_hbm, wd_hbm,
    out_ref,
    wg, wu, wd,
    qs_send, qs_recv, at_send, at_recv, op_send, op_recv, ds_send, ds_recv,
    mixed, nb, gat, held, acc_g, acc_u, hid, pair, transit, ysum, zsum, zcross, rt_send, rt_recv,
    raw_send, raw_recv, cs_send, cs_recv, cr_recv, y_send, y_recv,
    w_sem, q_sem, a_sem, o_sem, d_sem, g_sem, r_sem, t_sem, raw_sem, dc_sem, ec_sem, y_sem,
):
    dp = lax.axis_index("dp")
    ex = lax.axis_index("expert")
    y = dp // 4
    zl = (dp // 2) % 2
    core = dp % 2

    def at_dp(dy, flip_z=0, flip_c=0):
        yy = (y + dy) % 4
        zz = 1 - zl if flip_z else zl
        cc = 1 - core if flip_c else core
        return yy * 4 + zz * 2 + cc

    to_arrive, to_leave = [], []

    def start(copy):
        copy.start()
        to_arrive.append(copy)
        to_leave.append(copy)

    def arrived(copy):
        copy.wait_recv()
        to_arrive[:] = [c for c in to_arrive if c is not copy]

    def left(copy):
        copy.wait_send()
        to_leave[:] = [c for c in to_leave if c is not copy]

    def remote(src, dst, sems, idx, to_dp, to_ex):
        return pltpu.make_async_remote_copy(
            src_ref=src,
            dst_ref=dst,
            send_sem=sems.at[(0, *idx)],
            recv_sem=sems.at[(1, *idx)],
            device_id=(to_dp, to_ex),
            device_id_type=MESH,
        )

    wo = pair.at[pl.ds(0, 3 * HEAD)]
    weights = [
        pltpu.make_async_copy(src, dst, w_sem.at[i])
        for i, (src, dst) in enumerate(((wo_hbm, wo), (wg_hbm, wg), (wu_hbm, wu), (wd_hbm, wd)))
    ]
    for copy in weights:
        copy.start()

    barrier = pltpu.get_barrier_semaphore()
    for d in range(1, NDP):
        pl.semaphore_signal(barrier, inc=1, device_id=((dp + d) % NDP, ex), device_id_type=MESH)
    for d in range(1, NEX):
        pl.semaphore_signal(barrier, inc=1, device_id=(dp, (ex + d) % NEX), device_id_type=MESH)
    for d in range(4):
        other = (4 - ex // 4 * 4) + d
        pl.semaphore_signal(barrier, inc=1, device_id=(at_dp(0, 1), other), device_id_type=MESH)

    row = iota((256, 128), 0)
    part_of = (row & 15) >> 2
    slot_rows = [slot_ref[t : t + 1, :] for t in range(STEPS)]
    r64 = iota((256, GROUPS), 0)
    want = 4 * (r64 >> 4) + (r64 & 3)

    def by_part(full):
        picked = jnp.zeros((256, HEAD), F32)
        for a in range(4):
            picked = jnp.where(part_of == a, full[:, a * HEAD : (a + 1) * HEAD], picked)
        return picked.astype(BF).reshape(NDP, 16, HEAD)

    for t in range(STEPS):
        order = ones_where(slot_rows[t] == want)
        first = dot(order, jnp.concatenate([q_ref[t], nkv_ref[t][:, :HEAD]], axis=1))
        qs_send[t, :, 0] = by_part(first)
        if t == 0:
            zero = jnp.zeros((GROUPS, 3 * HEAD), BF)
            second = jnp.concatenate([zero, nkv_ref[0][:, HEAD:]], axis=1)
        else:
            zero = jnp.zeros((GROUPS, HEAD), BF)
            second = jnp.concatenate([nkv_ref[0][:, :HEAD], zero, nkv_ref[0][:, HEAD:], nkv_ref[1][:, HEAD:]], axis=1)
        qs_send[t, :, 1] = by_part(dot(order, second))

    pl.semaphore_wait(barrier, NDP - 1 + NEX - 1 + 4)

    def spread_dp(send, recv, sems, t):
        copies = []
        for d in range(1, NDP):
            to = (dp + d) % NDP
            copies.append(remote(send.at[t, to], recv.at[t, dp], sems, (t, d - 1), to, ex))
        for copy in copies:
            start(copy)
        recv[t, dp] = send[t, dp]
        return copies

    q_copies = [spread_dp(qs_send, qs_recv, q_sem, t) for t in range(STEPS)]

    factor = 1.0 / math.sqrt(HEAD)
    r_s = iota((256, 1024), 0)
    own_prompt = (r_s & 3) == (iota((256, 1024), 1) >> 8)
    r_e, c_e = iota((256, 256), 0), iota((256, 256), 1)
    same_source = (r_e >> 4) == (c_e >> 4)

    def pick(block, base):
        return dot(ones_where(same_source & ((c_e & 15) == base + (r_e & 3))), block)

    a_copies = []
    for t in range(STEPS):
        for copy in q_copies[t]:
            arrived(copy)
        first = qs_recv[t, :, 0].reshape(256, HEAD)
        second = qs_recv[t, :, 1].reshape(256, HEAD)
        stored = pkv_ref[t].reshape(1024, 2 * HEAD)
        scores = jnp.where(own_prompt, dot_nt(first, stored[:, :HEAD]) * factor, NEG)
        first_f = first.astype(F32)
        recent = [(pick(first, 12), pick(second, 12))]
        if t == 1:
            recent.append((pick(second, 0), pick(second, 8)))
        recent_scores = [jnp.sum(first_f * keys, axis=1, keepdims=True) * factor for keys, _ in recent]
        peak = jnp.max(scores, axis=1, keepdims=True)
        for s in recent_scores:
            peak = jnp.maximum(peak, s)
        weight = jnp.exp(scores - peak)
        total = jnp.sum(weight, axis=1, keepdims=True)
        summed = dot(weight.astype(BF), stored[:, HEAD:])
        for s, (_, values) in zip(recent_scores, recent):
            w = jnp.exp(s - peak)
            total = total + w
            summed = summed + w.astype(BF).astype(F32) * values
        at_send[t] = (summed / total).astype(BF).reshape(NDP, 16, HEAD)
        a_copies.append(spread_dp(at_send, at_recv, a_sem, t))

    c64 = iota((GROUPS, 256), 1)
    want_c = 4 * (c64 >> 4) + (c64 & 3)
    weights[0].wait()

    def crossing(other):
        return y * 4 + (zl + other // 4 + ex // 4) % 2 * 2 + core

    def spread_ex(send, recv, sems, t, nearest=True):
        copies = []
        for d in range(1, NEX):
            other = (ex + d) % NEX
            to = crossing(other) if nearest else dp
            copies.append(remote(send.at[t, other], recv.at[t, ex], sems, (t, d - 1), to, other))
        return copies

    o_copies = []
    for t in range(STEPS):
        for copy in a_copies[t]:
            arrived(copy)
        back = at_recv[t].reshape(256, HEAD)
        back_f = back.astype(F32)
        parted = jnp.concatenate([jnp.where(part_of == a, back_f, 0.0).astype(BF) for a in range(3)], axis=1)
        order = ones_where(to_column(slot_rows[t]) == want_c)
        attended = dot(order, parted).astype(BF)

        def project(i, t=t, attended=attended):
            lo = dot(attended, pair[pl.ds(0, 3 * HEAD), tile_at(i)])
            hi = dot(attended, pair[pl.ds(0, 3 * HEAD), tile_at(i, HALF)])
            for e in range(NEX):
                both = jnp.concatenate([lo[e * 8 : e * 8 + 8], hi[e * 8 : e * 8 + 8]], axis=0)
                op_send[t, e, :, tile_at(i)] = both.astype(BF)

        loop(HALF // TILE, project)
        o_copies.append(spread_ex(op_send, op_recv, o_sem, t, nearest=False))
        if t == 0:
            for copy in o_copies[0]:
                start(copy)

    d_copies = [None, None]
    targets = [None, None]
    raw_copies = [[], []]
    chip = dp // 2

    def mix(t):
        for copy in o_copies[t]:
            arrived(copy)

        def add(i, squares):
            total = op_send[t, ex, :, tile_at(i)].astype(F32)
            for d in range(1, NEX):
                total = total + op_recv[t, (ex + d) % NEX, :, tile_at(i)].astype(F32)
            lo = res_ref[t, :, tile_at(i)].astype(F32)
            hi = res_ref[t, :, tile_at(i, HALF)].astype(F32)
            total = total + jnp.concatenate([lo, hi], axis=0)
            mixed[t, :, tile_at(i)] = total
            return squares + total * total

        squares = lax.fori_loop(0, HALF // TILE, add, jnp.zeros((16, TILE), F32))
        per_half = jnp.sum(squares, axis=1, keepdims=True)
        inverse = 1.0 / jnp.sqrt((per_half[:8] + per_half[8:]) / D + 1e-05)
        inverse = jnp.concatenate([inverse, inverse], axis=0)

        def scale(i):
            lower = iota((16, TILE), 0) < 8
            gain = jnp.where(lower, gain_ref[:, tile_at(i)], gain_ref[:, tile_at(i, HALF)])
            nb[:, tile_at(i)] = (mixed[t, :, tile_at(i)] * inverse * gain).astype(BF)

        loop(HALF // TILE, scale)
        normed = nb[...].astype(F32)
        lo, hi = normed[:8], normed[8:]
        logits = dot_nt(lo.astype(BF), wr_ref[:, :HALF]) + dot_nt(hi.astype(BF), wr_ref[:, HALF:])
        rows = [routes_ref[t][k : k + 1, :] for k in range(2)]
        cols = [to_column(r) for r in rows]
        chosen = [jnp.sum(jnp.where(iota((8, 8), 1) == c, logits, 0.0), axis=1, keepdims=True) for c in cols]
        before = iota((8, 8), 1) < iota((8, 8), 0)
        cells, gates = [], []
        for k in range(2):
            gate = jax.nn.sigmoid(chosen[k] - chosen[1 - k])
            gat[t, k] = jnp.broadcast_to(gate, (8, 128))
            rounded = gate.astype(BF).astype(F32)
            gates += [rounded, gate - rounded]
            place = jnp.zeros((8, 1), jnp.int32)
            for other in rows:
                place = place + jnp.sum(jnp.where(before & (cols[k] == other), 1, 0), axis=1, keepdims=True)
            cells.append(cols[k] * 4 + place)
        targets[t] = cells
        c32 = iota((8, 32), 1) & 7
        cell_rows = [jnp.sum(jnp.where(c32 == iota((8, 32), 0), c, 0), axis=0, keepdims=True) for c in cells]
        r_d, c_d = iota((128, 32), 0), iota((128, 32), 1)
        cell = 4 * (r_d >> 4) + (r_d & 3)
        same_quarter = ((r_d & 15) >> 2) == (c_d >> 3)
        choose = ones_where(same_quarter & ((cell_rows[0] == cell) | (cell_rows[1] == cell)))
        quarters = jnp.concatenate([lo[:, :QUART], lo[:, QUART : 2 * QUART], lo[:, 2 * QUART :], hi[:, :QUART]], axis=0).astype(BF)
        for i in range(QUART // TILE):
            cut = slice(i * TILE, (i + 1) * TILE)
            ds_send[t, :, :, cut] = dot(choose, quarters[:, cut]).astype(BF).reshape(NEX, 16, TILE)
        d_copies[t] = spread_ex(ds_send, ds_recv, d_sem, t)
        for copy in d_copies[t]:
            start(copy)
        lane = iota((8, 128), 1)
        info = jnp.zeros((8, 128), F32)
        for i, v in enumerate([c.astype(F32) for c in cells] + gates):
            info = jnp.where(lane == i, v, info)
        raw_send[t, :, NC // 2 :] = jnp.concatenate([info, info], axis=0).astype(BF)
        raw_send[t, :, : NC // 2] = jnp.concatenate([hi[:, QUART : 2 * QUART], hi[:, 2 * QUART :]], axis=0).astype(BF)
        for d in range(1, 8):
            copy = remote(raw_send.at[t], raw_recv.at[t, chip], raw_sem, (t, d), at_dp(d // 2, d % 2), ex)
            start(copy)
            raw_copies[t].append(copy)
        raw_recv[t, chip] = raw_send[t]
        if t == 0:
            for copy in o_copies[1]:
                start(copy)

    r_u, c_u = iota((128, 128), 0), iota((128, 128), 1)
    unfold_matrix = ones_where(((r_u >> 5) == ((c_u & 15) >> 2)) & (((r_u & 31) >> 2) == (c_u >> 4)) & ((r_u & 3) == (c_u & 3)))
    fold_matrix = ones_where(((c_u >> 5) == ((r_u & 15) >> 2)) & (((c_u & 31) >> 2) == (r_u >> 4)) & ((c_u & 3) == (r_u & 3)))


    def unfold(t):
        for copy in d_copies[t]:
            arrived(copy)
        ds_recv[t, ex] = ds_send[t, ex]
        for i in range(QUART // TILE):
            cut = slice(i * TILE, (i + 1) * TILE)
            rows = dot(unfold_matrix, ds_recv[t, :, :, cut].reshape(128, TILE)).astype(BF)
            for quarter in range(4):
                start = quarter * QUART + i * TILE
                held[t, dp, :, start : start + TILE] = rows[quarter * SLOTS : (quarter + 1) * SLOTS]

    zh = ex // 4
    r256, c256 = iota((256, 256), 0), iota((256, 256), 1)

    def swap(cross_of, flip_row):
        cross = (cross_of >> 2) ^ zh
        major, minor = r256 >> 5, (r256 & 31) >> 2
        col_major, col_minor = c256 >> 5, (c256 & 31) >> 2
        if flip_row:
            same = (minor == col_major) & ((major ^ cross) == col_minor)
        else:
            same = (major == col_minor) & (minor == (col_major ^ cross))
        return ones_where(same & ((r256 & 3) == (c256 & 3)))

    to_chips = swap((r256 & 31) >> 2, True)
    to_experts = swap(r256 >> 5, False)
    dc_copies = [None, None]
    info_of = [None, None]

    def dispatch_c(t):
        for copy in raw_copies[t]:
            arrived(copy)
        info = raw_recv[t, :, :, NC // 2 :].reshape(128, 128).astype(F32)
        info_of[t] = info
        eye = iota((128, 128), 0) == iota((128, 128), 1)
        wanted = [jnp.sum(jnp.where(eye, info[:, k : k + 1], 0.0), axis=0, keepdims=True) for k in range(2)]
        r, c = iota((256, 128), 0), iota((256, 128), 1)
        cell = (4 * (r >> 5) + (r & 3)).astype(F32)
        match = ((wanted[0] == cell) | (wanted[1] == cell)) & (((r & 31) >> 2) == (c >> 4))
        for h in range(2):
            choose = ones_where(match & (((c & 15) >> 3) == h))
            for i in range(NC // 2 // TILE):
                cut = slice(i * TILE, (i + 1) * TILE)
                out = dot(choose, raw_recv[t, :, :, cut].reshape(128, TILE)).astype(BF)
                cs_send[t, :, :, h * (NC // 2) + i * TILE : h * (NC // 2) + (i + 1) * TILE] = out.reshape(NEX, SLOTS, TILE)
        dc_copies[t] = spread_ex(cs_send, cs_recv, dc_sem, t)
        for copy in dc_copies[t]:
            start(copy)
        cs_recv[t, ex] = cs_send[t, ex]

    def place_c(t):
        for copy in dc_copies[t]:
            arrived(copy)
        for i in range(NC // TILE):
            cut = slice(i * TILE, (i + 1) * TILE)
            out = dot(to_chips, cs_recv[t, :, :, cut].reshape(256, TILE)).astype(BF)
            for k in range(8):
                held[t, k * 2 + core, :, AB + i * TILE : AB + (i + 1) * TILE] = out[k * SLOTS : (k + 1) * SLOTS]
        for d in range(8):
            give(t, f"last{d}", at_dp(d // 2, d % 2), at_dp(0, 0, 1), columns=part_c)

    part_a, part_b = pl.ds(0, NA), pl.ds(NA, AB - NA)
    part_ab, part_c = pl.ds(0, AB), pl.ds(AB, NC)
    whole = slice(None)
    lower, upper = pl.ds(0, 16), pl.ds(16, 16)
    g_copies = [{}, {}]

    def give(t, name, device, to_dp, rows=whole, columns=part_ab):
        ref = held.at[t, device, rows, columns]
        copy = remote(ref, ref, g_sem, (t, len(g_copies[t])), to_dp, ex)
        start(copy)
        g_copies[t][name] = copy

    def got(t, *names):
        for name in names:
            arrived(g_copies[t][name])

    def to_core(t, dy, plane):
        give(t, f"core{dy}{plane}", at_dp(dy, plane), at_dp(0, 0, 1))

    def gather_own(t):
        give(t, "z", dp, at_dp(0, 1), columns=part_a)
        give(t, "up0", dp, at_dp(1))
        give(t, "down0", dp, at_dp(3))
        give(t, "cross0", dp, at_dp(0, 1), columns=part_b)
        to_core(t, 0, 0)

    def gather_z(t):
        got(t, "z")
        give(t, "up1", at_dp(0, 1), at_dp(1), columns=part_a)
        give(t, "down1", at_dp(0, 1), at_dp(3), columns=part_a)

    def gather_near(t, plane):
        columns = part_a if plane else part_ab
        got(t, f"up{plane}")
        give(t, f"far_up{plane}", at_dp(3, plane), at_dp(1), lower, columns)
        got(t, f"down{plane}")
        give(t, f"far_down{plane}", at_dp(1, plane), at_dp(3), upper, columns)
        if plane == 0:
            for dy in (3, 1):
                give(t, f"cross{dy}", at_dp(dy), at_dp(0, 1), columns=part_b)
                to_core(t, dy, 0)

    def gather_far(t):
        got(t, "far_up0", "far_down0")
        give(t, "cross2", at_dp(2), at_dp(0, 1), columns=part_b)
        to_core(t, 2, 0)

    def gather_cross(t, *dys):
        for dy in dys:
            if dy == 2:
                got(t, "far_up1", "far_down1")
            got(t, f"cross{dy}")
            to_core(t, dy, 1)

    def gather_end(t):
        for dy in (0, 1, 3, 2):
            got(t, f"core{dy}0", f"core{dy}1")

    def gather_last(t):
        got(t, *(f"last{d}" for d in range(8)))

    def gate_up(t, first, last):
        if first == 0:
            acc_g[...] = jnp.zeros_like(acc_g)
            acc_u[...] = jnp.zeros_like(acc_u)

        def step(i):
            x = held[t, :, :, tile_at(i, first * TILE)].reshape(NDP * SLOTS, TILE)
            acc_g[...] += dot(x, wg[tile_at(i, first * TILE), :])
            acc_u[...] += dot(x, wu[tile_at(i, first * TILE), :])

        loop(last - first, step)

    def activate(t):
        hid[...] = (jax.nn.silu(acc_g[...]) * acc_u[...]).astype(BF)
        for copy in g_copies[t].values():
            left(copy)

    def down(t, first, last):
        def step(i):
            y_part = dot(hid[...], wd[:, tile_at(i, first * TILE)])
            held[t, :, :, tile_at(i, first * TILE)] = y_part.astype(BF).reshape(NDP, SLOTS, TILE)

        loop(last - first, step)

    r_copies = [{}, {}]

    def pass_on(t, name, src, dst, to_dp):
        copy = remote(src, dst, r_sem, (t, len(r_copies[t])), to_dp, ex)
        start(copy)
        r_copies[t][name] = copy

    def came(t, *names):
        for name in names:
            if any(c is r_copies[t][name] for c in to_arrive):
                arrived(r_copies[t][name])

    def pair_rows(t, kind, rows=whole):
        start, size = (0, SLOTS) if rows is whole else (rows.start, rows.size)
        return pl.ds(pl.multiple_of((t * 8 + kind) * SLOTS + start, 16), size)

    def part(t, dy, plane, rows, cut):
        other = pair[pair_rows(t, 2 * dy + plane, rows), cut]
        return held[t, at_dp(dy, plane), rows, cut].astype(F32) + other.astype(F32)

    def crossed(t, dy, rows, i):
        return zcross[t, dy, rows, tile_at(i)].astype(F32)

    def over_a(t, dy, plane, rows, *more):
        def step(i):
            cut = tile_at(i)
            total = part(t, dy, plane, rows, cut)
            for term in more:
                total = total + term(cut)
            held[t, at_dp(dy, plane), rows, cut] = total.astype(BF)

        loop(NA // TILE, step)

    def over_b(t, dy, plane, rows, *more):
        def step(i):
            cut = tile_at(i, NA)
            total = part(t, dy, plane, rows, cut)
            if plane == 0:
                total = total + crossed(t, dy, rows, i)
            for term in more:
                total = total + term(cut)
            held[t, at_dp(dy, plane), rows, cut] = total.astype(BF)

        loop((AB - NA) // TILE, step)

    def reduce_cores(t, name, columns):
        for dy, plane in ((2, 1), (1, 1), (3, 1), (0, 1), (2, 0), (1, 0), (3, 0), (0, 0)):
            src = held.at[t, at_dp(dy, plane, 1), whole, columns]
            dst = pair.at[pair_rows(t, 2 * dy + plane), columns]
            pass_on(t, f"{name}{dy}{plane}", src, dst, at_dp(0, 0, 1))

    def send_transit(t, plane):
        columns = part_a if plane else part_ab
        for way, to_dy, rows in ((0, 1, lower), (1, 3, upper)):
            src = held.at[t, at_dp(2, plane), rows, columns]
            dst = transit.at[t, way, plane, whole, columns]
            pass_on(t, f"transit{way}{plane}", src, dst, at_dp(to_dy))

    def reduce_cross(t):
        for dy in (2, 1, 3, 0):
            came(t, f"core{dy}1")
            over_b(t, dy, 1, whole)
            pass_on(t, f"cross{dy}", held.at[t, at_dp(dy, 1), whole, part_b], zcross.at[t, dy], at_dp(0, 1))
            if dy == 2:
                over_a(t, 2, 1, whole)
                send_transit(t, 1)

    def send_sum(t, name, way, plane, rows):
        columns = part_a if plane else part_ab
        dy = 1 if way == 0 else 3
        src = held.at[t, at_dp(dy, plane), rows, columns]
        pass_on(t, f"{name}{way}{plane}", src, ysum.at[t, way, plane, rows, columns], at_dp(dy))

    def reduce_free1(t):
        for way, dy, rows in ((0, 1, upper), (1, 3, lower)):
            over_a(t, dy, 1, rows)
            send_sum(t, "free", way, 1, rows)

    def reduce_far(t):
        came(t, "core20", "cross2")
        over_a(t, 2, 0, whole)
        over_b(t, 2, 0, whole)
        send_transit(t, 0)

    def reduce_free0(t):
        for way, dy, rows in ((0, 1, upper), (1, 3, lower)):
            came(t, f"core{dy}0", f"cross{dy}")
            over_a(t, dy, 0, rows)
            over_b(t, dy, 0, rows)
            send_sum(t, "free", way, 0, rows)

    def reduce_bound(t, plane):
        for way, dy, rows in ((0, 1, lower), (1, 3, upper)):
            came(t, f"transit{way}{plane}")

            def moved(cut, way=way):
                return transit[t, way, plane, :, cut].astype(F32)

            over_a(t, dy, plane, rows, moved)
            if plane == 0:
                over_b(t, dy, plane, rows, moved)
            send_sum(t, "bound", way, plane, rows)

    def around(t, plane, cut):
        return ysum[t, 0, plane, :, cut].astype(F32) + ysum[t, 1, plane, :, cut].astype(F32)

    def came_around(t, plane):
        came(t, *(f"{name}{way}{plane}" for name in ("free", "bound") for way in range(2)))

    def reduce_here(t):
        came_around(t, 1)
        over_a(t, 0, 1, whole, lambda cut: around(t, 1, cut))
        pass_on(t, "z", held.at[t, at_dp(0, 1), whole, part_a], zsum.at[t], at_dp(0, 1))

    ec_copies = [None, None]
    y_copies = [[], []]

    def reduce_c(t):
        for copy in dc_copies[t]:
            left(copy)
        came(t, *(f"last{dy}{plane}" for dy in range(4) for plane in range(2)))
        for i in range(NC // TILE):
            cut = slice(AB + i * TILE, AB + (i + 1) * TILE)
            parts = []
            for k in range(8):
                kind = (k // 2 + 4 - y) % 4 * 2 + (k % 2 + zl) % 2
                total = held[t, k * 2 + core, :, cut].astype(F32) + pair[pair_rows(t, kind), cut].astype(F32)
                parts.append(total.astype(BF))
            out = dot(to_experts, jnp.concatenate(parts, axis=0)).astype(BF)
            cs_send[t, :, :, i * TILE : (i + 1) * TILE] = out.reshape(NEX, SLOTS, TILE)
        ec_copies[t] = spread_ex(cs_send, cr_recv, ec_sem, t)
        for copy in ec_copies[t]:
            start(copy)
        cr_recv[t, ex] = cs_send[t, ex]

    def combine_c(t):
        for copy in ec_copies[t]:
            arrived(copy)
        info = raw_recv[t, :, :, NC // 2 :].reshape(128, 128).astype(F32)
        r, c = iota((128, 256), 0), iota((128, 256), 1)
        cell = (4 * (c >> 5) + (c & 3)).astype(F32)
        same = ((c & 31) >> 2) == (r >> 4)
        choose = [ones_where(same & (info[:, k : k + 1] == cell)) for k in range(2)]
        gate = [info[:, 2 + 2 * k : 3 + 2 * k] + info[:, 3 + 2 * k : 4 + 2 * k] for k in range(2)]
        first_half = (iota((128, TILE), 0) & 15) < 8

        def both(start):
            came_in = cr_recv[t, :, :, start : start + TILE].reshape(256, TILE)
            return gate[0] * dot(choose[0], came_in) + gate[1] * dot(choose[1], came_in)

        for i in range(NC // 2 // TILE):
            out = jnp.where(first_half, both(i * TILE), both(NC // 2 + i * TILE)).astype(BF)
            y_send[t, :, :, i * TILE : (i + 1) * TILE] = out.reshape(8, 16, TILE)
        for d in range(1, 8):
            to_y, to_z = (y + d // 2) % 4, (zl + d % 2) % 2
            src = y_send.at[t, to_y * 2 + to_z]
            copy = remote(src, y_recv.at[t, chip], y_sem, (t, d), at_dp(d // 2, d % 2), ex)
            start(copy)
            y_copies[t].append(copy)
        y_recv[t, chip] = y_send[t, chip]

    t_copies = [None, None]

    def finish(t):
        came_around(t, 0)
        came(t, "core00", "cross0", "z")
        for i in range(QUART // TILE):
            parts = []
            for quarter in range(4):
                cut = slice(quarter * QUART + i * TILE, quarter * QUART + (i + 1) * TILE)
                total = part(t, 0, 0, whole, cut) + around(t, 0, cut)
                if cut.start < NA:
                    total = total + zsum[t, :, cut].astype(F32)
                else:
                    total = total + zcross[t, 0, :, cut.start - NA : cut.stop - NA].astype(F32)
                parts.append(total.astype(BF))
            folded = dot(fold_matrix, jnp.concatenate(parts, axis=0)).astype(BF)
            rt_send[t, :, :, i * TILE : (i + 1) * TILE] = folded.reshape(NEX, 16, TILE)
        t_copies[t] = spread_ex(rt_send, rt_recv, t_sem, t)
        for copy in t_copies[t]:
            start(copy)
        rt_recv[t, ex] = rt_send[t, ex]

    def combine(t):
        for copy in t_copies[t]:
            arrived(copy)
        both = jnp.concatenate(targets[t], axis=0)
        c_c = iota((16, 128), 1)
        mine = both == 4 * (c_c >> 4) + (c_c & 3)
        gate0, gate1 = gat[t, 0][:, :1], gat[t, 1][:, :1]
        for i in range(QUART // TILE):
            came = rt_recv[t, :, :, i * TILE : (i + 1) * TILE].reshape(128, TILE)
            for quarter in range(4):
                out = dot(ones_where(mine & (((c_c & 15) >> 2) == quarter)), came)
                place = quarter * QUART + i * TILE
                first, start = place // HALF * 8, place % HALF
                total = mixed[t, first : first + 8, start : start + TILE] + gate0 * out[:8] + gate1 * out[8:]
                out_ref[t, :, place : place + TILE] = total.astype(BF)

    def combine_last(t):
        for copy in y_copies[t]:
            arrived(copy)
        for i in range(NC // 2 // TILE):
            total = jnp.zeros((16, TILE), F32)
            for k in range(8):
                total = total + y_recv[t, k, :, i * TILE : (i + 1) * TILE].astype(F32)
            for h in range(2):
                place = AB + h * (NC // 2) + i * TILE
                both = mixed[t, 8:, place - HALF : place - HALF + TILE] + total[8 * h : 8 * h + 8]
                out_ref[t, :, place : place + TILE] = both.astype(BF)

    mix(0)
    unfold(0)
    gather_own(0)
    gather_z(0)
    gather_near(0, 0)
    mix(1)
    dispatch_c(0)
    gather_near(0, 1)
    unfold(1)
    gather_own(1)
    gather_cross(0, 0, 1, 3)
    gather_far(0)
    gather_cross(0, 2)
    dispatch_c(1)
    gather_z(1)
    for copy in weights[1:]:
        copy.wait()
    gather_end(0)
    gate_up(0, 0, 4)
    gather_near(1, 0)
    gate_up(0, 4, 8)
    place_c(0)
    gather_near(1, 1)
    gather_cross(1, 0, 1, 3)
    gather_last(0)
    gate_up(0, 8, 12)
    gather_far(1)
    activate(0)
    down(0, 8, 12)
    reduce_cores(0, "last", part_c)
    gather_cross(1, 2)
    down(0, 0, 8)
    reduce_cores(0, "core", part_ab)
    reduce_c(0)
    gather_end(1)
    reduce_cross(0)
    reduce_free1(0)
    gate_up(1, 0, 2)
    reduce_far(0)
    gate_up(1, 2, 5)
    reduce_bound(0, 1)
    reduce_free0(0)
    gate_up(1, 5, 8)
    place_c(1)
    reduce_bound(0, 0)
    gather_last(1)
    gate_up(1, 8, 12)
    activate(1)
    down(1, 8, 12)
    reduce_cores(1, "last", part_c)
    down(1, 0, 4)
    reduce_here(0)
    reduce_c(1)
    down(1, 4, 8)
    reduce_cores(1, "core", part_ab)
    reduce_cross(1)
    reduce_free1(1)
    reduce_far(1)
    combine_c(0)
    reduce_bound(1, 1)
    reduce_free0(1)
    reduce_bound(1, 0)
    finish(0)
    combine_c(1)
    combine(0)
    combine_last(0)
    reduce_here(1)
    finish(1)
    combine_last(1)
    combine(1)

    for copy in list(to_arrive):
        arrived(copy)
    for copy in list(to_leave):
        left(copy)


def body(queries, prompt_kv, new_kv, prompt_slot, residual, w_out, norm_gain, w_router, routes, w_gate, w_up, w_down):
    vmem = pl.BlockSpec(memory_space=pltpu.VMEM)
    hbm = pl.BlockSpec(memory_space=pl.ANY)
    dma = pltpu.SemaphoreType.DMA
    return pl.pallas_call(
        kernel,
        out_shape=jax.ShapeDtypeStruct((STEPS, ROWS, D), BF),
        in_specs=[vmem] * 5 + [hbm] + [vmem] * 3 + [hbm] * 3,
        out_specs=vmem,
        scratch_shapes=[
            pltpu.VMEM((D, FFD), BF),
            pltpu.VMEM((D, FFD), BF),
            pltpu.VMEM((FFD, D), BF),
            pltpu.VMEM((STEPS, NDP, 2, 16, HEAD), BF),
            pltpu.VMEM((STEPS, NDP, 2, 16, HEAD), BF),
            pltpu.VMEM((STEPS, NDP, 16, HEAD), BF),
            pltpu.VMEM((STEPS, NDP, 16, HEAD), BF),
            pltpu.VMEM((STEPS, NEX, 16, HALF), BF),
            pltpu.VMEM((STEPS, NEX, 16, HALF), BF),
            pltpu.VMEM((STEPS, NEX, 16, QUART), BF),
            pltpu.VMEM((STEPS, NEX, 16, QUART), BF),
            pltpu.VMEM((STEPS, 16, HALF), F32),
            pltpu.VMEM((16, HALF), BF),
            pltpu.VMEM((STEPS, 2, 8, 128), F32),
            pltpu.VMEM((STEPS, NDP, SLOTS, D), BF),
            pltpu.VMEM((NDP * SLOTS, FFD), F32),
            pltpu.VMEM((NDP * SLOTS, FFD), F32),
            pltpu.VMEM((NDP * SLOTS, FFD), BF),
            pltpu.VMEM((STEPS * 8 * SLOTS, D), BF),
            pltpu.VMEM((STEPS, 2, 2, 16, AB), BF),
            pltpu.VMEM((STEPS, 2, 2, SLOTS, AB), BF),
            pltpu.VMEM((STEPS, SLOTS, NA), BF),
            pltpu.VMEM((STEPS, 4, SLOTS, AB - NA), BF),
            pltpu.VMEM((STEPS, NEX, 16, QUART), BF),
            pltpu.VMEM((STEPS, NEX, 16, QUART), BF),
            pltpu.VMEM((STEPS, 16, RAW), BF),
            pltpu.VMEM((STEPS, 8, 16, RAW), BF),
            pltpu.VMEM((STEPS, NEX, SLOTS, NC), BF),
            pltpu.VMEM((STEPS, NEX, SLOTS, NC), BF),
            pltpu.VMEM((STEPS, NEX, SLOTS, NC), BF),
            pltpu.VMEM((STEPS, 8, 16, NC // 2), BF),
            pltpu.VMEM((STEPS, 8, 16, NC // 2), BF),
            dma((4,)),
            dma((2, STEPS, NDP - 1)),
            dma((2, STEPS, NDP - 1)),
            dma((2, STEPS, NEX - 1)),
            dma((2, STEPS, NEX - 1)),
            dma((2, STEPS, 40)),
            dma((2, STEPS, 40)),
            dma((2, STEPS, NEX - 1)),
            dma((2, STEPS, 8)),
            dma((2, STEPS, NEX - 1)),
            dma((2, STEPS, NEX - 1)),
            dma((2, STEPS, 8)),
        ],
        compiler_params=pltpu.CompilerParams(
            collective_id=0, has_side_effects=True, vmem_limit_bytes=63 * 1024 * 1024
        ),
    )(
        queries,
        prompt_kv[:, :, :, 0, :],
        new_kv[:, :, 0, :],
        prompt_slot,
        residual,
        w_out,
        norm_gain.reshape(1, D),
        w_router.T,
        jnp.transpose(routes, (0, 2, 1)),
        w_gate[0],
        w_up[0],
        w_down[0],
    )


def solution(mesh):
    placed = (
        P(None, "dp", "expert"),
        P(None, "dp", None, "expert", None),
        P(None, "dp", "expert", None),
        P(),
        P(None, ("dp", "expert"), None),
        P("expert", None),
        P(),
        P(),
        P(None, ("dp", "expert"), None),
        P("expert", None, "dp"),
        P("expert", None, "dp"),
        P("expert", "dp", None),
    )
    return jax.shard_map(body, mesh=mesh, in_specs=placed, out_specs=P(None, ("dp", "expert"), None), check_vma=False)
```

```python
import math

import jax
import jax.numpy as jnp
from jax import lax
from jax.experimental import pallas as pl
from jax.experimental.pallas import tpu as pltpu
from jax.sharding import PartitionSpec as P

HEAD = 128
MESH = pl.DeviceIdType.MESH
BF = jnp.bfloat16
F32 = jnp.float32
NEG = -1e30

STEPS = 2
NDP = 16
NEX = 8
GROUPS = 64
D = 6144
HALF = D // 2
NC = 2048
AB = D - NC
QUART = AB // 4
RAW = NC // 2 + 128
FFD = 512
ROWS = 8
SLOTS = 32
TILE = 512
NA = 3072


def iota(shape, dim):
    return lax.broadcasted_iota(jnp.int32, shape, dim)


def dot(a, b):
    return jnp.dot(a, b, preferred_element_type=F32)


def dot_nt(a, b):
    return lax.dot_general(a, b, (((1,), (1,)), ((), ())), preferred_element_type=F32)


def ones_where(cond):
    return jnp.where(cond, 1.0, 0.0).astype(BF)


def to_column(row):
    n = row.shape[1]
    eye = iota((n, n), 0) == iota((n, n), 1)
    return jnp.sum(jnp.where(eye, row, 0), axis=1, keepdims=True)


def loop(n, fn):
    lax.fori_loop(0, n, lambda i, c: (fn(i), c)[1], 0)


def tile_at(i, base=0):
    return pl.ds(pl.multiple_of(base + i * TILE, TILE), TILE)


def kernel(
    q_ref, pkv_ref, nkv_ref, slot_ref, res_ref, wo_hbm, gain_ref, wr_ref, routes_ref, wg_hbm, wu_hbm, wd_hbm,
    out_ref,
    wg, wu, wd,
    qs_send, qs_recv, at_send, at_recv, op_send, op_recv, ds_send, ds_recv,
    mixed, nb, gat, held, acc_g, acc_u, hid, pair, transit, ysum, zsum, zcross, rt_send, rt_recv,
    raw_send, raw_recv, cs_send, cs_recv, cr_recv, y_send, y_recv,
    w_sem, q_sem, a_sem, o_sem, d_sem, g_sem, r_sem, t_sem, raw_sem, dc_sem, ec_sem, y_sem,
):
    dp = lax.axis_index("dp")
    ex = lax.axis_index("expert")
    y = dp // 4
    zl = (dp // 2) % 2
    core = dp % 2

    def at_dp(dy, flip_z=0, flip_c=0):
        yy = (y + dy) % 4
        zz = 1 - zl if flip_z else zl
        cc = 1 - core if flip_c else core
        return yy * 4 + zz * 2 + cc

    to_arrive, to_leave = [], []

    def start(copy):
        copy.start()
        to_arrive.append(copy)
        to_leave.append(copy)

    def arrived(copy):
        copy.wait_recv()
        to_arrive[:] = [c for c in to_arrive if c is not copy]

    def left(copy):
        copy.wait_send()
        to_leave[:] = [c for c in to_leave if c is not copy]

    def remote(src, dst, sems, idx, to_dp, to_ex):
        return pltpu.make_async_remote_copy(
            src_ref=src,
            dst_ref=dst,
            send_sem=sems.at[(0, *idx)],
            recv_sem=sems.at[(1, *idx)],
            device_id=(to_dp, to_ex),
            device_id_type=MESH,
        )

    wo = pair.at[pl.ds(0, 3 * HEAD)]
    weights = [
        pltpu.make_async_copy(src, dst, w_sem.at[i])
        for i, (src, dst) in enumerate(((wo_hbm, wo), (wg_hbm, wg), (wu_hbm, wu), (wd_hbm, wd)))
    ]
    for copy in weights:
        copy.start()

    barrier = pltpu.get_barrier_semaphore()
    for d in range(1, NDP):
        pl.semaphore_signal(barrier, inc=1, device_id=((dp + d) % NDP, ex), device_id_type=MESH)
    for d in range(1, NEX):
        pl.semaphore_signal(barrier, inc=1, device_id=(dp, (ex + d) % NEX), device_id_type=MESH)
    for d in range(4):
        other = (4 - ex // 4 * 4) + d
        pl.semaphore_signal(barrier, inc=1, device_id=(at_dp(0, 1), other), device_id_type=MESH)

    row = iota((256, 128), 0)
    part_of = (row & 15) >> 2
    slot_rows = [slot_ref[t : t + 1, :] for t in range(STEPS)]
    r64 = iota((256, GROUPS), 0)
    want = 4 * (r64 >> 4) + (r64 & 3)

    def by_part(full):
        picked = jnp.zeros((256, HEAD), F32)
        for a in range(4):
            picked = jnp.where(part_of == a, full[:, a * HEAD : (a + 1) * HEAD], picked)
        return picked.astype(BF).reshape(NDP, 16, HEAD)

    for t in range(STEPS):
        order = ones_where(slot_rows[t] == want)
        first = dot(order, jnp.concatenate([q_ref[t], nkv_ref[t][:, :HEAD]], axis=1))
        qs_send[t, :, 0] = by_part(first)
        if t == 0:
            zero = jnp.zeros((GROUPS, 3 * HEAD), BF)
            second = jnp.concatenate([zero, nkv_ref[0][:, HEAD:]], axis=1)
        else:
            zero = jnp.zeros((GROUPS, HEAD), BF)
            second = jnp.concatenate([nkv_ref[0][:, :HEAD], zero, nkv_ref[0][:, HEAD:], nkv_ref[1][:, HEAD:]], axis=1)
        qs_send[t, :, 1] = by_part(dot(order, second))

    pl.semaphore_wait(barrier, NDP - 1 + NEX - 1 + 4)

    def spread_dp(send, recv, sems, t):
        copies = []
        for d in range(1, NDP):
            to = (dp + d) % NDP
            copies.append(remote(send.at[t, to], recv.at[t, dp], sems, (t, d - 1), to, ex))
        for copy in copies:
            start(copy)
        recv[t, dp] = send[t, dp]
        return copies

    q_copies = [spread_dp(qs_send, qs_recv, q_sem, t) for t in range(STEPS)]

    factor = 1.0 / math.sqrt(HEAD)
    r_s = iota((256, 1024), 0)
    own_prompt = (r_s & 3) == (iota((256, 1024), 1) >> 8)
    r_e, c_e = iota((256, 256), 0), iota((256, 256), 1)
    same_source = (r_e >> 4) == (c_e >> 4)

    def pick(block, base):
        return dot(ones_where(same_source & ((c_e & 15) == base + (r_e & 3))), block)

    a_copies = []
    for t in range(STEPS):
        for copy in q_copies[t]:
            arrived(copy)
        first = qs_recv[t, :, 0].reshape(256, HEAD)
        second = qs_recv[t, :, 1].reshape(256, HEAD)
        stored = pkv_ref[t].reshape(1024, 2 * HEAD)
        scores = jnp.where(own_prompt, dot_nt(first, stored[:, :HEAD]) * factor, NEG)
        first_f = first.astype(F32)
        recent = [(pick(first, 12), pick(second, 12))]
        if t == 1:
            recent.append((pick(second, 0), pick(second, 8)))
        recent_scores = [jnp.sum(first_f * keys, axis=1, keepdims=True) * factor for keys, _ in recent]
        peak = jnp.max(scores, axis=1, keepdims=True)
        for s in recent_scores:
            peak = jnp.maximum(peak, s)
        weight = jnp.exp(scores - peak)
        total = jnp.sum(weight, axis=1, keepdims=True)
        summed = dot(weight.astype(BF), stored[:, HEAD:])
        for s, (_, values) in zip(recent_scores, recent):
            w = jnp.exp(s - peak)
            total = total + w
            summed = summed + w.astype(BF).astype(F32) * values
        at_send[t] = (summed / total).astype(BF).reshape(NDP, 16, HEAD)
        a_copies.append(spread_dp(at_send, at_recv, a_sem, t))

    c64 = iota((GROUPS, 256), 1)
    want_c = 4 * (c64 >> 4) + (c64 & 3)
    weights[0].wait()

    def crossing(other):
        return y * 4 + (zl + other // 4 + ex // 4) % 2 * 2 + core

    def spread_ex(send, recv, sems, t, nearest=True):
        copies = []
        for d in range(1, NEX):
            other = (ex + d) % NEX
            to = crossing(other) if nearest else dp
            copies.append(remote(send.at[t, other], recv.at[t, ex], sems, (t, d - 1), to, other))
        return copies

    o_copies = []
    for t in range(STEPS):
        for copy in a_copies[t]:
            arrived(copy)
        back = at_recv[t].reshape(256, HEAD)
        back_f = back.astype(F32)
        parted = jnp.concatenate([jnp.where(part_of == a, back_f, 0.0).astype(BF) for a in range(3)], axis=1)
        order = ones_where(to_column(slot_rows[t]) == want_c)
        attended = dot(order, parted).astype(BF)

        def project(i, t=t, attended=attended):
            lo = dot(attended, pair[pl.ds(0, 3 * HEAD), tile_at(i)])
            hi = dot(attended, pair[pl.ds(0, 3 * HEAD), tile_at(i, HALF)])
            for e in range(NEX):
                both = jnp.concatenate([lo[e * 8 : e * 8 + 8], hi[e * 8 : e * 8 + 8]], axis=0)
                op_send[t, e, :, tile_at(i)] = both.astype(BF)

        loop(HALF // TILE, project)
        o_copies.append(spread_ex(op_send, op_recv, o_sem, t, nearest=False))
        if t == 0:
            for copy in o_copies[0]:
                start(copy)

    d_copies = [None, None]
    targets = [None, None]
    raw_copies = [[], []]
    chip = dp // 2

    def mix(t):
        for copy in o_copies[t]:
            arrived(copy)

        def add(i, squares):
            total = op_send[t, ex, :, tile_at(i)].astype(F32)
            for d in range(1, NEX):
                total = total + op_recv[t, (ex + d) % NEX, :, tile_at(i)].astype(F32)
            lo = res_ref[t, :, tile_at(i)].astype(F32)
            hi = res_ref[t, :, tile_at(i, HALF)].astype(F32)
            total = total + jnp.concatenate([lo, hi], axis=0)
            mixed[t, :, tile_at(i)] = total
            return squares + total * total

        squares = lax.fori_loop(0, HALF // TILE, add, jnp.zeros((16, TILE), F32))
        per_half = jnp.sum(squares, axis=1, keepdims=True)
        inverse = 1.0 / jnp.sqrt((per_half[:8] + per_half[8:]) / D + 1e-05)
        inverse = jnp.concatenate([inverse, inverse], axis=0)

        def scale(i):
            lower = iota((16, TILE), 0) < 8
            gain = jnp.where(lower, gain_ref[:, tile_at(i)], gain_ref[:, tile_at(i, HALF)])
            nb[:, tile_at(i)] = (mixed[t, :, tile_at(i)] * inverse * gain).astype(BF)

        loop(HALF // TILE, scale)
        normed = nb[...].astype(F32)
        lo, hi = normed[:8], normed[8:]
        logits = dot_nt(lo.astype(BF), wr_ref[:, :HALF]) + dot_nt(hi.astype(BF), wr_ref[:, HALF:])
        rows = [routes_ref[t][k : k + 1, :] for k in range(2)]
        cols = [to_column(r) for r in rows]
        chosen = [jnp.sum(jnp.where(iota((8, 8), 1) == c, logits, 0.0), axis=1, keepdims=True) for c in cols]
        before = iota((8, 8), 1) < iota((8, 8), 0)
        cells, gates = [], []
        for k in range(2):
            gate = jax.nn.sigmoid(chosen[k] - chosen[1 - k])
            gat[t, k] = jnp.broadcast_to(gate, (8, 128))
            rounded = gate.astype(BF).astype(F32)
            gates += [rounded, gate - rounded]
            place = jnp.zeros((8, 1), jnp.int32)
            for other in rows:
                place = place + jnp.sum(jnp.where(before & (cols[k] == other), 1, 0), axis=1, keepdims=True)
            cells.append(cols[k] * 4 + place)
        targets[t] = cells
        c32 = iota((8, 32), 1) & 7
        cell_rows = [jnp.sum(jnp.where(c32 == iota((8, 32), 0), c, 0), axis=0, keepdims=True) for c in cells]
        r_d, c_d = iota((128, 32), 0), iota((128, 32), 1)
        cell = 4 * (r_d >> 4) + (r_d & 3)
        same_quarter = ((r_d & 15) >> 2) == (c_d >> 3)
        choose = ones_where(same_quarter & ((cell_rows[0] == cell) | (cell_rows[1] == cell)))
        quarters = jnp.concatenate([lo[:, :QUART], lo[:, QUART : 2 * QUART], lo[:, 2 * QUART :], hi[:, :QUART]], axis=0).astype(BF)
        for i in range(QUART // TILE):
            cut = slice(i * TILE, (i + 1) * TILE)
            ds_send[t, :, :, cut] = dot(choose, quarters[:, cut]).astype(BF).reshape(NEX, 16, TILE)
        d_copies[t] = spread_ex(ds_send, ds_recv, d_sem, t)
        for copy in d_copies[t]:
            start(copy)
        lane = iota((8, 128), 1)
        info = jnp.zeros((8, 128), F32)
        for i, v in enumerate([c.astype(F32) for c in cells] + gates):
            info = jnp.where(lane == i, v, info)
        raw_send[t, :, NC // 2 :] = jnp.concatenate([info, info], axis=0).astype(BF)
        raw_send[t, :, : NC // 2] = jnp.concatenate([hi[:, QUART : 2 * QUART], hi[:, 2 * QUART :]], axis=0).astype(BF)
        for d in range(1, 8):
            copy = remote(raw_send.at[t], raw_recv.at[t, chip], raw_sem, (t, d), at_dp(d // 2, d % 2), ex)
            start(copy)
            raw_copies[t].append(copy)
        raw_recv[t, chip] = raw_send[t]
        if t == 0:
            for copy in o_copies[1]:
                start(copy)

    r_u, c_u = iota((128, 128), 0), iota((128, 128), 1)
    unfold_matrix = ones_where(((r_u >> 5) == ((c_u & 15) >> 2)) & (((r_u & 31) >> 2) == (c_u >> 4)) & ((r_u & 3) == (c_u & 3)))
    fold_matrix = ones_where(((c_u >> 5) == ((r_u & 15) >> 2)) & (((c_u & 31) >> 2) == (r_u >> 4)) & ((c_u & 3) == (r_u & 3)))


    def unfold(t):
        for copy in d_copies[t]:
            arrived(copy)
        ds_recv[t, ex] = ds_send[t, ex]
        for i in range(QUART // TILE):
            cut = slice(i * TILE, (i + 1) * TILE)
            rows = dot(unfold_matrix, ds_recv[t, :, :, cut].reshape(128, TILE)).astype(BF)
            for quarter in range(4):
                start = quarter * QUART + i * TILE
                held[t, dp, :, start : start + TILE] = rows[quarter * SLOTS : (quarter + 1) * SLOTS]

    zh = ex // 4
    r256, c256 = iota((256, 256), 0), iota((256, 256), 1)

    def swap(cross_of, flip_row):
        cross = (cross_of >> 2) ^ zh
        major, minor = r256 >> 5, (r256 & 31) >> 2
        col_major, col_minor = c256 >> 5, (c256 & 31) >> 2
        if flip_row:
            same = (minor == col_major) & ((major ^ cross) == col_minor)
        else:
            same = (major == col_minor) & (minor == (col_major ^ cross))
        return ones_where(same & ((r256 & 3) == (c256 & 3)))

    to_chips = swap((r256 & 31) >> 2, True)
    to_experts = swap(r256 >> 5, False)
    dc_copies = [None, None]
    info_of = [None, None]

    def dispatch_c(t):
        for copy in raw_copies[t]:
            arrived(copy)
        info = raw_recv[t, :, :, NC // 2 :].reshape(128, 128).astype(F32)
        info_of[t] = info
        eye = iota((128, 128), 0) == iota((128, 128), 1)
        wanted = [jnp.sum(jnp.where(eye, info[:, k : k + 1], 0.0), axis=0, keepdims=True) for k in range(2)]
        r, c = iota((256, 128), 0), iota((256, 128), 1)
        cell = (4 * (r >> 5) + (r & 3)).astype(F32)
        match = ((wanted[0] == cell) | (wanted[1] == cell)) & (((r & 31) >> 2) == (c >> 4))
        for h in range(2):
            choose = ones_where(match & (((c & 15) >> 3) == h))
            for i in range(NC // 2 // TILE):
                cut = slice(i * TILE, (i + 1) * TILE)
                out = dot(choose, raw_recv[t, :, :, cut].reshape(128, TILE)).astype(BF)
                cs_send[t, :, :, h * (NC // 2) + i * TILE : h * (NC // 2) + (i + 1) * TILE] = out.reshape(NEX, SLOTS, TILE)
        dc_copies[t] = spread_ex(cs_send, cs_recv, dc_sem, t)
        for copy in dc_copies[t]:
            start(copy)
        cs_recv[t, ex] = cs_send[t, ex]

    def place_c(t):
        for copy in dc_copies[t]:
            arrived(copy)
        for i in range(NC // TILE):
            cut = slice(i * TILE, (i + 1) * TILE)
            out = dot(to_chips, cs_recv[t, :, :, cut].reshape(256, TILE)).astype(BF)
            for k in range(8):
                held[t, k * 2 + core, :, AB + i * TILE : AB + (i + 1) * TILE] = out[k * SLOTS : (k + 1) * SLOTS]
        for d in range(8):
            give(t, f"last{d}", at_dp(d // 2, d % 2), at_dp(0, 0, 1), columns=part_c)

    part_a, part_b = pl.ds(0, NA), pl.ds(NA, AB - NA)
    part_ab, part_c = pl.ds(0, AB), pl.ds(AB, NC)
    whole = slice(None)
    lower, upper = pl.ds(0, 16), pl.ds(16, 16)
    g_copies = [{}, {}]

    def give(t, name, device, to_dp, rows=whole, columns=part_ab):
        ref = held.at[t, device, rows, columns]
        copy = remote(ref, ref, g_sem, (t, len(g_copies[t])), to_dp, ex)
        start(copy)
        g_copies[t][name] = copy

    def got(t, *names):
        for name in names:
            arrived(g_copies[t][name])

    def to_core(t, dy, plane):
        give(t, f"core{dy}{plane}", at_dp(dy, plane), at_dp(0, 0, 1))

    def gather_own(t):
        give(t, "z", dp, at_dp(0, 1), columns=part_a)
        give(t, "up0", dp, at_dp(1))
        give(t, "down0", dp, at_dp(3))
        give(t, "cross0", dp, at_dp(0, 1), columns=part_b)
        to_core(t, 0, 0)

    def gather_z(t):
        got(t, "z")
        give(t, "up1", at_dp(0, 1), at_dp(1), columns=part_a)
        give(t, "down1", at_dp(0, 1), at_dp(3), columns=part_a)

    def gather_near(t, plane):
        columns = part_a if plane else part_ab
        got(t, f"up{plane}")
        give(t, f"far_up{plane}", at_dp(3, plane), at_dp(1), lower, columns)
        got(t, f"down{plane}")
        give(t, f"far_down{plane}", at_dp(1, plane), at_dp(3), upper, columns)
        if plane == 0:
            for dy in (3, 1):
                give(t, f"cross{dy}", at_dp(dy), at_dp(0, 1), columns=part_b)
                to_core(t, dy, 0)

    def gather_far(t):
        got(t, "far_up0", "far_down0")
        give(t, "cross2", at_dp(2), at_dp(0, 1), columns=part_b)
        to_core(t, 2, 0)

    def gather_cross(t, *dys):
        for dy in dys:
            if dy == 2:
                got(t, "far_up1", "far_down1")
            got(t, f"cross{dy}")
            to_core(t, dy, 1)

    def gather_end(t):
        for dy in (0, 1, 3, 2):
            got(t, f"core{dy}0", f"core{dy}1")

    def gather_last(t):
        got(t, *(f"last{d}" for d in range(8)))

    def gate_up(t, first, last):
        if first == 0:
            acc_g[...] = jnp.zeros_like(acc_g)
            acc_u[...] = jnp.zeros_like(acc_u)

        def step(i):
            x = held[t, :, :, tile_at(i, first * TILE)].reshape(NDP * SLOTS, TILE)
            acc_g[...] += dot(x, wg[tile_at(i, first * TILE), :])
            acc_u[...] += dot(x, wu[tile_at(i, first * TILE), :])

        loop(last - first, step)

    def activate(t):
        hid[...] = (jax.nn.silu(acc_g[...]) * acc_u[...]).astype(BF)
        for copy in g_copies[t].values():
            left(copy)

    def down(t, first, last):
        def step(i):
            y_part = dot(hid[...], wd[:, tile_at(i, first * TILE)])
            held[t, :, :, tile_at(i, first * TILE)] = y_part.astype(BF).reshape(NDP, SLOTS, TILE)

        loop(last - first, step)

    r_copies = [{}, {}]

    def pass_on(t, name, src, dst, to_dp):
        copy = remote(src, dst, r_sem, (t, len(r_copies[t])), to_dp, ex)
        start(copy)
        r_copies[t][name] = copy

    def came(t, *names):
        for name in names:
            if any(c is r_copies[t][name] for c in to_arrive):
                arrived(r_copies[t][name])

    def pair_rows(t, kind, rows=whole):
        start, size = (0, SLOTS) if rows is whole else (rows.start, rows.size)
        return pl.ds(pl.multiple_of((t * 8 + kind) * SLOTS + start, 16), size)

    def part(t, dy, plane, rows, cut):
        other = pair[pair_rows(t, 2 * dy + plane, rows), cut]
        return held[t, at_dp(dy, plane), rows, cut].astype(F32) + other.astype(F32)

    def crossed(t, dy, rows, i):
        return zcross[t, dy, rows, tile_at(i)].astype(F32)

    def over_a(t, dy, plane, rows, *more):
        def step(i):
            cut = tile_at(i)
            total = part(t, dy, plane, rows, cut)
            for term in more:
                total = total + term(cut)
            held[t, at_dp(dy, plane), rows, cut] = total.astype(BF)

        loop(NA // TILE, step)

    def over_b(t, dy, plane, rows, *more):
        def step(i):
            cut = tile_at(i, NA)
            total = part(t, dy, plane, rows, cut)
            if plane == 0:
                total = total + crossed(t, dy, rows, i)
            for term in more:
                total = total + term(cut)
            held[t, at_dp(dy, plane), rows, cut] = total.astype(BF)

        loop((AB - NA) // TILE, step)

    def reduce_cores(t, name, columns):
        for dy, plane in ((2, 1), (1, 1), (3, 1), (0, 1), (2, 0), (1, 0), (3, 0), (0, 0)):
            src = held.at[t, at_dp(dy, plane, 1), whole, columns]
            dst = pair.at[pair_rows(t, 2 * dy + plane), columns]
            pass_on(t, f"{name}{dy}{plane}", src, dst, at_dp(0, 0, 1))

    def send_transit(t, plane):
        columns = part_a if plane else part_ab
        for way, to_dy, rows in ((0, 1, lower), (1, 3, upper)):
            src = held.at[t, at_dp(2, plane), rows, columns]
            dst = transit.at[t, way, plane, whole, columns]
            pass_on(t, f"transit{way}{plane}", src, dst, at_dp(to_dy))

    def reduce_cross(t):
        for dy in (2, 1, 3, 0):
            came(t, f"core{dy}1")
            over_b(t, dy, 1, whole)
            pass_on(t, f"cross{dy}", held.at[t, at_dp(dy, 1), whole, part_b], zcross.at[t, dy], at_dp(0, 1))
            if dy == 2:
                over_a(t, 2, 1, whole)
                send_transit(t, 1)

    def send_sum(t, name, way, plane, rows):
        columns = part_a if plane else part_ab
        dy = 1 if way == 0 else 3
        src = held.at[t, at_dp(dy, plane), rows, columns]
        pass_on(t, f"{name}{way}{plane}", src, ysum.at[t, way, plane, rows, columns], at_dp(dy))

    def reduce_free1(t):
        for way, dy, rows in ((0, 1, upper), (1, 3, lower)):
            over_a(t, dy, 1, rows)
            send_sum(t, "free", way, 1, rows)

    def reduce_far(t):
        came(t, "core20", "cross2")
        over_a(t, 2, 0, whole)
        over_b(t, 2, 0, whole)
        send_transit(t, 0)

    def reduce_free0(t):
        for way, dy, rows in ((0, 1, upper), (1, 3, lower)):
            came(t, f"core{dy}0", f"cross{dy}")
            over_a(t, dy, 0, rows)
            over_b(t, dy, 0, rows)
            send_sum(t, "free", way, 0, rows)

    def reduce_bound(t, plane):
        for way, dy, rows in ((0, 1, lower), (1, 3, upper)):
            came(t, f"transit{way}{plane}")

            def moved(cut, way=way):
                return transit[t, way, plane, :, cut].astype(F32)

            over_a(t, dy, plane, rows, moved)
            if plane == 0:
                over_b(t, dy, plane, rows, moved)
            send_sum(t, "bound", way, plane, rows)

    def around(t, plane, cut):
        return ysum[t, 0, plane, :, cut].astype(F32) + ysum[t, 1, plane, :, cut].astype(F32)

    def came_around(t, plane):
        came(t, *(f"{name}{way}{plane}" for name in ("free", "bound") for way in range(2)))

    def reduce_here(t):
        came_around(t, 1)
        over_a(t, 0, 1, whole, lambda cut: around(t, 1, cut))
        pass_on(t, "z", held.at[t, at_dp(0, 1), whole, part_a], zsum.at[t], at_dp(0, 1))

    ec_copies = [None, None]
    y_copies = [[], []]

    def reduce_c(t):
        for copy in dc_copies[t]:
            left(copy)
        came(t, *(f"last{dy}{plane}" for dy in range(4) for plane in range(2)))
        for i in range(NC // TILE):
            cut = slice(AB + i * TILE, AB + (i + 1) * TILE)
            parts = []
            for k in range(8):
                kind = (k // 2 + 4 - y) % 4 * 2 + (k % 2 + zl) % 2
                total = held[t, k * 2 + core, :, cut].astype(F32) + pair[pair_rows(t, kind), cut].astype(F32)
                parts.append(total.astype(BF))
            out = dot(to_experts, jnp.concatenate(parts, axis=0)).astype(BF)
            cs_send[t, :, :, i * TILE : (i + 1) * TILE] = out.reshape(NEX, SLOTS, TILE)
        ec_copies[t] = spread_ex(cs_send, cr_recv, ec_sem, t)
        for copy in ec_copies[t]:
            start(copy)
        cr_recv[t, ex] = cs_send[t, ex]

    def combine_c(t):
        for copy in ec_copies[t]:
            arrived(copy)
        info = raw_recv[t, :, :, NC // 2 :].reshape(128, 128).astype(F32)
        r, c = iota((128, 256), 0), iota((128, 256), 1)
        cell = (4 * (c >> 5) + (c & 3)).astype(F32)
        same = ((c & 31) >> 2) == (r >> 4)
        choose = [ones_where(same & (info[:, k : k + 1] == cell)) for k in range(2)]
        gate = [info[:, 2 + 2 * k : 3 + 2 * k] + info[:, 3 + 2 * k : 4 + 2 * k] for k in range(2)]
        first_half = (iota((128, TILE), 0) & 15) < 8

        def both(start):
            came_in = cr_recv[t, :, :, start : start + TILE].reshape(256, TILE)
            return gate[0] * dot(choose[0], came_in) + gate[1] * dot(choose[1], came_in)

        for i in range(NC // 2 // TILE):
            out = jnp.where(first_half, both(i * TILE), both(NC // 2 + i * TILE)).astype(BF)
            y_send[t, :, :, i * TILE : (i + 1) * TILE] = out.reshape(8, 16, TILE)
        for d in range(1, 8):
            to_y, to_z = (y + d // 2) % 4, (zl + d % 2) % 2
            src = y_send.at[t, to_y * 2 + to_z]
            copy = remote(src, y_recv.at[t, chip], y_sem, (t, d), at_dp(d // 2, d % 2), ex)
            start(copy)
            y_copies[t].append(copy)
        y_recv[t, chip] = y_send[t, chip]

    t_copies = [None, None]

    def finish(t):
        came_around(t, 0)
        came(t, "core00", "cross0", "z")
        for i in range(QUART // TILE):
            parts = []
            for quarter in range(4):
                cut = slice(quarter * QUART + i * TILE, quarter * QUART + (i + 1) * TILE)
                total = part(t, 0, 0, whole, cut) + around(t, 0, cut)
                if cut.start < NA:
                    total = total + zsum[t, :, cut].astype(F32)
                else:
                    total = total + zcross[t, 0, :, cut.start - NA : cut.stop - NA].astype(F32)
                parts.append(total.astype(BF))
            folded = dot(fold_matrix, jnp.concatenate(parts, axis=0)).astype(BF)
            rt_send[t, :, :, i * TILE : (i + 1) * TILE] = folded.reshape(NEX, 16, TILE)
        t_copies[t] = spread_ex(rt_send, rt_recv, t_sem, t)
        for copy in t_copies[t]:
            start(copy)
        rt_recv[t, ex] = rt_send[t, ex]

    def combine(t):
        for copy in t_copies[t]:
            arrived(copy)
        both = jnp.concatenate(targets[t], axis=0)
        c_c = iota((16, 128), 1)
        mine = both == 4 * (c_c >> 4) + (c_c & 3)
        gate0, gate1 = gat[t, 0][:, :1], gat[t, 1][:, :1]
        for i in range(QUART // TILE):
            came = rt_recv[t, :, :, i * TILE : (i + 1) * TILE].reshape(128, TILE)
            for quarter in range(4):
                out = dot(ones_where(mine & (((c_c & 15) >> 2) == quarter)), came)
                place = quarter * QUART + i * TILE
                first, start = place // HALF * 8, place % HALF
                total = mixed[t, first : first + 8, start : start + TILE] + gate0 * out[:8] + gate1 * out[8:]
                out_ref[t, :, place : place + TILE] = total.astype(BF)

    def combine_last(t):
        for copy in y_copies[t]:
            arrived(copy)
        for i in range(NC // 2 // TILE):
            total = jnp.zeros((16, TILE), F32)
            for k in range(8):
                total = total + y_recv[t, k, :, i * TILE : (i + 1) * TILE].astype(F32)
            for h in range(2):
                place = AB + h * (NC // 2) + i * TILE
                both = mixed[t, 8:, place - HALF : place - HALF + TILE] + total[8 * h : 8 * h + 8]
                out_ref[t, :, place : place + TILE] = both.astype(BF)

    mix(0)
    unfold(0)
    gather_own(0)
    gather_z(0)
    gather_near(0, 0)
    mix(1)
    dispatch_c(0)
    gather_near(0, 1)
    unfold(1)
    gather_own(1)
    gather_cross(0, 0, 1, 3)
    gather_far(0)
    gather_cross(0, 2)
    dispatch_c(1)
    gather_z(1)
    for copy in weights[1:]:
        copy.wait()
    gather_end(0)
    gate_up(0, 0, 4)
    gather_near(1, 0)
    gate_up(0, 4, 8)
    place_c(0)
    gather_near(1, 1)
    gather_cross(1, 0, 1, 3)
    gather_last(0)
    gate_up(0, 8, 12)
    gather_far(1)
    activate(0)
    down(0, 8, 12)
    reduce_cores(0, "last", part_c)
    gather_cross(1, 2)
    down(0, 0, 8)
    reduce_cores(0, "core", part_ab)
    reduce_c(0)
    gather_end(1)
    reduce_cross(0)
    reduce_free1(0)
    gate_up(1, 0, 2)
    reduce_far(0)
    gate_up(1, 2, 5)
    reduce_bound(0, 1)
    reduce_free0(0)
    gate_up(1, 5, 8)
    place_c(1)
    reduce_bound(0, 0)
    gather_last(1)
    gate_up(1, 8, 12)
    activate(1)
    down(1, 8, 12)
    reduce_cores(1, "last", part_c)
    down(1, 0, 4)
    reduce_c(1)
    reduce_here(0)
    down(1, 4, 8)
    reduce_cores(1, "core", part_ab)
    reduce_cross(1)
    reduce_free1(1)
    reduce_far(1)
    combine_c(0)
    reduce_bound(1, 1)
    reduce_free0(1)
    reduce_bound(1, 0)
    finish(0)
    combine_c(1)
    combine(0)
    combine_last(0)
    reduce_here(1)
    finish(1)
    combine_last(1)
    combine(1)

    for copy in list(to_arrive):
        arrived(copy)
    for copy in list(to_leave):
        left(copy)


def body(queries, prompt_kv, new_kv, prompt_slot, residual, w_out, norm_gain, w_router, routes, w_gate, w_up, w_down):
    vmem = pl.BlockSpec(memory_space=pltpu.VMEM)
    hbm = pl.BlockSpec(memory_space=pl.ANY)
    dma = pltpu.SemaphoreType.DMA
    return pl.pallas_call(
        kernel,
        out_shape=jax.ShapeDtypeStruct((STEPS, ROWS, D), BF),
        in_specs=[vmem] * 5 + [hbm] + [vmem] * 3 + [hbm] * 3,
        out_specs=vmem,
        scratch_shapes=[
            pltpu.VMEM((D, FFD), BF),
            pltpu.VMEM((D, FFD), BF),
            pltpu.VMEM((FFD, D), BF),
            pltpu.VMEM((STEPS, NDP, 2, 16, HEAD), BF),
            pltpu.VMEM((STEPS, NDP, 2, 16, HEAD), BF),
            pltpu.VMEM((STEPS, NDP, 16, HEAD), BF),
            pltpu.VMEM((STEPS, NDP, 16, HEAD), BF),
            pltpu.VMEM((STEPS, NEX, 16, HALF), BF),
            pltpu.VMEM((STEPS, NEX, 16, HALF), BF),
            pltpu.VMEM((STEPS, NEX, 16, QUART), BF),
            pltpu.VMEM((STEPS, NEX, 16, QUART), BF),
            pltpu.VMEM((STEPS, 16, HALF), F32),
            pltpu.VMEM((16, HALF), BF),
            pltpu.VMEM((STEPS, 2, 8, 128), F32),
            pltpu.VMEM((STEPS, NDP, SLOTS, D), BF),
            pltpu.VMEM((NDP * SLOTS, FFD), F32),
            pltpu.VMEM((NDP * SLOTS, FFD), F32),
            pltpu.VMEM((NDP * SLOTS, FFD), BF),
            pltpu.VMEM((STEPS * 8 * SLOTS, D), BF),
            pltpu.VMEM((STEPS, 2, 2, 16, AB), BF),
            pltpu.VMEM((STEPS, 2, 2, SLOTS, AB), BF),
            pltpu.VMEM((STEPS, SLOTS, NA), BF),
            pltpu.VMEM((STEPS, 4, SLOTS, AB - NA), BF),
            pltpu.VMEM((STEPS, NEX, 16, QUART), BF),
            pltpu.VMEM((STEPS, NEX, 16, QUART), BF),
            pltpu.VMEM((STEPS, 16, RAW), BF),
            pltpu.VMEM((STEPS, 8, 16, RAW), BF),
            pltpu.VMEM((STEPS, NEX, SLOTS, NC), BF),
            pltpu.VMEM((STEPS, NEX, SLOTS, NC), BF),
            pltpu.VMEM((STEPS, NEX, SLOTS, NC), BF),
            pltpu.VMEM((STEPS, 8, 16, NC // 2), BF),
            pltpu.VMEM((STEPS, 8, 16, NC // 2), BF),
            dma((4,)),
            dma((2, STEPS, NDP - 1)),
            dma((2, STEPS, NDP - 1)),
            dma((2, STEPS, NEX - 1)),
            dma((2, STEPS, NEX - 1)),
            dma((2, STEPS, 40)),
            dma((2, STEPS, 40)),
            dma((2, STEPS, NEX - 1)),
            dma((2, STEPS, 8)),
            dma((2, STEPS, NEX - 1)),
            dma((2, STEPS, NEX - 1)),
            dma((2, STEPS, 8)),
        ],
        compiler_params=pltpu.CompilerParams(
            collective_id=0, has_side_effects=True, vmem_limit_bytes=63 * 1024 * 1024
        ),
    )(
        queries,
        prompt_kv[:, :, :, 0, :],
        new_kv[:, :, 0, :],
        prompt_slot,
        residual,
        w_out,
        norm_gain.reshape(1, D),
        w_router.T,
        jnp.transpose(routes, (0, 2, 1)),
        w_gate[0],
        w_up[0],
        w_down[0],
    )


def solution(mesh):
    placed = (
        P(None, "dp", "expert"),
        P(None, "dp", None, "expert", None),
        P(None, "dp", "expert", None),
        P(),
        P(None, ("dp", "expert"), None),
        P("expert", None),
        P(),
        P(),
        P(None, ("dp", "expert"), None),
        P("expert", None, "dp"),
        P("expert", None, "dp"),
        P("expert", "dp", None),
    )
    return jax.shard_map(body, mesh=mesh, in_specs=placed, out_specs=P(None, ("dp", "expert"), None), check_vma=False)
```
